32 devices in a mesh: lon: 8 (over z, x), lat: 4 (over y, core).
Axes of the slice: x: 2, y: 2, z: 4, core: 2. Of those that a mesh axis runs over, the one named last changes fastest.
Arguments:
- right_side: float32 [2, 32, 64, 1024], P(None, None, 'lat', 'lon'), may hold values from -36 to 36
- sea_mask: int32 [32, 64, 1024], P(None, 'lat', 'lon'), may hold values 0 or 1
- levels: int32 [64, 1024], P('lat', 'lon'), may hold values from 0 to 32
- east_diffusivity: bfloat16 [32, 64, 1024], P(None, 'lat', 'lon'), may hold values from 1 to 8
- north_diffusivity: bfloat16 [32, 64, 1024], P(None, 'lat', 'lon'), may hold values from 1 to 8
- vertical_diffusivity: bfloat16 [32, 64, 1024], P(None, 'lat', 'lon'), may hold values from 0.5 to 8
Outputs:
- solution_field: float32 [2, 32, 64, 1024], P(None, None, 'lat', 'lon')
- residual: float32 [2, 32, 64, 1024], P(None, None, 'lat', 'lon')
The draws below stay inside these ranges and needn't reach their ends.
All inputs are finite; a program needn't handle non-finite values. No bound on the sum of `sea_mask` on one device may be relied on, other than what follows from the above.
Results may differ from the reference program's by a relative error of at most 0.004.
Values sent between devices are 32-bit elements; how exact they have to be, the bound alone decides.
No kernel may reach another device: no remote copies, remote signals or barrier semaphores. Data moves between devices by JAX's collectives and lax.ppermute only.
A program may use at most 64 MiB of HBM per device.

```python
import math
import jax
import jax.numpy as jnp
from jax import lax

NZ = 32
TRACERS = 2
ITERS = 2
NLON = 1024
NLAT = 64


def draw_right_side(key, part):
    lat_pos = jnp.arange(NLAT, dtype=jnp.float32)[:, None] / max(NLAT - 1, 1)
    lon_pos = jnp.arange(NLON, dtype=jnp.float32)[None, :] / max(NLON - 1, 1)
    scales = jnp.exp(math.log(3.0) * (lat_pos + lon_pos))
    shape = (TRACERS, NZ, NLAT, NLON)
    rough = jnp.clip(jax.random.normal(key, shape, jnp.float32), -4.0, 4.0)
    return (rough * scales[None, None]).astype(jnp.float32)


def with_ends(array, key, low, top_value):
    longest = array.shape.index(max(array.shape))
    spots = []
    for shift in (0, 1):
        where = [jax.random.randint(jax.random.fold_in(key, axis), (), 0, length) for axis, length in enumerate(array.shape)]
        where[longest] = (where[longest] + shift) % array.shape[longest]
        spots.append(tuple(where))
    return array.at[spots[0]].set(low).at[spots[1]].set(top_value)


def block_scale(key, shape, split, low, high):
    def one(axis_at, parts):
        steps = jax.random.uniform(jax.random.fold_in(jax.random.fold_in(key, 6), axis_at), (parts,), jnp.float32, low / len(split), high / len(split))
        return jnp.repeat(jnp.exp(steps), shape[axis_at] // parts).reshape((-1,) + (1,) * (len(shape) - axis_at - 1))

    loudness = one(*split[0])
    for cut in split[1:]:
        loudness = loudness * one(*cut)
    return loudness


def setup_inputs(seed: int = 0) -> dict:
    key_list = jax.random.split(jax.random.key(seed), 7)
    return {
        "right_side": draw_right_side(jax.random.fold_in(key_list[6], 71), 0),
        "sea_mask": with_ends((jax.random.randint(key_list[1], (NZ, NLAT, NLON), 0, 10) < 9).astype(jnp.int32), jax.random.fold_in(key_list[1], 1), 0, 1),
        "levels": with_ends(jax.random.randint(key_list[2], (NLAT, NLON), 0, NZ + 1), jax.random.fold_in(key_list[2], 1), 0, NZ).astype(jnp.int32),
        "east_diffusivity": jnp.clip(jnp.exp(math.log(8.0) - 2.0794415 * jax.random.uniform(key_list[3], (NZ, NLAT, NLON), jnp.float32) ** block_scale(key_list[3], (NZ, NLAT, NLON), ((1, 4), (2, 8)), -0.2, 0.2)), 1.0, 8.0).astype(jnp.bfloat16),
        "north_diffusivity": jnp.clip(jnp.exp(math.log(8.0) - 2.0794415 * jax.random.uniform(key_list[4], (NZ, NLAT, NLON), jnp.float32) ** block_scale(key_list[4], (NZ, NLAT, NLON), ((1, 4), (2, 8)), -0.2, 0.2)), 1.0, 8.0).astype(jnp.bfloat16),
        "vertical_diffusivity": jnp.clip(jnp.exp(math.log(8.0) - 2.7725887 * jax.random.uniform(key_list[5], (NZ, NLAT, NLON), jnp.float32) ** block_scale(key_list[5], (NZ, NLAT, NLON), ((1, 4), (2, 8)), -0.2, 0.2)), 0.5, 8.0).astype(jnp.bfloat16),
    }


def operator(field, coef_east, coef_north, coef_down):
    value_east = jnp.roll(field, -1, axis=2)
    value_north = jnp.concatenate([field[:, 1:], jnp.zeros_like(field[:, :1])], axis=1)
    value_below = jnp.concatenate([field[1:], jnp.zeros_like(field[:1])], axis=0)
    flux_east = coef_east * (value_east - field)
    flux_north = coef_north * (value_north - field)
    flux_down = coef_down * (value_below - field)
    flux_west = jnp.roll(flux_east, 1, axis=2)
    flux_south = jnp.concatenate([jnp.zeros_like(flux_north[:, :1]), flux_north[:, :-1]], axis=1)
    flux_above = jnp.concatenate([jnp.zeros_like(flux_down[:1]), flux_down[:-1]], axis=0)
    return field + (flux_west - flux_east) + (flux_south - flux_north) + (flux_above - flux_down)


def reference(right_side, sea_mask, levels, east_diffusivity, north_diffusivity, vertical_diffusivity):
    depth_index = lax.broadcasted_iota(jnp.int32, sea_mask.shape, 0)
    ocean = ((sea_mask == 1) & (depth_index < levels[None])).astype(jnp.float32)
    ocean_east = jnp.roll(ocean, -1, axis=2)
    ocean_north = jnp.concatenate([ocean[:, 1:], jnp.zeros_like(ocean[:, :1])], axis=1)
    ocean_below = jnp.concatenate([ocean[1:], jnp.zeros_like(ocean[:1])], axis=0)
    coef_east = east_diffusivity.astype(jnp.float32) * ocean * ocean_east
    coef_north = north_diffusivity.astype(jnp.float32) * ocean * ocean_north
    coef_down = vertical_diffusivity.astype(jnp.float32) * ocean * ocean_below

    def solve_one(source):
        solution = jnp.zeros_like(source)
        residual = source
        direction = source
        norm_now = jnp.sum(residual * residual)
        for iteration in range(ITERS):
            image = operator(direction, coef_east, coef_north, coef_down)
            step_size = norm_now / jnp.sum(direction * image)
            solution = solution + step_size * direction
            residual = residual - step_size * image
            norm_next = jnp.sum(residual * residual)
            direction = residual + (norm_next / norm_now) * direction
            norm_now = norm_next
        return solution, residual

    solution_field, residual = lax.map(solve_one, right_side)
    return solution_field, residual
```

```python
import functools

import jax
import jax.numpy as jnp
from jax import lax
from jax.experimental import pallas as pl
from jax.experimental.pallas import tpu as pltpu
from jax.sharding import PartitionSpec as P

F32 = jnp.float32
SIDES = 2
FIELDS = 6


def iota(shape, axis):
    return lax.broadcasted_iota(jnp.int32, shape, axis)


def is_even(axis):
    return lax.rem(lax.axis_index(axis), 2) == 0


def laplacian(value, below, flux_above, east_coef, north_coef, down_coef):
    rows, lanes = value.shape
    flux_east = east_coef * (pltpu.roll(value, lanes - 1, 1) - value)
    flux_north = north_coef * (pltpu.roll(value, rows - 1, 0) - value)
    change = (pltpu.roll(flux_east, 1, 1) - flux_east) + (pltpu.roll(flux_north, 1, 0) - flux_north)
    if below is None:
        return change + flux_above, None
    flux_down = down_coef * (below - value)
    change = change - flux_down
    return (change if flux_above is None else change + flux_above), flux_down


def packed_into(total, plane, slot, lane):
    return jnp.where(lane // 2 == slot, pltpu.roll(plane, 2 * slot + 1, 1), total)


def unpacked(packed, slot):
    lanes = packed.shape[1]
    return pltpu.roll(packed, lanes - 1 - 2 * slot, 1)


def from_neighbours(east, west, lane):
    lanes = lane.shape[1]
    return jnp.where(lane % 2 == 0, pltpu.roll(east, lanes - 1, 1), pltpu.roll(west, 1, 1))


def face(own, other, lane):
    return jnp.where(lane % 2 == 0, own * (other > 0).astype(F32), other * (own > 0).astype(F32))


def prepare_kernel(tracers, nz, rows, field, mask, levels, east, north, down,
                   coef_east, coef_north, coef_down, image, packed, rows_a, rows_b, east_own, north_own):
    lanes = field.shape[1]
    lane, row = iota((rows, lanes), 1), iota((rows, lanes), 0)
    depth = levels[...]

    def plane(k, t=0):
        return pl.ds((t * nz + k) * rows, rows)

    def wet(k):
        return ((mask[plane(k), :] == 1) & (k < depth)).astype(F32)

    ocean = wet(0)
    above = [None] * tracers
    packed_image = jnp.zeros((rows, lanes), F32)
    packed_field = jnp.zeros((rows, lanes), F32)
    packed_east = jnp.zeros((rows, lanes), F32)
    for k in range(nz):
        ocean_below = wet(k + 1) if k + 1 < nz else None
        own_east = east[plane(k), :].astype(F32) * ocean
        own_north = north[plane(k), :].astype(F32) * ocean
        c_east = jnp.where(lane == lanes - 1, 0.0, own_east * pltpu.roll(ocean, lanes - 1, 1))
        c_north = jnp.where(row == rows - 1, 0.0, own_north * pltpu.roll(ocean, rows - 1, 0))
        east_own[plane(k), :] = own_east
        north_own[plane(k), :] = own_north
        coef_east[plane(k), :] = c_east
        coef_north[plane(k), :] = c_north
        c_down = None
        if ocean_below is not None:
            c_down = down[plane(k), :].astype(F32) * ocean * ocean_below
            coef_down[plane(k), :] = c_down
        else:
            coef_down[plane(k), :] = jnp.zeros((rows, lanes), F32)
        packed_east = packed_into(packed_east, own_east, k, lane)
        for t in range(tracers):
            value = field[plane(k, t), :]
            below = field[plane(k + 1, t), :] if k + 1 < nz else None
            change, above[t] = laplacian(value, below, above[t], c_east, c_north, c_down)
            image[plane(k, t), :] = change
            packed_image = packed_into(packed_image, change, t * nz + k, lane)
            packed_field = packed_into(packed_field, value, t * nz + k, lane)
        ocean = ocean_below
    packed[pl.ds(0, rows), :] = packed_image
    packed[pl.ds(rows, rows), :] = packed_field
    total = packed_east
    for t in range(1, tracers):
        total = total + pltpu.roll(packed_east, 2 * nz * t, 1)
    packed[pl.ds(2 * rows, rows), :] = total

    even = is_even("lat")

    def edge(side):
        first = (rows - 1) * side
        out = [image[pl.ds(first + t * nz * rows, nz, rows), :] for t in range(tracers)]
        out += [field[pl.ds(first + t * nz * rows, nz, rows), :] for t in range(tracers)]
        return out + [east_own[pl.ds(first, nz, rows), :], north_own[pl.ds(first, nz, rows), :]]

    for at, (south, north_) in enumerate(zip(edge(0), edge(1))):
        rows_a[pl.ds(at * nz, nz), :] = jnp.where(even, north_, south)
        rows_b[pl.ds(at * nz, nz), :] = jnp.where(even, south, north_)


def rows_kernel(tracers, nz, rows, own_a, own_b, got_a, got_b, packed, message, flux, ring, coef):
    lanes = packed.shape[1]
    lane = iota((nz, lanes), 1)
    even = is_even("lat")
    lane_of_pair = iota((nz, lanes), 1) // 2
    level = iota((nz, lanes), 0)
    corner = jnp.zeros((nz, lanes), F32)
    row_change = []
    for side in range(SIDES):
        def part(at, a, b):
            first, second = (b, a) if side == 0 else (a, b)
            return jnp.where(even, first[pl.ds(at * nz, nz), :], second[pl.ds(at * nz, nz), :])

        own = lambda at: part(at, own_a, own_b)
        got = lambda at: part(at, got_a, got_b)
        own_east, got_east = own(2 * tracers), got(2 * tracers)
        if side == 0:
            c = got(2 * tracers + 1) * (own_east > 0).astype(F32)
        else:
            c = own(2 * tracers + 1) * (got_east > 0).astype(F32)
        coef[pl.ds(side * nz, nz), :] = c
        change = jnp.zeros((1, lanes), F32)
        for t in range(tracers):
            other = got(tracers + t)
            f = c * (other - own(tracers + t))
            at = pl.ds((side * tracers + t) * nz, nz)
            flux[at, :] = f
            ring[at, :] = got(t) + f
            spread = pltpu.roll(f, 2 * nz * t + 1, 1, stride=2, stride_axis=0)
            change = change + jnp.sum(jnp.where(lane_of_pair == level + nz * t, spread, 0.0), axis=0, keepdims=True)
            corner = packed_into(corner, other, side * (tracers + 1) + t, lane)
        corner = packed_into(corner, got_east, side * (tracers + 1) + tracers, lane)
        row_change.append(change)
    row = iota((rows, lanes), 0)
    first = packed[pl.ds(0, rows), :]
    first = first - jnp.where(row == 0, row_change[0], 0.0) - jnp.where(row == rows - 1, row_change[1], 0.0)
    message[pl.ds(0, rows), :] = first
    message[pl.ds(rows, 2 * rows), :] = packed[pl.ds(rows, 2 * rows), :]
    message[pl.ds(3 * rows, nz), :] = corner


def apply_kernel(tracers, nz, rows, devices, field, start, coef_east, coef_north, coef_down, flux, ring, coef,
                 own, got_a, got_b, image, twice, sums):
    lanes = field.shape[1]
    lane, row = iota((rows, lanes), 1), iota((rows, lanes), 0)
    even = is_even("lon")

    def plane(k, t=0):
        return pl.ds((t * nz + k) * rows, rows)

    def edge(side, t):
        return pl.ds((rows - 1) * side + t * nz * rows, nz, rows)

    def neighbours(at, lane):
        a, b = got_a[at, :], got_b[at, :]
        return from_neighbours(jnp.where(even, a, b), jnp.where(even, b, a), lane)

    parts = [pl.ds(i * rows, rows) for i in range(3)]
    own_image, own_field, own_east = [own[p, :] for p in parts]
    got_image, got_field, got_east = [neighbours(p, lane) for p in parts]
    c = face(own_east, got_east, lane)
    f = c * (got_field - own_field)
    f_twice = c * ((got_image + f) - (own_image - f))
    wide = iota((nz, lanes), 1)
    at = pl.ds(3 * rows, nz)
    own_corner, got_corner = own[at, :], neighbours(at, wide)
    c_corner = face(own_corner, got_corner, wide)
    difference = got_corner - own_corner
    ends = (wide == 0) | (wide == lanes - 1)
    ring_rows = {}
    for side in range(SIDES):
        for t in range(tracers):
            slot = side * (tracers + 1) + t
            moved = pltpu.roll(c_corner, lanes - 2 * (tracers - t), 1)
            change = unpacked(moved * difference, slot)
            r = ring[pl.ds((side * tracers + t) * nz, nz), :]
            ring_rows[side, t] = r - jnp.where(ends, change, 0.0)

    edges = (lane == 0) | (lane == lanes - 1)
    for t in range(tracers):
        for k in range(nz):
            image[plane(k, t), :] = start[plane(k, t), :] - jnp.where(edges, unpacked(f, t * nz + k), 0.0)
        for side in range(SIDES):
            at = edge(side, t)
            image[at, :] = image[at, :] - flux[pl.ds((side * tracers + t) * nz, nz), :]

    lane_of_sums = iota((8, lanes), 1)
    result = jnp.zeros((8, lanes), F32)
    for t in range(tracers):
        zero = jnp.zeros((rows, lanes), F32)
        total = [zero] * 4
        above = None
        for k in range(nz):
            v = field[plane(k, t), :]
            w = image[plane(k, t), :]
            below = image[plane(k + 1, t), :] if k + 1 < nz else None
            p = plane(k)
            y, above = laplacian(w, below, above, coef_east[p, :], coef_north[p, :], coef_down[p, :])
            y = y - jnp.where(edges, unpacked(f_twice, t * nz + k), 0.0)
            twice[plane(k, t), :] = y
            for i, product in enumerate((v * v, v * w, w * w, w * y)):
                total[i] = total[i] + product
        last = jnp.zeros((nz, lanes), F32)
        for side in range(SIDES):
            at = edge(side, t)
            w = image[at, :]
            change = coef[pl.ds(side * nz, nz), :] * (ring_rows[side, t] - w)
            twice[at, :] = twice[at, :] - change
            last = last - w * change
        for i in range(4):
            whole = jnp.sum(total[i])
            if i == 3:
                whole = whole + jnp.sum(last)
            result = jnp.where(lane_of_sums == 4 * t + i, whole, result)
    for i in range(devices // 8):
        sums[pl.ds(i * 8, 8), :] = result


def finish_kernel(tracers, field, image, twice, sums, solution, residual):
    lanes = field.shape[1]
    size = field.shape[0] // tracers
    total = jnp.sum(sums[...], axis=0, keepdims=True)
    lane = iota((1, lanes), 1)

    def number(i):
        return jnp.sum(jnp.where(lane == i, total, 0.0), axis=1, keepdims=True)

    for t in range(tracers):
        bb, bw, ww, wy = [number(4 * t + i) for i in range(4)]
        whole = bb + bw
        step = bb / whole
        rest = bw / whole
        new = rest * rest * bb - 2.0 * rest * step * bw + step * step * ww
        beta = new / bb
        tau = beta + rest
        step_next = new / (new + beta * beta * bb + tau * tau * bw - 2.0 * tau * step * ww + step * step * wy)
        both = step * step_next
        s_b = step + step_next * tau
        r_b = rest - step_next * tau
        r_w = both - step - step_next * tau
        chunk = 64
        for i in range(size // chunk):
            at = pl.ds(t * size + i * chunk, chunk)
            v, w, y = field[at, :], image[at, :], twice[at, :]
            solution[at, :] = s_b * v - both * w
            residual[at, :] = r_b * v + r_w * w + both * y


def swaps(devices, second, periodic):
    pairs = []
    for i in range(devices):
        j = i + 1 if (i % 2 == 0) != second else i - 1
        if periodic or 0 <= j < devices:
            pairs.append((i, j % devices))
    return pairs


def swapped(x, axis, second, periodic):
    return lax.ppermute(x, axis, swaps(lax.axis_size(axis), second, periodic))


def body(right_side, sea_mask, levels, east_diffusivity, north_diffusivity, vertical_diffusivity):
    tracers, nz, rows, lanes = right_side.shape
    devices = lax.axis_size("lon") * lax.axis_size("lat")
    flat = lambda x: x.reshape(-1, lanes)
    shape = lambda n: jax.ShapeDtypeStruct((n, lanes), F32)
    field = flat(right_side)
    n = nz * rows
    params = pltpu.CompilerParams(vmem_limit_bytes=32 * 1024 * 1024)
    coef_east, coef_north, coef_down, start, packed, rows_a, rows_b = pl.pallas_call(
        functools.partial(prepare_kernel, tracers, nz, rows),
        out_shape=[shape(n)] * 3 + [shape(tracers * n), shape(3 * rows)] + [shape(FIELDS * nz)] * 2,
        scratch_shapes=[pltpu.VMEM((n, lanes), F32)] * 2,
        compiler_params=params,
        name="prepare",
    )(field, flat(sea_mask), levels, flat(east_diffusivity), flat(north_diffusivity), flat(vertical_diffusivity))
    got_a = swapped(rows_a, "lat", False, False)
    got_b = swapped(rows_b, "lat", True, False)
    message, flux, ring, coef = pl.pallas_call(
        functools.partial(rows_kernel, tracers, nz, rows),
        out_shape=[shape(3 * rows + nz), shape(SIDES * tracers * nz), shape(SIDES * tracers * nz), shape(SIDES * nz)],
        compiler_params=params,
        name="rows",
    )(rows_a, rows_b, got_a, got_b, packed)
    got_a = swapped(message, "lon", False, True)
    got_b = swapped(message, "lon", True, True)
    image, twice, sums = pl.pallas_call(
        functools.partial(apply_kernel, tracers, nz, rows, devices),
        out_shape=[shape(tracers * n)] * 2 + [shape(devices)],
        compiler_params=params,
        name="apply",
    )(field, start, coef_east, coef_north, coef_down, flux, ring, coef, message, got_a, got_b)
    sums = lax.all_to_all(sums, ("lon", "lat"), 0, 0, tiled=True)
    solution_field, residual = pl.pallas_call(
        functools.partial(finish_kernel, tracers),
        out_shape=[shape(tracers * n)] * 2,
        compiler_params=params,
        name="finish",
    )(field, image, twice, sums)
    return solution_field.reshape(right_side.shape), residual.reshape(right_side.shape)


def solution(mesh):
    return jax.shard_map(
        body,
        mesh=mesh,
        in_specs=(
            P(None, None, "lat", "lon"),
            P(None, "lat", "lon"),
            P("lat", "lon"),
            P(None, "lat", "lon"),
            P(None, "lat", "lon"),
            P(None, "lat", "lon"),
        ),
        out_specs=(P(None, None, "lat", "lon"), P(None, None, "lat", "lon")),
        check_vma=False,
    )
```

```python
import functools

import jax
import jax.numpy as jnp
from jax import lax
from jax.experimental import pallas as pl
from jax.experimental.pallas import tpu as pltpu
from jax.sharding import PartitionSpec as P

F32 = jnp.float32
CHUNK = 8
SIDES = 2
FIELDS = 6


def iota(shape, axis):
    return lax.broadcasted_iota(jnp.int32, shape, axis)


def is_even(axis):
    return (lax.axis_index(axis) & 1) == 0


def levels_of(ref, first, count, rows):
    return ref[pl.ds(first * rows, count * rows), :].reshape(count, rows, ref.shape[1])


def put_levels(ref, first, value):
    count, rows, lanes = value.shape
    ref[pl.ds(first * rows, count * rows), :] = value.reshape(count * rows, lanes)


def laplacian(value, below, flux_above, east_coef, north_coef, down_coef):
    _, rows, lanes = value.shape
    flux_east = east_coef * (pltpu.roll(value, lanes - 1, 2) - value)
    flux_north = north_coef * (pltpu.roll(value, rows - 1, 1) - value)
    flux_down = down_coef * (jnp.concatenate([value[1:], below], axis=0) - value)
    from_above = jnp.concatenate([flux_above, flux_down[:-1]], axis=0)
    change = (pltpu.roll(flux_east, 1, 2) - flux_east) + (pltpu.roll(flux_north, 1, 1) - flux_north)
    return change + (from_above - flux_down), flux_down[-1:]


def packed_into(total, planes, slot, pair):
    moved = [pltpu.roll(planes[i], 2 * (slot + i) + 1, 1) for i in range(planes.shape[0])]
    for i, plane in enumerate(moved):
        total = jnp.where(pair == slot + i, plane, total)
    return total


def unpacked(packed, slot, count, offset=1):
    lanes = packed.shape[1]
    return jnp.stack([pltpu.roll(packed, (2 * lanes - offset - 2 * (slot + i)) % lanes, 1) for i in range(count)])


def spread(plane, slot, pair, level):
    moved = pltpu.roll(plane, 2 * slot + 1, 1, stride=2, stride_axis=0)
    return jnp.sum(jnp.where(pair == level + slot, moved, 0.0), axis=0, keepdims=True)


def from_neighbours(east, west, even_lane):
    return jnp.where(even_lane, pltpu.roll(east, east.shape[1] - 1, 1), pltpu.roll(west, 1, 1))


def face(own, other, even_lane):
    return jnp.where(even_lane, own * (other > 0).astype(F32), other * (own > 0).astype(F32))


def prepare_kernel(tracers, nz, rows, field_in, mask_in, levels_in, east_in, north_in, down_in,
                   field, coef_east, coef_north, coef_down, east_own, rows_a, rows_b,
                   mask, levels, east, north, down, north_own, sems):
    copies = [
        pltpu.make_async_copy(a, b, sems.at[i])
        for i, (a, b) in enumerate(((levels_in, levels), (mask_in, mask), (east_in, east), (north_in, north),
                                    (down_in, down), (field_in, field)))
    ]
    for copy in copies:
        copy.start()
    for copy in copies[:-1]:
        copy.wait()
    lanes = field.shape[1]
    shape = (CHUNK, rows, lanes)
    last_lane, last_row = iota(shape, 2) == lanes - 1, iota(shape, 1) == rows - 1
    depth = levels[...]

    level = iota((CHUNK + 1, rows, lanes), 0)
    for k in range(0, nz, CHUNK):
        count = min(CHUNK + 1, nz - k)
        wet = (levels_of(mask, k, count, rows) == 1) & (level[:count] + k < depth[None])
        wet = jnp.where(wet, 1.0, 0.0)
        if count == CHUNK:
            wet = jnp.concatenate([wet, jnp.zeros((1, rows, lanes), F32)], axis=0)
        ocean = wet[:CHUNK]
        own_east = levels_of(east, k, CHUNK, rows).astype(F32) * ocean
        own_north = levels_of(north, k, CHUNK, rows).astype(F32) * ocean
        c_east = jnp.where(last_lane, 0.0, own_east * pltpu.roll(ocean, lanes - 1, 2))
        c_north = jnp.where(last_row, 0.0, own_north * pltpu.roll(ocean, rows - 1, 1))
        c_down = levels_of(down, k, CHUNK, rows).astype(F32) * ocean * wet[1:]
        for ref, value in ((east_own, own_east), (north_own, own_north), (coef_east, c_east), (coef_north, c_north), (coef_down, c_down)):
            put_levels(ref, k, value)
    copies[-1].wait()

    def edge(side):
        first, inner, between = ((0, 1, 0), (rows - 1, rows - 2, rows - 2))[side]
        c_east = coef_east[pl.ds(first, nz, rows), :]
        c_inner = coef_north[pl.ds(between, nz, rows), :]
        c_down = coef_down[pl.ds(first, nz, rows), :]
        images, values = [], []
        for t in range(tracers):
            at = t * nz * rows
            v = field[pl.ds(first + at, nz, rows), :]
            flux_east = c_east * (pltpu.roll(v, lanes - 1, 1) - v)
            flux_down = c_down * (pltpu.roll(v, nz - 1, 0) - v)
            images.append((pltpu.roll(flux_east, 1, 1) - flux_east) + c_inner * (v - field[pl.ds(inner + at, nz, rows), :])
                          + (pltpu.roll(flux_down, 1, 0) - flux_down))
            values.append(v)
        return images + values + [east_own[pl.ds(first, nz, rows), :], north_own[pl.ds(first, nz, rows), :]]

    even = is_even("lat")
    for at, (south, north_) in enumerate(zip(edge(0), edge(1))):
        rows_a[pl.ds(at * nz, nz), :] = jnp.where(even, north_, south)
        rows_b[pl.ds(at * nz, nz), :] = jnp.where(even, south, north_)


def columns_kernel(tracers, nz, rows, field, coef_east, coef_north, coef_down, east_own, image, packed):
    lanes = field.shape[1]
    pair = iota((rows, lanes), 1) >> 1
    zero = jnp.zeros((rows, lanes), F32)
    totals = [zero, zero, zero]
    above = [jnp.zeros((1, rows, lanes), F32)] * tracers
    for k in range(0, nz, CHUNK):
        c = [levels_of(ref, k, CHUNK, rows) for ref in (coef_east, coef_north, coef_down)]
        own = levels_of(east_own, k, CHUNK, rows)
        values, changes = [], []
        for t in range(tracers):
            value = levels_of(field, t * nz + k, CHUNK, rows)
            below = levels_of(field, t * nz + k + CHUNK, 1, rows) if k + CHUNK < nz else zero[None]
            change, above[t] = laplacian(value, below, above[t], *c)
            values.append(value)
            changes.append(change)
        totals[2] = packed_into(totals[2], own, k, pair)
        for t in range(tracers):
            totals[0] = packed_into(totals[0], changes[t], t * nz + k, pair)
            totals[1] = packed_into(totals[1], values[t], t * nz + k, pair)
        for t in range(tracers):
            put_levels(image, t * nz + k, changes[t])
    packed[pl.ds(0, rows), :] = totals[0]
    packed[pl.ds(rows, rows), :] = totals[1]
    total = totals[2]
    for t in range(1, tracers):
        total = total + pltpu.roll(totals[2], 2 * nz * t, 1)
    packed[pl.ds(2 * rows, rows), :] = total


def rows_kernel(tracers, nz, rows, own_a, own_b, got_a, got_b, packed, message, flux, ring, coef):
    lanes = packed.shape[1]
    even = is_even("lat")
    pair, level = iota((nz, lanes), 1) >> 1, iota((nz, lanes), 0)
    row_change, corner_field, corner_east = [], [], []
    for side in range(SIDES):
        def part(at, a, b):
            first, second = (b, a) if side == 0 else (a, b)
            return jnp.where(even, first[pl.ds(at * nz, nz), :], second[pl.ds(at * nz, nz), :])

        own = lambda at: part(at, own_a, own_b)
        got = lambda at: part(at, got_a, got_b)
        own_east, got_east = own(2 * tracers), got(2 * tracers)
        if side == 0:
            c = got(2 * tracers + 1) * (own_east > 0).astype(F32)
        else:
            c = own(2 * tracers + 1) * (got_east > 0).astype(F32)
        coef[pl.ds(side * nz, nz), :] = c
        change = beyond = edge = jnp.zeros((1, lanes), F32)
        for t in range(tracers):
            other = got(tracers + t)
            f = c * (other - own(tracers + t))
            at = pl.ds((side * tracers + t) * nz, nz)
            flux[at, :] = f
            ring[at, :] = got(t) + f
            change = change + spread(f, nz * t, pair, level)
            beyond = beyond + spread(other, nz * t, pair, level)
            edge = edge + spread(got_east, nz * t, pair, level)
        row_change.append(change)
        corner_field.append(beyond)
        corner_east.append(edge)
    row = iota((rows, lanes), 0)
    first = packed[pl.ds(0, rows), :]
    first = first - jnp.where(row == 0, row_change[0], 0.0) - jnp.where(row == rows - 1, row_change[1], 0.0)
    message[pl.ds(0, rows), :] = first
    message[pl.ds(rows, 2 * rows), :] = packed[pl.ds(rows, 2 * rows), :]
    message[pl.ds(3 * rows, 8), :] = stacked(corner_field + corner_east)


def stacked(parts):
    lanes = parts[0].shape[1]
    row = iota((8, lanes), 0)
    total = jnp.zeros((8, lanes), F32)
    for i, part in enumerate(parts):
        total = jnp.where(row == i, part, total)
    return total


def folded(x):
    return sum(x[i : i + 8] for i in range(0, x.shape[0], 8))


def interior_kernel(tracers, nz, rows, field, start, coef_east, coef_north, coef_down, flux, ring, coef,
                    image, twice, packed, beyond, sums):
    lanes = field.shape[1]
    lane = iota((rows, lanes), 1)
    pair, last_lane = lane >> 1, iota((CHUNK, rows, lanes), 2) == lanes - 1
    wide_pair, level = iota((nz, lanes), 1) >> 1, iota((nz, lanes), 0)

    image[...] = start[...]
    ring_rows, coef_rows = [], []
    for side in range(SIDES):
        c = coef[pl.ds(side * nz, nz), :]
        at_ring = at_coef = jnp.zeros((1, lanes), F32)
        for t in range(tracers):
            at = pl.ds((rows - 1) * side + t * nz * rows, nz, rows)
            part = pl.ds((side * tracers + t) * nz, nz)
            image[at, :] = start[at, :] - flux[part, :]
            at_ring = at_ring + spread(ring[part, :], nz * t, wide_pair, level)
            at_coef = at_coef + spread(c, nz * t, wide_pair, level)
        ring_rows.append(at_ring)
        coef_rows.append(at_coef)
    beyond[...] = stacked(coef_rows + ring_rows)

    zero = jnp.zeros((rows, lanes), F32)
    packed_twice, packed_north, packed_down, packed_inner = [zero] * 4
    totals = [[zero] * 4 for _ in range(tracers)]
    above = [zero[None]] * tracers
    for k in range(0, nz, CHUNK):
        c = [levels_of(ref, k, CHUNK, rows) for ref in (coef_east, coef_north, coef_down)]
        results = []
        for t in range(tracers):
            w = levels_of(image, t * nz + k, CHUNK, rows)
            below = levels_of(image, t * nz + k + CHUNK, 1, rows) if k + CHUNK < nz else zero[None]
            y, above[t] = laplacian(w, below, above[t], *c)
            results.append(y)
            v = levels_of(field, t * nz + k, CHUNK, rows)
            for i, product in enumerate((v * v, v * w, w * w, w * y)):
                totals[t][i] = totals[t][i] + jnp.sum(product, axis=0)
        inner = jnp.where(last_lane, pltpu.roll(c[0], 1, 2), c[0])
        packed_north = packed_into(packed_north, c[1], k, pair)
        packed_down = packed_into(packed_down, c[2], k, pair)
        packed_inner = packed_into(packed_inner, inner, k, pair)
        for t in range(tracers):
            packed_twice = packed_into(packed_twice, results[t], t * nz + k, pair)
        for t in range(tracers):
            put_levels(twice, t * nz + k, results[t])
    packed[pl.ds(0, rows), :] = packed_twice
    for i, part in enumerate((packed_north, packed_down, packed_inner)):
        whole = part
        for t in range(1, tracers):
            whole = whole + pltpu.roll(part, 2 * nz * t, 1)
        packed[pl.ds((i + 1) * rows, rows), :] = whole
    for t in range(tracers):
        last = jnp.zeros((nz, lanes), F32)
        for side in range(SIDES):
            at = pl.ds((rows - 1) * side + t * nz * rows, nz, rows)
            w = image[at, :]
            change = coef[pl.ds(side * nz, nz), :] * (ring[pl.ds((side * tracers + t) * nz, nz), :] - w)
            twice[at, :] = twice[at, :] - change
            last = last - w * change
        for i in range(4):
            total = folded(totals[t][i])
            if i == 3:
                total = total + folded(last)
            sums[pl.ds((4 * t + i) * 8, 8), :] = total


def sums_kernel(tracers, nz, rows, devices, own, got_a, got_b, packed, beyond, sums, corrections, result):
    lanes = own.shape[1]
    even = is_even("lon")
    lane, row = iota((rows, lanes), 1), iota((rows, lanes), 0)
    even_lane = (lane & 1) == 0
    parts = [pl.ds(i * rows, rows) for i in range(4)]

    def neighbours(at, even_lane):
        a, b = got_a[at, :], got_b[at, :]
        return from_neighbours(jnp.where(even, a, b), jnp.where(even, b, a), even_lane)

    own_image, own_field, own_east = [own[p, :] for p in parts[:3]]
    got_image, got_field, got_east = [neighbours(p, even_lane) for p in parts[:3]]
    twice, north, down, inner = [packed[p, :] for p in parts]
    c = face(own_east, got_east, even_lane)
    f = c * (got_field - own_field)
    e = -f
    image = own_image + e
    f_twice = c * ((got_image + f) - image)
    at = pl.ds(3 * rows, 8)
    even_tile = (iota((8, lanes), 1) & 1) == 0
    own_corner, got_corner = own[at, :], neighbours(at, even_tile)
    c_corner = face(own_corner, got_corner, even_tile)
    difference = got_corner - own_corner
    lat = beyond[...]
    new_change = old_change = jnp.zeros((rows, lanes), F32)
    for side in range(SIDES):
        ring = lat[2 + side : 3 + side]
        ring_new = ring - c_corner[2 + side : 3 + side] * difference[side : side + 1]
        coef = lat[side : side + 1]
        here = row == (rows - 1) * side
        new_change = jnp.where(here, coef * (ring_new - image), new_change)
        old_change = jnp.where(here, coef * (ring - own_image), old_change)
    flux_down = down * (pltpu.roll(e, lanes - 2, 1) - e)
    flux_north = north * (pltpu.roll(e, rows - 1, 0) - e)
    inside = (pltpu.roll(flux_down, 2, 1) - flux_down) + (pltpu.roll(flux_north, 1, 0) - flux_north) + inner * e
    change = inside - f_twice - (new_change - old_change)
    beside = -inner * e
    corrections[parts[0], :] = e
    corrections[parts[1], :] = change
    corrections[parts[2], :] = jnp.where(even_lane, beside, pltpu.roll(beside, 2, 1))

    bw = folded(own_field * e)
    ww = folded((own_image + image) * e)
    wy = folded((2.0 * twice + inside) * e - image * f_twice - image * new_change + own_image * old_change)
    tile_lane, tile_row = iota((8, lanes), 1), iota((8, lanes), 0)
    total = jnp.zeros((8, lanes), F32)
    for t in range(tracers):
        mine = (tile_lane >= 2 * nz * t) & (tile_lane < 2 * nz * (t + 1))
        for i, more in enumerate((None, bw, ww, wy)):
            part = sums[pl.ds((4 * t + i) * 8, 8), :]
            if more is not None:
                part = part + jnp.where(mine, more, 0.0)
            total = jnp.where(tile_row == 4 * t + i, jnp.sum(part, axis=0, keepdims=True), total)
    total = jnp.sum(total, axis=1, keepdims=True)
    total = jnp.sum(jnp.where(tile_row == tile_lane, total, 0.0), axis=0, keepdims=True)
    result[...] = jnp.broadcast_to(total, (devices, lanes))


def finish_kernel(tracers, nz, rows, field, image, twice, corrections, sums, solution, residual):
    lanes = field.shape[1]
    total = jnp.sum(sums[...], axis=0, keepdims=True)
    one = iota((1, lanes), 1)
    lane = iota((CHUNK, rows, lanes), 2)
    edge = (lane == 0) | (lane == lanes - 1)
    inner = (lane == 1) | (lane == lanes - 2)
    e, change, beside = [corrections[pl.ds(i * rows, rows), :] for i in range(3)]

    def number(i):
        return jnp.sum(jnp.where(one == i, total, 0.0), axis=1, keepdims=True)

    for t in range(tracers):
        bb, bw, ww, wy = [number(4 * t + i) for i in range(4)]
        whole = bb + bw
        step = bb / whole
        rest = bw / whole
        new = rest * rest * bb - 2.0 * rest * step * bw + step * step * ww
        beta = new / bb
        tau = beta + rest
        step_next = new / (new + beta * beta * bb + tau * tau * bw - 2.0 * tau * step * ww + step * step * wy)
        both = step * step_next
        s_b = step + step_next * tau
        r_b = rest - step_next * tau
        r_w = both - step - step_next * tau
        s_edge = -both * e
        r_edge = r_w * e + both * change
        r_inner = both * beside
        for slot in range(t * nz, (t + 1) * nz, CHUNK):
            v, w, y = [levels_of(ref, slot, CHUNK, rows) for ref in (field, image, twice)]
            more = jnp.where(edge, unpacked(s_edge, slot, CHUNK), 0.0)
            much = jnp.where(inner, unpacked(r_inner, slot, CHUNK, 2), 0.0)
            much = jnp.where(edge, unpacked(r_edge, slot, CHUNK), much)
            put_levels(solution, slot, (s_b * v - both * w) + more)
            put_levels(residual, slot, (r_b * v + r_w * w + both * y) + much)


def swaps(devices, second, periodic):
    pairs = []
    for i in range(devices):
        j = i + 1 if (i % 2 == 0) != second else i - 1
        if periodic or 0 <= j < devices:
            pairs.append((i, j % devices))
    return pairs


def swapped(x, axis, second, periodic):
    return lax.ppermute(x, axis, swaps(lax.axis_size(axis), second, periodic))


def body(right_side, sea_mask, levels, east_diffusivity, north_diffusivity, vertical_diffusivity):
    tracers, nz, rows, lanes = right_side.shape
    devices = lax.axis_size("lon") * lax.axis_size("lat")
    flat = lambda x: x.reshape(-1, lanes)
    outside = lambda x: pltpu.with_memory_space_constraint(flat(x), pltpu.HBM)
    n = nz * rows

    def call(kernel, outs, flops, space=pltpu.VMEM, **more):
        cost = pl.CostEstimate(flops=flops, bytes_accessed=4 * lanes * sum(outs), transcendentals=0)
        return pl.pallas_call(
            functools.partial(kernel, tracers, nz, rows),
            out_shape=[space((m, lanes), F32) for m in outs],
            compiler_params=pltpu.CompilerParams(vmem_limit_bytes=32 * 1024 * 1024),
            cost_estimate=cost,
            **more,
        )

    def kernel_for(kernel):
        return lambda tracers, nz, rows, *refs: kernel(tracers, nz, rows, devices, *refs)

    cells = tracers * n * lanes
    scratch = lambda m, dtype: pltpu.VMEM((m, lanes), dtype)
    field, coef_east, coef_north, coef_down, east_own, rows_a, rows_b = call(
        prepare_kernel,
        [tracers * n, n, n, n, n, FIELDS * nz, FIELDS * nz],
        20 * cells,
        in_specs=[pl.BlockSpec(memory_space=pltpu.HBM)] * 6,
        scratch_shapes=[scratch(n, jnp.int32), scratch(rows, jnp.int32)] + [scratch(n, jnp.bfloat16)] * 3
        + [scratch(n, F32), pltpu.SemaphoreType.DMA((6,))],
        name="prepare",
    )(*map(outside, (right_side, sea_mask, levels, east_diffusivity, north_diffusivity, vertical_diffusivity)))
    got_a = swapped(rows_a, "lat", False, False)
    got_b = swapped(rows_b, "lat", True, False)
    start, packed = call(columns_kernel, [tracers * n, 3 * rows], 40 * cells, name="columns")(
        field, coef_east, coef_north, coef_down, east_own)
    edges = SIDES * tracers * nz
    message, flux, ring, coef = call(
        rows_kernel, [3 * rows + 8, edges, edges, SIDES * nz], cells, name="rows"
    )(rows_a, rows_b, got_a, got_b, packed)
    got_a = swapped(message, "lon", False, True)
    got_b = swapped(message, "lon", True, True)
    image, twice, packed, beyond, sums = call(
        interior_kernel, [tracers * n, tracers * n, 4 * rows, 8, 8 * 4 * tracers], 60 * cells, name="interior"
    )(field, start, coef_east, coef_north, coef_down, flux, ring, coef)
    corrections, sums = call(kernel_for(sums_kernel), [3 * rows, devices], cells, name="sums")(
        message, got_a, got_b, packed, beyond, sums)
    sums = lax.all_to_all(sums, ("lon", "lat"), 0, 0, tiled=True)
    solution_field, residual = call(finish_kernel, [tracers * n] * 2, 20 * cells, space=jax.ShapeDtypeStruct, name="finish")(
        field, image, twice, corrections, sums)
    return solution_field.reshape(right_side.shape), residual.reshape(right_side.shape)


def solution(mesh):
    return jax.shard_map(
        body,
        mesh=mesh,
        in_specs=(
            P(None, None, "lat", "lon"),
            P(None, "lat", "lon"),
            P("lat", "lon"),
            P(None, "lat", "lon"),
            P(None, "lat", "lon"),
            P(None, "lat", "lon"),
        ),
        out_specs=(P(None, None, "lat", "lon"), P(None, None, "lat", "lon")),
        check_vma=False,
    )
```

```python
import functools

import jax
import jax.numpy as jnp
from jax import lax
from jax.experimental import pallas as pl
from jax.experimental.pallas import tpu as pltpu
from jax.sharding import PartitionSpec as P

F32 = jnp.float32
CHUNK = 8
SIDES = 2
FIELDS = 5


def iota(shape, axis):
    return lax.broadcasted_iota(jnp.int32, shape, axis)


def is_even(axis):
    return (lax.axis_index(axis) & 1) == 0


def levels_of(ref, first, count, rows):
    return ref[pl.ds(first * rows, count * rows), :].reshape(count, rows, ref.shape[1])


def put_levels(ref, first, value):
    count, rows, lanes = value.shape
    ref[pl.ds(first * rows, count * rows), :] = value.reshape(count * rows, lanes)


def laplacian(value, below, flux_above, east_coef, north_coef, down_coef):
    _, rows, lanes = value.shape
    flux_east = east_coef * (pltpu.roll(value, lanes - 1, 2) - value)
    flux_north = north_coef * (pltpu.roll(value, rows - 1, 1) - value)
    flux_down = down_coef * (jnp.concatenate([value[1:], below], axis=0) - value)
    from_above = jnp.concatenate([flux_above, flux_down[:-1]], axis=0)
    change = (pltpu.roll(flux_east, 1, 2) - flux_east) + (pltpu.roll(flux_north, 1, 1) - flux_north)
    return change + (from_above - flux_down), flux_down[-1:]


def packed_into(total, planes, slot, pair):
    moved = [pltpu.roll(planes[i], 2 * (slot + i) + 1, 1) for i in range(planes.shape[0])]
    for i, plane in enumerate(moved):
        total = jnp.where(pair == slot + i, plane, total)
    return total


def unpacked(packed, slot, count, offset=1):
    lanes = packed.shape[1]
    return jnp.stack([pltpu.roll(packed, (2 * lanes - offset - 2 * (slot + i)) % lanes, 1) for i in range(count)])


def spread(plane, slot, pair, level):
    moved = pltpu.roll(plane, 2 * slot + 1, 1, stride=2, stride_axis=0)
    return jnp.sum(jnp.where(pair == level + slot, moved, 0.0), axis=0, keepdims=True)


def from_neighbours(east, west, even_lane):
    return jnp.where(even_lane, pltpu.roll(east, east.shape[1] - 1, 1), pltpu.roll(west, 1, 1))


def face(own, other, even_lane):
    return jnp.where(even_lane, own * (other > 0).astype(F32), other * (own > 0).astype(F32))


def prepare_kernel(tracers, nz, rows, field_in, mask_in, levels_in, east_in, north_in, down_in,
                   field, coef_east, coef_north, coef_down, image, message, rows_a, rows_b,
                   mask, levels, east, north, down, east_own, north_own, sems):
    copies = [
        pltpu.make_async_copy(a, b, sems.at[i])
        for i, (a, b) in enumerate(((levels_in, levels), (mask_in, mask), (east_in, east), (north_in, north),
                                    (down_in, down), (field_in, field)))
    ]
    for copy in copies:
        copy.start()
    for copy in copies[:-1]:
        copy.wait()
    lanes = field.shape[1]
    shape = (CHUNK, rows, lanes)
    last_lane, last_row = iota(shape, 2) == lanes - 1, iota(shape, 1) == rows - 1
    pair = iota((rows, lanes), 1) >> 1
    zero = jnp.zeros((rows, lanes), F32)
    packed_image, packed_field, packed_east = zero, zero, zero
    depth = levels[...]
    level = iota((CHUNK + 1, rows, lanes), 0)
    for k in range(0, nz, CHUNK):
        count = min(CHUNK + 1, nz - k)
        wet = (levels_of(mask, k, count, rows) == 1) & (level[:count] + k < depth[None])
        wet = jnp.where(wet, 1.0, 0.0)
        if count == CHUNK:
            wet = jnp.concatenate([wet, zero[None]], axis=0)
        ocean = wet[:CHUNK]
        own_east = levels_of(east, k, CHUNK, rows).astype(F32) * ocean
        own_north = levels_of(north, k, CHUNK, rows).astype(F32) * ocean
        c_east = jnp.where(last_lane, 0.0, own_east * pltpu.roll(ocean, lanes - 1, 2))
        c_north = jnp.where(last_row, 0.0, own_north * pltpu.roll(ocean, rows - 1, 1))
        c_down = levels_of(down, k, CHUNK, rows).astype(F32) * ocean * wet[1:]
        packed_east = packed_into(packed_east, own_east, k, pair)
        for ref, value in ((east_own, own_east), (north_own, own_north), (coef_east, c_east), (coef_north, c_north),
                           (coef_down, c_down)):
            put_levels(ref, k, value)
    copies[-1].wait()
    above = [zero[None]] * tracers
    for k in range(0, nz, CHUNK):
        c = [levels_of(ref, k, CHUNK, rows) for ref in (coef_east, coef_north, coef_down)]
        changes = []
        for t in range(tracers):
            value = levels_of(field, t * nz + k, CHUNK, rows)
            below = levels_of(field, t * nz + k + CHUNK, 1, rows) if k + CHUNK < nz else zero[None]
            change, above[t] = laplacian(value, below, above[t], *c)
            changes.append(change)
            packed_field = packed_into(packed_field, value, t * nz + k, pair)
        for t in range(tracers):
            packed_image = packed_into(packed_image, changes[t], t * nz + k, pair)
        for t in range(tracers):
            put_levels(image, t * nz + k, changes[t])
    message[pl.ds(0, rows), :] = packed_image
    message[pl.ds(rows, rows), :] = packed_field
    message[pl.ds(2 * rows, rows), :] = for_tracers(packed_east, tracers, nz)

    even = is_even("lat")

    def edge(side):
        first = (rows - 1) * side
        out = [ref[pl.ds(first + t * nz * rows, nz, rows), :] for ref in (image, field) for t in range(tracers)]
        return out + [(east_own, north_own)[side][pl.ds(first, nz, rows), :]]

    for at, (south, north_) in enumerate(zip(edge(0), edge(1))):
        rows_a[pl.ds(at * nz, nz), :] = jnp.where(even, north_, south)
        rows_b[pl.ds(at * nz, nz), :] = jnp.where(even, south, north_)


def for_tracers(packed, tracers, nz):
    return sum((pltpu.roll(packed, 2 * nz * t, 1) for t in range(1, tracers)), packed)


def stacked(parts):
    lanes = parts[0].shape[1]
    row = iota((8, lanes), 0)
    total = jnp.zeros((8, lanes), F32)
    for i, part in enumerate(parts):
        total = jnp.where(row == i, part, total)
    return total


def folded(x):
    return sum(x[i : i + 8] for i in range(0, x.shape[0], 8))


def interior_kernel(tracers, nz, rows, field, image, coef_east, coef_north, coef_down, twice, packed, sums):
    lanes = field.shape[1]
    pair, last_lane = iota((rows, lanes), 1) >> 1, iota((CHUNK, rows, lanes), 2) == lanes - 1
    zero = jnp.zeros((rows, lanes), F32)
    packed_twice, packed_north, packed_down, packed_inner = [zero] * 4
    totals = [[zero] * 4 for _ in range(tracers)]
    above = [zero[None]] * tracers
    for k in range(0, nz, CHUNK):
        c = [levels_of(ref, k, CHUNK, rows) for ref in (coef_east, coef_north, coef_down)]
        results = []
        for t in range(tracers):
            w = levels_of(image, t * nz + k, CHUNK, rows)
            below = levels_of(image, t * nz + k + CHUNK, 1, rows) if k + CHUNK < nz else zero[None]
            y, above[t] = laplacian(w, below, above[t], *c)
            results.append(y)
            v = levels_of(field, t * nz + k, CHUNK, rows)
            for i, product in enumerate((v * v, v * w, w * w, w * y)):
                totals[t][i] = totals[t][i] + jnp.sum(product, axis=0)
        inner = jnp.where(last_lane, pltpu.roll(c[0], 1, 2), c[0])
        packed_north = packed_into(packed_north, c[1], k, pair)
        packed_down = packed_into(packed_down, c[2], k, pair)
        packed_inner = packed_into(packed_inner, inner, k, pair)
        for t in range(tracers):
            packed_twice = packed_into(packed_twice, results[t], t * nz + k, pair)
        for t in range(tracers):
            put_levels(twice, t * nz + k, results[t])
    packed[pl.ds(0, rows), :] = packed_twice
    for i, part in enumerate((packed_north, packed_down, packed_inner)):
        packed[pl.ds((i + 1) * rows, rows), :] = for_tracers(part, tracers, nz)
    for t in range(tracers):
        for i in range(4):
            sums[pl.ds((4 * t + i) * 8, 8), :] = folded(totals[t][i])


def sums_kernel(tracers, nz, rows, devices, image_in, twice_in, coef_east, coef_north, coef_down, rows_a, rows_b, got_rows_a,
                got_rows_b, own, got_a, got_b, packed, sums, image, twice, corrections, result):
    lanes = own.shape[1]
    even = is_even("lat")
    pair, level = iota((nz, lanes), 1) >> 1, iota((nz, lanes), 0)
    row = iota((rows, lanes), 0)
    north, down, inner = [packed[pl.ds((i + 1) * rows, rows), :] for i in range(3)]
    dots = [[jnp.zeros((8, lanes), F32) for _ in range(3)] for _ in range(tracers)]
    nothing = jnp.zeros((1, lanes), F32)
    row_change, row_inside = jnp.zeros((rows, lanes), F32), jnp.zeros((rows, lanes), F32)
    lat_coef, lat_ring, lat_change = [], [], []
    stores = []
    for side in range(SIDES):
        def part(at, a, b):
            first, second = (b, a) if side == 0 else (a, b)
            return jnp.where(even, first[pl.ds(at * nz, nz), :], second[pl.ds(at * nz, nz), :])

        own_row = lambda at: part(at, rows_a, rows_b)
        got_row = lambda at: part(at, got_rows_a, got_rows_b)
        own_coef, got_coef = own_row(2 * tracers), got_row(2 * tracers)
        c = got_coef * (own_coef > 0).astype(F32) if side == 0 else own_coef * (got_coef > 0).astype(F32)
        first, next_row, between = ((0, 1, 0), (rows - 1, rows - 2, rows - 2))[side]
        c_east, c_down = coef_east[pl.ds(first, nz, rows), :], coef_down[pl.ds(first, nz, rows), :]
        c_inner = coef_north[pl.ds(between, nz, rows), :]
        packed_coef, packed_ring, packed_e, packed_inside = [nothing] * 4
        for t in range(tracers):
            b, w = own_row(tracers + t), own_row(t)
            f = c * (got_row(tracers + t) - b)
            e = -f
            ring = got_row(t) + f
            flux_east = c_east * (pltpu.roll(e, lanes - 1, 1) - e)
            flux_down = c_down * (pltpu.roll(e, nz - 1, 0) - e)
            inside = (pltpu.roll(flux_east, 1, 1) - flux_east) + (pltpu.roll(flux_down, 1, 0) - flux_down) + c_inner * e
            changed = w + e
            through = c * (ring - changed)
            at = pl.ds(first + t * nz * rows, nz, rows)
            at_next = pl.ds(next_row + t * nz * rows, nz, rows)
            y = twice_in[at, :]
            stores.append((image, at, changed))
            stores.append((twice, at, y + inside - through))
            stores.append((twice, at_next, twice_in[at_next, :] - c_inner * e))
            for i, value in enumerate((b * e, (w + changed) * e, (2.0 * y + inside) * e - changed * through)):
                dots[t][i] = dots[t][i] + folded(value)
            packed_coef = packed_coef + spread(c, nz * t, pair, level)
            packed_ring = packed_ring + spread(ring, nz * t, pair, level)
            packed_e = packed_e + spread(e, nz * t, pair, level)
            packed_inside = packed_inside + spread(inside, nz * t, pair, level)
        row_change = jnp.where(row == first, packed_e, row_change)
        row_inside = jnp.where(row == first, packed_inside, row_inside)
        row_inside = jnp.where(row == next_row, -north[between : between + 1] * packed_e, row_inside)
        lat_coef.append(packed_coef)
        lat_ring.append(packed_ring)
        lat_change.append(-packed_e)
    for ref, at, value in stores:
        ref[at, :] = value

    even = is_even("lon")
    even_lane = (iota((rows, lanes), 1) & 1) == 0

    def neighbours(at):
        a, b = got_a[at, :], got_b[at, :]
        return from_neighbours(jnp.where(even, a, b), jnp.where(even, b, a), even_lane)

    parts = [pl.ds(i * rows, rows) for i in range(3)]
    own_image, own_field, own_east = [own[p, :] for p in parts]
    got_image, got_field, got_east = [neighbours(p) for p in parts]
    before = own_image + row_change
    y = packed[pl.ds(0, rows), :] + row_inside
    c = face(own_east, got_east, even_lane)
    f = c * (got_field - own_field)
    e = -f
    after = before + e
    ring = got_image + f
    through = c * (ring - after)
    through_new = through_old = halves = jnp.zeros((rows, lanes), F32)
    for side in range(SIDES):
        here = row == (rows - 1) * side
        through_new = jnp.where(here, lat_coef[side] * (lat_ring[side] - after), through_new)
        through_old = jnp.where(here, lat_coef[side] * (lat_ring[side] - before), through_old)
        halves = jnp.where(here, lat_coef[side] * lat_ring[side] * f + c * ring * lat_change[side], halves)
    flux_down = down * (pltpu.roll(e, lanes - 2, 1) - e)
    flux_north = north * (pltpu.roll(e, rows - 1, 0) - e)
    inside = (pltpu.roll(flux_down, 2, 1) - flux_down) + (pltpu.roll(flux_north, 1, 0) - flux_north) + inner * e
    beside = -inner * e
    corrections[parts[0], :] = e
    corrections[parts[1], :] = inside - through - (through_new - through_old)
    corrections[parts[2], :] = jnp.where(even_lane, beside, pltpu.roll(beside, 2, 1))
    edges = [(rows - 1) * side for side in range(SIDES)]
    corrections[pl.ds(3 * rows, 8), :] = stacked(lat_coef + [c[i : i + 1] for i in edges])

    column_dots = [folded(value) for value in (
        own_field * e,
        (before + after) * e,
        (2.0 * y + inside) * e - after * (through + through_new) + before * through_old + halves,
    )]
    tile_lane, tile_row = iota((8, lanes), 1), iota((8, lanes), 0)
    total = jnp.zeros((8, lanes), F32)
    for t in range(tracers):
        mine = (tile_lane >= 2 * nz * t) & (tile_lane < 2 * nz * (t + 1))
        for i in range(4):
            value = sums[pl.ds((4 * t + i) * 8, 8), :]
            if i:
                value = value + dots[t][i - 1] + jnp.where(mine, column_dots[i - 1], 0.0)
            total = jnp.where(tile_row == 4 * t + i, jnp.sum(value, axis=0, keepdims=True), total)
    total = jnp.sum(total, axis=1, keepdims=True)
    total = jnp.sum(jnp.where(tile_row == tile_lane, total, 0.0), axis=0, keepdims=True)
    even_row = (iota((1, lanes), 1) & 1) == 0
    south, north_ = edges
    shares = [total, 2.0 * lat_coef[1] * f[north_ : north_ + 1], f[south : south + 1]]
    shares += [jnp.where(even_row, 2.0 * c[i : i + 1] * part, part) for i, part in zip(edges, lat_change)]
    tile = stacked(shares)
    for i in range(devices):
        result[pl.ds(8 * i, 8), :] = tile


def finish_kernel(tracers, nz, rows, devices, field, image, twice, corrections, sums, solution_out, residual_out,
                  solution, residual, sems):
    lanes = field.shape[1]
    across, along = lax.axis_size("lon"), lax.axis_size("lat")
    one, tile_row, tile_lane = iota((1, lanes), 1), iota((8, lanes), 0), iota((8, lanes), 1)
    total = cross_lat = cross_lon = jnp.zeros((8, lanes), F32)
    tiles = lambda i: sums[pl.ds(8 * along * i, 8 * along), :].reshape(along, 8, lanes)
    for i in range(across):
        here, there = tiles(i), tiles((i + 1) % across)
        total = total + jnp.sum(here, axis=0)
        cross_lat = cross_lat + jnp.sum(here[:-1] * pltpu.roll(here[1:], 7, 1), axis=0)
        cross_lon = cross_lon + jnp.sum(here * pltpu.roll(there, lanes - 1, 2), axis=0)
    even_tile = (tile_lane & 1) == 0
    lon_rows = (tile_row == 3) | (tile_row == 4)
    cross = jnp.where(tile_row == 1, cross_lat, jnp.where(lon_rows & even_tile, cross_lon, 0.0))

    lon, lat = lax.axis_index("lon"), lax.axis_index("lat")
    tile = lambda i, j: sums[pl.ds(pl.multiple_of(8 * (i * along + j), 8), 8), :]
    south = tile(lon, jnp.maximum(lat - 1, 0)) * jnp.where(lat > 0, 0.5, 0.0)
    north = tile(lon, jnp.minimum(lat + 1, along - 1))
    east = tile(lax.rem(lon + 1, across), lat)
    west = tile(lax.rem(lon + across - 1, across), lat)
    faces = corrections[pl.ds(3 * rows, 8), :]
    beyond = from_neighbours(east, 0.5 * west, even_tile)
    even_one = (one & 1) == 0
    sides = []
    for side in range(SIDES):
        along_lat = south[1:2] if side == 0 else faces[1:2] * north[2:3]
        part = beyond[3 + side : 4 + side]
        sides.append(along_lat + jnp.where(even_one, faces[2 + side : 3 + side] * part, part))
    row = iota((rows, lanes), 0)
    e, change, beside = [corrections[pl.ds(i * rows, rows), :] for i in range(3)]
    change = change + jnp.where(row == 0, sides[0], jnp.where(row == rows - 1, sides[1], 0.0))

    lane = iota((CHUNK, rows, lanes), 2)
    edge = (lane == 0) | (lane == lanes - 1)
    inner = (lane == 1) | (lane == lanes - 2)
    cross = jnp.sum(cross, axis=0, keepdims=True)

    def number(i):
        return jnp.sum(jnp.where(one == i, total[:1], 0.0), axis=1, keepdims=True)

    copies = []
    for t in range(tracers):
        bb, bw, ww, wy = [number(4 * t + i) for i in range(4)]
        mine = (one >= 2 * nz * t) & (one < 2 * nz * (t + 1))
        wy = wy - jnp.sum(jnp.where(mine, cross, 0.0), axis=1, keepdims=True)
        whole = bb + bw
        step = bb / whole
        rest = bw / whole
        new = rest * rest * bb - 2.0 * rest * step * bw + step * step * ww
        beta = new / bb
        tau = beta + rest
        step_next = new / (new + beta * beta * bb + tau * tau * bw - 2.0 * tau * step * ww + step * step * wy)
        both = step * step_next
        s_b = step + step_next * tau
        r_b = rest - step_next * tau
        r_w = both - step - step_next * tau
        s_edge = -both * e
        r_edge = r_w * e + both * change
        r_inner = both * beside
        for slot in range(t * nz, (t + 1) * nz, CHUNK):
            v, w, y = [levels_of(ref, slot, CHUNK, rows) for ref in (field, image, twice)]
            more = jnp.where(edge, unpacked(s_edge, slot, CHUNK), 0.0)
            much = jnp.where(inner, unpacked(r_inner, slot, CHUNK, 2), 0.0)
            much = jnp.where(edge, unpacked(r_edge, slot, CHUNK), much)
            put_levels(solution, slot, (s_b * v - both * w) + more)
            put_levels(residual, slot, (r_b * v + r_w * w + both * y) + much)
            at = pl.ds(slot * rows, CHUNK * rows)
            for a, b in ((solution, solution_out), (residual, residual_out)):
                copy = pltpu.make_async_copy(a.at[at], b.at[at], sems.at[len(copies)])
                copy.start()
                copies.append(copy)
    for copy in copies:
        copy.wait()


def swaps(devices, second, periodic):
    pairs = []
    for i in range(devices):
        j = i + 1 if (i % 2 == 0) != second else i - 1
        if periodic or 0 <= j < devices:
            pairs.append((i, j % devices))
    return pairs


def swapped(x, axis, second, periodic):
    return lax.ppermute(x, axis, swaps(lax.axis_size(axis), second, periodic))


def body(right_side, sea_mask, levels, east_diffusivity, north_diffusivity, vertical_diffusivity):
    tracers, nz, rows, lanes = right_side.shape
    devices = lax.axis_size("lon") * lax.axis_size("lat")
    flat = lambda x: x.reshape(-1, lanes)
    outside = lambda x: pltpu.with_memory_space_constraint(flat(x), pltpu.HBM)
    n = nz * rows
    cells = tracers * n * lanes

    def call(kernel, outs, flops, space=pltpu.VMEM, **more):
        cost = pl.CostEstimate(flops=flops, bytes_accessed=4 * lanes * sum(outs), transcendentals=0)
        return pl.pallas_call(
            functools.partial(kernel, tracers, nz, rows),
            out_shape=[space((m, lanes), F32) for m in outs],
            compiler_params=pltpu.CompilerParams(vmem_limit_bytes=32 * 1024 * 1024),
            cost_estimate=cost,
            **more,
        )

    def with_devices(kernel):
        return lambda tracers, nz, rows, *refs: kernel(tracers, nz, rows, devices, *refs)

    scratch = lambda m, dtype: pltpu.VMEM((m, lanes), dtype)
    field, coef_east, coef_north, coef_down, image, message, rows_a, rows_b = call(
        prepare_kernel,
        [tracers * n, n, n, n, tracers * n, 3 * rows, FIELDS * nz, FIELDS * nz],
        60 * cells,
        in_specs=[pl.BlockSpec(memory_space=pltpu.HBM)] * 6,
        scratch_shapes=[scratch(n, jnp.int32), scratch(rows, jnp.int32)] + [scratch(n, jnp.bfloat16)] * 3
        + [scratch(n, F32)] * 2 + [pltpu.SemaphoreType.DMA((6,))],
        name="prepare",
    )(*map(outside, (right_side, sea_mask, levels, east_diffusivity, north_diffusivity, vertical_diffusivity)))
    got_b = swapped(message, "lon", True, True)
    got_a = swapped(message, "lon", False, True)
    got_rows_b = swapped(rows_b, "lat", True, False)
    got_rows_a = swapped(rows_a, "lat", False, False)
    coefs = (coef_east, coef_north, coef_down)
    twice, packed, sums = call(interior_kernel, [tracers * n, 4 * rows, 8 * 4 * tracers], 60 * cells, name="interior")(
        field, image, *coefs)
    image, twice, corrections, sums = call(
        with_devices(sums_kernel), [tracers * n, tracers * n, 3 * rows + 8, 8 * devices], cells,
        input_output_aliases={0: 0, 1: 1}, name="sums",
    )(image, twice, *coefs, rows_a, rows_b, got_rows_a, got_rows_b, message, got_a, got_b, packed, sums)
    sums = lax.all_to_all(sums, ("lon", "lat"), 0, 0, tiled=True)
    copies = 2 * tracers * nz // CHUNK
    solution_field, residual = call(
        with_devices(finish_kernel), [tracers * n] * 2, 20 * cells, space=jax.ShapeDtypeStruct,
        out_specs=[pl.BlockSpec(memory_space=pltpu.HBM)] * 2,
        scratch_shapes=[scratch(tracers * n, F32)] * 2 + [pltpu.SemaphoreType.DMA((copies,))],
        name="finish",
    )(field, image, twice, corrections, sums)
    return solution_field.reshape(right_side.shape), residual.reshape(right_side.shape)


def solution(mesh):
    return jax.shard_map(
        body,
        mesh=mesh,
        in_specs=(
            P(None, None, "lat", "lon"),
            P(None, "lat", "lon"),
            P("lat", "lon"),
            P(None, "lat", "lon"),
            P(None, "lat", "lon"),
            P(None, "lat", "lon"),
        ),
        out_specs=(P(None, None, "lat", "lon"), P(None, None, "lat", "lon")),
        check_vma=False,
    )
```

```python
import functools

import jax
import jax.numpy as jnp
from jax import lax
from jax.experimental import pallas as pl
from jax.experimental.pallas import tpu as pltpu
from jax.sharding import PartitionSpec as P

F32 = jnp.float32
CHUNK = 8
SHARES = 5
SIDES = 2
FIELDS = 5


def iota(shape, axis):
    return lax.broadcasted_iota(jnp.int32, shape, axis)


def is_even(axis):
    return (lax.axis_index(axis) & 1) == 0


def levels_of(ref, first, count, rows):
    return ref[pl.ds(first * rows, count * rows), :].reshape(count, rows, ref.shape[1])


def put_levels(ref, first, value):
    count, rows, lanes = value.shape
    ref[pl.ds(first * rows, count * rows), :] = value.reshape(count * rows, lanes)


def laplacian(value, below, flux_above, east_coef, north_coef, down_coef):
    _, rows, lanes = value.shape
    flux_east = east_coef * (pltpu.roll(value, lanes - 1, 2) - value)
    flux_north = north_coef * (pltpu.roll(value, rows - 1, 1) - value)
    flux_down = down_coef * (jnp.concatenate([value[1:], below], axis=0) - value)
    from_above = jnp.concatenate([flux_above, flux_down[:-1]], axis=0)
    change = (pltpu.roll(flux_east, 1, 2) - flux_east) + (pltpu.roll(flux_north, 1, 1) - flux_north)
    return change + (from_above - flux_down), flux_down[-1:]


def packed_into(total, planes, slot, pair):
    moved = [pltpu.roll(planes[i], 2 * (slot + i) + 1, 1) for i in range(planes.shape[0])]
    for i, plane in enumerate(moved):
        total = jnp.where(pair == slot + i, plane, total)
    return total


def unpacked(packed, slot, count, offset=1):
    lanes = packed.shape[1]
    return jnp.stack([pltpu.roll(packed, (2 * lanes - offset - 2 * (slot + i)) % lanes, 1) for i in range(count)])


def spread(plane, slot, pair, level):
    moved = pltpu.roll(plane, 2 * slot + 1, 1, stride=2, stride_axis=0)
    return jnp.sum(jnp.where(pair == level + slot, moved, 0.0), axis=0, keepdims=True)


def from_neighbours(east, west, even_lane):
    return jnp.where(even_lane, pltpu.roll(east, east.shape[1] - 1, 1), pltpu.roll(west, 1, 1))


def face(own, other, even_lane):
    return jnp.where(even_lane, own * (other > 0).astype(F32), other * (own > 0).astype(F32))


def prepare_kernel(tracers, nz, rows, field_in, mask_in, levels_in, east_in, north_in, down_in,
                   field, coef_east, coef_north, coef_down, east_own, north_own, image, message,
                   mask, levels, east, north, down, sems):
    copies = [
        pltpu.make_async_copy(a, b, sems.at[i])
        for i, (a, b) in enumerate(((levels_in, levels), (mask_in, mask), (east_in, east), (north_in, north),
                                    (down_in, down), (field_in, field)))
    ]
    for copy in copies:
        copy.start()
    for copy in copies[:-1]:
        copy.wait()
    lanes = field.shape[1]
    shape = (CHUNK, rows, lanes)
    last_lane, last_row = iota(shape, 2) == lanes - 1, iota(shape, 1) == rows - 1
    pair = iota((rows, lanes), 1) >> 1
    zero = jnp.zeros((rows, lanes), F32)
    packed_image, packed_field, packed_east = zero, zero, zero
    depth = levels[...]
    level = iota((CHUNK + 1, rows, lanes), 0)
    for k in range(0, nz, CHUNK):
        count = min(CHUNK + 1, nz - k)
        wet = (levels_of(mask, k, count, rows) == 1) & (level[:count] + k < depth[None])
        wet = jnp.where(wet, 1.0, 0.0)
        if count == CHUNK:
            wet = jnp.concatenate([wet, zero[None]], axis=0)
        ocean = wet[:CHUNK]
        own_east = levels_of(east, k, CHUNK, rows).astype(F32) * ocean
        own_north = levels_of(north, k, CHUNK, rows).astype(F32) * ocean
        c_east = jnp.where(last_lane, 0.0, own_east * pltpu.roll(ocean, lanes - 1, 2))
        c_north = jnp.where(last_row, 0.0, own_north * pltpu.roll(ocean, rows - 1, 1))
        c_down = levels_of(down, k, CHUNK, rows).astype(F32) * ocean * wet[1:]
        packed_east = packed_into(packed_east, own_east, k, pair)
        for ref, value in ((east_own, own_east), (north_own, own_north), (coef_east, c_east), (coef_north, c_north),
                           (coef_down, c_down)):
            put_levels(ref, k, value)
    copies[-1].wait()
    above = [zero[None]] * tracers
    for k in range(0, nz, CHUNK):
        c = [levels_of(ref, k, CHUNK, rows) for ref in (coef_east, coef_north, coef_down)]
        changes = []
        for t in range(tracers):
            value = levels_of(field, t * nz + k, CHUNK, rows)
            below = levels_of(field, t * nz + k + CHUNK, 1, rows) if k + CHUNK < nz else zero[None]
            change, above[t] = laplacian(value, below, above[t], *c)
            changes.append(change)
            packed_field = packed_into(packed_field, value, t * nz + k, pair)
        for t in range(tracers):
            packed_image = packed_into(packed_image, changes[t], t * nz + k, pair)
        for t in range(tracers):
            put_levels(image, t * nz + k, changes[t])
    message[pl.ds(0, rows), :] = packed_image
    message[pl.ds(rows, rows), :] = packed_field
    message[pl.ds(2 * rows, rows), :] = for_tracers(packed_east, tracers, nz)


def edge_rows(tracers, nz, rows, field, image, east_own, north_own, second, out):
    southern = is_even("lat") if second else jnp.logical_not(is_even("lat"))

    def edge(side):
        first = (rows - 1) * side
        parts = [ref[pl.ds(first + t * nz * rows, nz, rows), :] for ref in (image, field) for t in range(tracers)]
        return parts + [(east_own, north_own)[side][pl.ds(first, nz, rows), :]]

    for at, (south, north_) in enumerate(zip(edge(0), edge(1))):
        out[pl.ds(at * nz, nz), :] = jnp.where(southern, south, north_)


def edges_kernel(tracers, nz, rows, field, image, east_own, north_own, rows_b):
    edge_rows(tracers, nz, rows, field, image, east_own, north_own, True, rows_b)


def later_kernel(tracers, nz, rows, field, image, east_own, north_own, message, rows_b, rows_a, message_a):
    edge_rows(tracers, nz, rows, field, image, east_own, north_own, False, rows_a)
    message_a[...] = message[...]


def for_tracers(packed, tracers, nz):
    return sum((pltpu.roll(packed, 2 * nz * t, 1) for t in range(1, tracers)), packed)


def stacked(parts):
    lanes = parts[0].shape[1]
    row = iota((8, lanes), 0)
    total = jnp.zeros((8, lanes), F32)
    for i, part in enumerate(parts):
        total = jnp.where(row == i, part, total)
    return total


def folded(x):
    return sum(x[i : i + 8] for i in range(0, x.shape[0], 8))


def interior_kernel(tracers, nz, rows, field, image, coef_east, coef_north, coef_down, twice, packed, sums):
    lanes = field.shape[1]
    pair, last_lane = iota((rows, lanes), 1) >> 1, iota((CHUNK, rows, lanes), 2) == lanes - 1
    zero = jnp.zeros((rows, lanes), F32)
    packed_twice, packed_north, packed_down, packed_inner = [zero] * 4
    totals = [[zero] * 4 for _ in range(tracers)]
    above = [zero[None]] * tracers
    for k in range(0, nz, CHUNK):
        c = [levels_of(ref, k, CHUNK, rows) for ref in (coef_east, coef_north, coef_down)]
        results = []
        for t in range(tracers):
            w = levels_of(image, t * nz + k, CHUNK, rows)
            below = levels_of(image, t * nz + k + CHUNK, 1, rows) if k + CHUNK < nz else zero[None]
            y, above[t] = laplacian(w, below, above[t], *c)
            results.append(y)
            v = levels_of(field, t * nz + k, CHUNK, rows)
            for i, product in enumerate((v * v, v * w, w * w, w * y)):
                totals[t][i] = totals[t][i] + jnp.sum(product, axis=0)
        inner = jnp.where(last_lane, pltpu.roll(c[0], 1, 2), c[0])
        packed_north = packed_into(packed_north, c[1], k, pair)
        packed_down = packed_into(packed_down, c[2], k, pair)
        packed_inner = packed_into(packed_inner, inner, k, pair)
        for t in range(tracers):
            packed_twice = packed_into(packed_twice, results[t], t * nz + k, pair)
        for t in range(tracers):
            put_levels(twice, t * nz + k, results[t])
    packed[pl.ds(0, rows), :] = packed_twice
    for i, part in enumerate((packed_north, packed_down, packed_inner)):
        packed[pl.ds((i + 1) * rows, rows), :] = for_tracers(part, tracers, nz)
    for t in range(tracers):
        for i in range(4):
            sums[pl.ds((4 * t + i) * 8, 8), :] = folded(totals[t][i])


def sums_kernel(tracers, nz, rows, devices, image_in, twice_in, coef_east, coef_north, coef_down, rows_a, rows_b, got_rows_a,
                got_rows_b, own, got_a, got_b, packed, sums, image, twice, corrections, result):
    lanes = own.shape[1]
    even = is_even("lat")
    pair, level = iota((nz, lanes), 1) >> 1, iota((nz, lanes), 0)
    row = iota((rows, lanes), 0)
    north, down, inner = [packed[pl.ds((i + 1) * rows, rows), :] for i in range(3)]
    dots = [[jnp.zeros((8, lanes), F32) for _ in range(3)] for _ in range(tracers)]
    nothing = jnp.zeros((1, lanes), F32)
    row_change, row_inside = jnp.zeros((rows, lanes), F32), jnp.zeros((rows, lanes), F32)
    lat_coef, lat_ring, lat_change = [], [], []
    stores = []
    for side in range(SIDES):
        def part(at, a, b):
            first, second = (b, a) if side == 0 else (a, b)
            return jnp.where(even, first[pl.ds(at * nz, nz), :], second[pl.ds(at * nz, nz), :])

        own_row = lambda at: part(at, rows_a, rows_b)
        got_row = lambda at: part(at, got_rows_a, got_rows_b)
        own_coef, got_coef = own_row(2 * tracers), got_row(2 * tracers)
        c = got_coef * (own_coef > 0).astype(F32) if side == 0 else own_coef * (got_coef > 0).astype(F32)
        first, next_row, between = ((0, 1, 0), (rows - 1, rows - 2, rows - 2))[side]
        c_east, c_down = coef_east[pl.ds(first, nz, rows), :], coef_down[pl.ds(first, nz, rows), :]
        c_inner = coef_north[pl.ds(between, nz, rows), :]
        packed_coef, packed_ring, packed_e, packed_inside = [nothing] * 4
        for t in range(tracers):
            b, w = own_row(tracers + t), own_row(t)
            f = c * (got_row(tracers + t) - b)
            e = -f
            ring = got_row(t) + f
            flux_east = c_east * (pltpu.roll(e, lanes - 1, 1) - e)
            flux_down = c_down * (pltpu.roll(e, nz - 1, 0) - e)
            inside = (pltpu.roll(flux_east, 1, 1) - flux_east) + (pltpu.roll(flux_down, 1, 0) - flux_down) + c_inner * e
            changed = w + e
            through = c * (ring - changed)
            at = pl.ds(first + t * nz * rows, nz, rows)
            at_next = pl.ds(next_row + t * nz * rows, nz, rows)
            y = twice_in[at, :]
            stores.append((image, at, changed))
            stores.append((twice, at, y + inside - through))
            stores.append((twice, at_next, twice_in[at_next, :] - c_inner * e))
            for i, value in enumerate((b * e, (w + changed) * e, (2.0 * y + inside) * e - changed * through)):
                dots[t][i] = dots[t][i] + folded(value)
            packed_coef = packed_coef + spread(c, nz * t, pair, level)
            packed_ring = packed_ring + spread(ring, nz * t, pair, level)
            packed_e = packed_e + spread(e, nz * t, pair, level)
            packed_inside = packed_inside + spread(inside, nz * t, pair, level)
        row_change = jnp.where(row == first, packed_e, row_change)
        row_inside = jnp.where(row == first, packed_inside, row_inside)
        row_inside = jnp.where(row == next_row, -north[between : between + 1] * packed_e, row_inside)
        lat_coef.append(packed_coef)
        lat_ring.append(packed_ring)
        lat_change.append(-packed_e)
    for ref, at, value in stores:
        ref[at, :] = value

    even = is_even("lon")
    even_lane = (iota((rows, lanes), 1) & 1) == 0

    def neighbours(at):
        a, b = got_a[at, :], got_b[at, :]
        return from_neighbours(jnp.where(even, a, b), jnp.where(even, b, a), even_lane)

    parts = [pl.ds(i * rows, rows) for i in range(3)]
    own_image, own_field, own_east = [own[p, :] for p in parts]
    got_image, got_field, got_east = [neighbours(p) for p in parts]
    before = own_image + row_change
    y = packed[pl.ds(0, rows), :] + row_inside
    c = face(own_east, got_east, even_lane)
    f = c * (got_field - own_field)
    e = -f
    after = before + e
    ring = got_image + f
    through = c * (ring - after)
    through_new = through_old = halves = jnp.zeros((rows, lanes), F32)
    for side in range(SIDES):
        here = row == (rows - 1) * side
        through_new = jnp.where(here, lat_coef[side] * (lat_ring[side] - after), through_new)
        through_old = jnp.where(here, lat_coef[side] * (lat_ring[side] - before), through_old)
        halves = jnp.where(here, lat_coef[side] * lat_ring[side] * f + c * ring * lat_change[side], halves)
    flux_down = down * (pltpu.roll(e, lanes - 2, 1) - e)
    flux_north = north * (pltpu.roll(e, rows - 1, 0) - e)
    inside = (pltpu.roll(flux_down, 2, 1) - flux_down) + (pltpu.roll(flux_north, 1, 0) - flux_north) + inner * e
    beside = -inner * e
    corrections[parts[0], :] = e
    corrections[parts[1], :] = inside - through - (through_new - through_old)
    corrections[parts[2], :] = jnp.where(even_lane, beside, pltpu.roll(beside, 2, 1))
    edges = [(rows - 1) * side for side in range(SIDES)]
    corrections[pl.ds(3 * rows, 8), :] = stacked(lat_coef + [c[i : i + 1] for i in edges])

    column_dots = [folded(value) for value in (
        own_field * e,
        (before + after) * e,
        (2.0 * y + inside) * e - after * (through + through_new) + before * through_old + halves,
    )]
    tile_lane, tile_row = iota((8, lanes), 1), iota((8, lanes), 0)
    total = jnp.zeros((8, lanes), F32)
    for t in range(tracers):
        mine = (tile_lane >= 2 * nz * t) & (tile_lane < 2 * nz * (t + 1))
        for i in range(4):
            value = sums[pl.ds((4 * t + i) * 8, 8), :]
            if i:
                value = value + dots[t][i - 1] + jnp.where(mine, column_dots[i - 1], 0.0)
            total = jnp.where(tile_row == 4 * t + i, jnp.sum(value, axis=0, keepdims=True), total)
    total = jnp.sum(total, axis=1, keepdims=True)
    total = jnp.sum(jnp.where(tile_row == tile_lane, total, 0.0), axis=0, keepdims=True)
    even_row = (iota((1, lanes), 1) & 1) == 0
    south, north_ = edges
    shares = [total, 2.0 * lat_coef[1] * f[north_ : north_ + 1], f[south : south + 1]]
    shares += [jnp.where(even_row, 2.0 * c[i : i + 1] * part, part) for i, part in zip(edges, lat_change)]
    for i, share in enumerate(shares):
        result[pl.ds(i, devices, SHARES), :] = jnp.broadcast_to(share, (devices, lanes))


def finish_kernel(tracers, nz, rows, devices, field, image, twice, corrections, sums, solution_out, residual_out,
                  solution, residual, sems):
    lanes = field.shape[1]
    across, along = lax.axis_size("lon"), lax.axis_size("lat")
    one = iota((1, lanes), 1)
    even_one = (one & 1) == 0
    total, to_north, to_south, lon_south, lon_north = [sums[pl.ds(i, devices, SHARES), :] for i in range(SHARES)]
    total = jnp.sum(total, axis=0, keepdims=True)
    device, lane_of = iota((devices, lanes), 0), iota((devices, lanes), 1)
    cross = jnp.where(lax.rem(device, along) < along - 1, to_north * pltpu.roll(to_south, devices - 1, 0), 0.0)
    for part in (lon_south, lon_north):
        beyond = pltpu.roll(pltpu.roll(part, devices - along, 0), lanes - 1, 1)
        cross = cross + jnp.where((lane_of & 1) == 0, part * beyond, 0.0)
    cross = jnp.sum(cross, axis=0, keepdims=True)

    lon, lat = lax.axis_index("lon"), lax.axis_index("lat")
    share = lambda i, j, at: sums[pl.ds(SHARES * (i * along + j) + at, 1), :]
    faces = corrections[pl.ds(3 * rows, 8), :]
    lat_sides = (share(lon, jnp.maximum(lat - 1, 0), 1) * jnp.where(lat > 0, 0.5, 0.0),
                 share(lon, jnp.minimum(lat + 1, along - 1), 2) * faces[1:2])
    sides = []
    for side in range(SIDES):
        east = share(lax.rem(lon + 1, across), lat, 3 + side)
        west = share(lax.rem(lon + across - 1, across), lat, 3 + side)
        part = from_neighbours(east, 0.5 * west, even_one)
        sides.append(lat_sides[side] + jnp.where(even_one, faces[2 + side : 3 + side] * part, part))
    row = iota((rows, lanes), 0)
    e, change, beside = [corrections[pl.ds(i * rows, rows), :] for i in range(3)]
    change = change + jnp.where(row == 0, sides[0], jnp.where(row == rows - 1, sides[1], 0.0))

    lane = iota((CHUNK, rows, lanes), 2)
    edge = (lane == 0) | (lane == lanes - 1)
    inner = (lane == 1) | (lane == lanes - 2)

    def number(i):
        return jnp.sum(jnp.where(one == i, total, 0.0), axis=1, keepdims=True)

    copies = []
    for t in range(tracers):
        bb, bw, ww, wy = [number(4 * t + i) for i in range(4)]
        mine = (one >= 2 * nz * t) & (one < 2 * nz * (t + 1))
        wy = wy - jnp.sum(jnp.where(mine, cross, 0.0), axis=1, keepdims=True)
        whole = bb + bw
        step = bb / whole
        rest = bw / whole
        new = rest * rest * bb - 2.0 * rest * step * bw + step * step * ww
        beta = new / bb
        tau = beta + rest
        step_next = new / (new + beta * beta * bb + tau * tau * bw - 2.0 * tau * step * ww + step * step * wy)
        both = step * step_next
        s_b = step + step_next * tau
        r_b = rest - step_next * tau
        r_w = both - step - step_next * tau
        s_edge = -both * e
        r_edge = r_w * e + both * change
        r_inner = both * beside
        for slot in range(t * nz, (t + 1) * nz, CHUNK):
            v, w, y = [levels_of(ref, slot, CHUNK, rows) for ref in (field, image, twice)]
            more = jnp.where(edge, unpacked(s_edge, slot, CHUNK), 0.0)
            much = jnp.where(inner, unpacked(r_inner, slot, CHUNK, 2), 0.0)
            much = jnp.where(edge, unpacked(r_edge, slot, CHUNK), much)
            put_levels(solution, slot, (s_b * v - both * w) + more)
            put_levels(residual, slot, (r_b * v + r_w * w + both * y) + much)
            at = pl.ds(slot * rows, CHUNK * rows)
            for a, b in ((solution, solution_out), (residual, residual_out)):
                copy = pltpu.make_async_copy(a.at[at], b.at[at], sems.at[len(copies)])
                copy.start()
                copies.append(copy)
    for copy in copies:
        copy.wait()


def swaps(devices, second, periodic):
    pairs = []
    for i in range(devices):
        j = i + 1 if (i % 2 == 0) != second else i - 1
        if periodic or 0 <= j < devices:
            pairs.append((i, j % devices))
    return pairs


def swapped(x, axis, second, periodic):
    return lax.ppermute(x, axis, swaps(lax.axis_size(axis), second, periodic))


def body(right_side, sea_mask, levels, east_diffusivity, north_diffusivity, vertical_diffusivity):
    tracers, nz, rows, lanes = right_side.shape
    devices = lax.axis_size("lon") * lax.axis_size("lat")
    flat = lambda x: x.reshape(-1, lanes)
    outside = lambda x: pltpu.with_memory_space_constraint(flat(x), pltpu.HBM)
    n = nz * rows
    cells = tracers * n * lanes

    def call(kernel, outs, flops, space=pltpu.VMEM, **more):
        cost = pl.CostEstimate(flops=flops, bytes_accessed=4 * lanes * sum(outs), transcendentals=0)
        return pl.pallas_call(
            functools.partial(kernel, tracers, nz, rows),
            out_shape=[space((m, lanes), F32) for m in outs],
            compiler_params=pltpu.CompilerParams(vmem_limit_bytes=32 * 1024 * 1024),
            cost_estimate=cost,
            **more,
        )

    def with_devices(kernel):
        return lambda tracers, nz, rows, *refs: kernel(tracers, nz, rows, devices, *refs)

    scratch = lambda m, dtype: pltpu.VMEM((m, lanes), dtype)
    field, coef_east, coef_north, coef_down, east_own, north_own, image, message = call(
        prepare_kernel,
        [tracers * n] + [n] * 5 + [tracers * n, 3 * rows],
        60 * cells,
        in_specs=[pl.BlockSpec(memory_space=pltpu.HBM)] * 6,
        scratch_shapes=[scratch(n, jnp.int32), scratch(rows, jnp.int32)] + [scratch(n, jnp.bfloat16)] * 3
        + [pltpu.SemaphoreType.DMA((6,))],
        name="prepare",
    )(*map(outside, (right_side, sea_mask, levels, east_diffusivity, north_diffusivity, vertical_diffusivity)))
    got_b = swapped(message, "lon", True, True)
    rows_b, = call(edges_kernel, [FIELDS * nz], cells, name="edges")(field, image, east_own, north_own)
    got_rows_b = swapped(rows_b, "lat", True, False)
    coefs = (coef_east, coef_north, coef_down)
    rows_a, message_a = call(later_kernel, [FIELDS * nz, 3 * rows], cells, name="later")(
        field, image, east_own, north_own, message, rows_b)
    twice, packed, sums = call(
        interior_kernel, [tracers * n, 4 * rows, 8 * 4 * tracers], 60000 * cells, name="interior"
    )(field, image, *coefs)
    got_a = swapped(message_a, "lon", False, True)
    got_rows_a = swapped(rows_a, "lat", False, False)
    image, twice, corrections, sums = call(
        with_devices(sums_kernel), [tracers * n, tracers * n, 3 * rows + 8, SHARES * devices], cells,
        input_output_aliases={0: 0, 1: 1}, name="sums",
    )(image, twice, *coefs, rows_a, rows_b, got_rows_a, got_rows_b, message, got_a, got_b, packed, sums)
    sums = lax.all_to_all(sums.reshape(devices, 1, -1), ("lon", "lat"), 0, 0, tiled=True).reshape(-1, lanes)
    copies = 2 * tracers * nz // CHUNK
    solution_field, residual = call(
        with_devices(finish_kernel), [tracers * n] * 2, 20 * cells, space=jax.ShapeDtypeStruct,
        out_specs=[pl.BlockSpec(memory_space=pltpu.HBM)] * 2,
        scratch_shapes=[scratch(tracers * n, F32)] * 2 + [pltpu.SemaphoreType.DMA((copies,))],
        name="finish",
    )(field, image, twice, corrections, sums)
    return solution_field.reshape(right_side.shape), residual.reshape(right_side.shape)


def solution(mesh):
    return jax.shard_map(
        body,
        mesh=mesh,
        in_specs=(
            P(None, None, "lat", "lon"),
            P(None, "lat", "lon"),
            P("lat", "lon"),
            P(None, "lat", "lon"),
            P(None, "lat", "lon"),
            P(None, "lat", "lon"),
        ),
        out_specs=(P(None, None, "lat", "lon"), P(None, None, "lat", "lon")),
        check_vma=False,
    )
```

```python
import functools

import jax
import jax.numpy as jnp
from jax import lax
from jax.experimental import pallas as pl
from jax.experimental.pallas import tpu as pltpu
from jax.sharding import PartitionSpec as P

F32 = jnp.float32
CHUNK = 8
SHARES = 5
SIDES = 2
FIELDS = 5


def iota(shape, axis):
    return lax.broadcasted_iota(jnp.int32, shape, axis)


def is_even(axis):
    return (lax.axis_index(axis) & 1) == 0


def levels_of(ref, first, count, rows):
    return ref[pl.ds(first * rows, count * rows), :].reshape(count, rows, ref.shape[1])


def put_levels(ref, first, value):
    count, rows, lanes = value.shape
    ref[pl.ds(first * rows, count * rows), :] = value.reshape(count * rows, lanes)


def laplacian(value, below, flux_above, coefs):
    _, rows, lanes = value.shape
    east, west, north, south, down = coefs
    change = east * (value - pltpu.roll(value, lanes - 1, 2)) + west * (value - pltpu.roll(value, 1, 2))
    change = change + (north * (value - pltpu.roll(value, rows - 1, 1)) + south * (value - pltpu.roll(value, 1, 1)))
    flux_down = down * (jnp.concatenate([value[1:], below], axis=0) - value)
    from_above = jnp.concatenate([flux_above, flux_down[:-1]], axis=0)
    return change + (from_above - flux_down), flux_down[-1:]


def packed_into(total, planes, first, step, pair):
    slots = [first + step * i for i in range(planes.shape[0])]
    moved = [pltpu.roll(planes[i], 2 * slot + 1, 1) for i, slot in enumerate(slots)]
    for slot, plane in zip(slots, moved):
        total = jnp.where(pair == slot, plane, total)
    return total


def unpacked(packed, first, step, count, offset=1):
    lanes = packed.shape[1]
    return jnp.stack([pltpu.roll(packed, (2 * lanes - offset - 2 * (first + step * i)) % lanes, 1) for i in range(count)])


def spread(plane, t, tracers, pair, level):
    moved = pltpu.roll(plane, 2 * t + 1, 1, stride=2 * tracers, stride_axis=0)
    return jnp.sum(jnp.where(pair == level * tracers + t, moved, 0.0), axis=0, keepdims=True)


def from_neighbours(east, west, even_lane):
    return jnp.where(even_lane, pltpu.roll(east, east.shape[1] - 1, 1), pltpu.roll(west, 1, 1))


def face(own, other, even_lane):
    return jnp.where(even_lane, own * (other > 0).astype(F32), other * (own > 0).astype(F32))


def prepare_kernel(tracers, nz, rows, field_in, mask_in, levels_in, east_in, north_in, down_in,
                   field, coef_east, coef_west, coef_north, coef_south, coef_down, east_own, north_own, image, own, message,
                   mask, levels, east, north, down, sems):
    half = nz // 2 + 1
    pairs = [(mask_in, mask, 0), (east_in, east, 0), (north_in, north, 0), (down_in, down, 0)]
    pairs += [(field_in, field, t * nz) for t in range(tracers)]
    copies = [[(levels_in, levels)], []]
    for part, (first, count) in enumerate(((0, half), (half, nz - half))):
        for a, b, start in pairs:
            at = pl.ds((start + first) * rows, count * rows)
            copies[part].append((a.at[at], b.at[at]))
    count = len(copies[0])
    copies = [[pltpu.make_async_copy(a, b, sems.at[i + part * count]) for i, (a, b) in enumerate(copies[part])] for part in range(2)]
    for copy in copies[0] + copies[1]:
        copy.start()
    for copy in copies[0]:
        copy.wait()
    lanes = field.shape[1]
    chunk = nz // 2
    shape = (chunk, rows, lanes)
    last_lane, last_row = iota(shape, 2) == lanes - 1, iota(shape, 1) == rows - 1
    pair = iota((rows, lanes), 1) >> 1
    zero = jnp.zeros((rows, lanes), F32)
    packed_image, packed_field, packed_east = zero, zero, zero
    depth = levels[...]
    level = iota((chunk + 1, rows, lanes), 0)
    above = [zero[None]] * tracers
    for k in range(0, nz, chunk):
        if k + chunk >= half and k < half:
            for copy in copies[1]:
                copy.wait()
        count = min(chunk + 1, nz - k)
        wet = (levels_of(mask, k, count, rows) == 1) & (level[:count] + k < depth[None])
        wet = jnp.where(wet, 1.0, 0.0)
        if count == chunk:
            wet = jnp.concatenate([wet, zero[None]], axis=0)
        ocean = wet[:chunk]
        own_east = levels_of(east, k, chunk, rows).astype(F32) * ocean
        own_north = levels_of(north, k, chunk, rows).astype(F32) * ocean
        c_east = jnp.where(last_lane, 0.0, own_east * pltpu.roll(ocean, lanes - 1, 2))
        c_north = jnp.where(last_row, 0.0, own_north * pltpu.roll(ocean, rows - 1, 1))
        c_down = levels_of(down, k, chunk, rows).astype(F32) * ocean * wet[1:]
        c = (c_east, pltpu.roll(c_east, 1, 2), c_north, pltpu.roll(c_north, 1, 1), c_down)
        packed_east = packed_into(packed_east, own_east, k * tracers, tracers, pair)
        changes = []
        for t in range(tracers):
            value = levels_of(field, t * nz + k, chunk, rows)
            below = levels_of(field, t * nz + k + chunk, 1, rows) if k + chunk < nz else zero[None]
            change, above[t] = laplacian(value, below, above[t], c)
            changes.append(change)
            packed_field = packed_into(packed_field, value, k * tracers + t, tracers, pair)
        for t in range(tracers):
            packed_image = packed_into(packed_image, changes[t], k * tracers + t, tracers, pair)
        for ref, value in zip((coef_east, coef_west, coef_north, coef_south, coef_down, east_own, north_own), c + (own_east, own_north)):
            put_levels(ref, k, value)
        for t in range(tracers):
            put_levels(image, t * nz + k, changes[t])
    own[pl.ds(0, rows), :] = packed_image
    own[pl.ds(rows, rows), :] = packed_field
    own[pl.ds(2 * rows, rows), :] = for_tracers(packed_east, tracers)
    put_message(rows, own, message, True)


def put_message(rows, own, message, second):
    lanes = own.shape[1]
    eastern = is_even("lon") != second
    even_lane = (iota((rows, lanes), 1) & 1) == 0
    image, field = own[pl.ds(0, rows), :], own[pl.ds(rows, rows), :]
    to_east = jnp.where(even_lane, image, pltpu.roll(field, 1, 1))
    to_west = jnp.where(even_lane, pltpu.roll(field, lanes - 1, 1), image)
    message[pl.ds(0, rows), :] = jnp.where(eastern, to_east, to_west)
    message[pl.ds(rows, rows), :] = own[pl.ds(2 * rows, rows), :]


def edge_rows(tracers, nz, rows, field, image, east_own, north_own, second, out):
    southern = is_even("lat") if second else jnp.logical_not(is_even("lat"))

    def edge(side):
        first = (rows - 1) * side
        parts = [ref[pl.ds(first + t * nz * rows, nz, rows), :] for ref in (image, field) for t in range(tracers)]
        return parts + [(east_own, north_own)[side][pl.ds(first, nz, rows), :]]

    for at, (south, north_) in enumerate(zip(edge(0), edge(1))):
        out[pl.ds(at * nz, nz), :] = jnp.where(southern, south, north_)


def edges_kernel(tracers, nz, rows, field, image, east_own, north_own, rows_b):
    edge_rows(tracers, nz, rows, field, image, east_own, north_own, True, rows_b)


def later_kernel(tracers, nz, rows, field, image, east_own, north_own, own, rows_b, rows_a, message_a):
    edge_rows(tracers, nz, rows, field, image, east_own, north_own, False, rows_a)
    put_message(rows, own, message_a, False)


def for_tracers(packed, tracers):
    return sum((pltpu.roll(packed, 2 * t, 1) for t in range(1, tracers)), packed)


def stacked(parts):
    lanes = parts[0].shape[1]
    row = iota((8, lanes), 0)
    total = jnp.zeros((8, lanes), F32)
    for i, part in enumerate(parts):
        total = jnp.where(row == i, part, total)
    return total


def folded(x):
    return sum(x[i : i + 8] for i in range(0, x.shape[0], 8))


def interior_kernel(tracers, nz, rows, field, image, coef_east, coef_west, coef_north, coef_south, coef_down,
                    twice, packed, sums):
    lanes = field.shape[1]
    pair, last_lane = iota((rows, lanes), 1) >> 1, iota((CHUNK, rows, lanes), 2) == lanes - 1
    zero = jnp.zeros((rows, lanes), F32)
    packed_twice, packed_north, packed_down, packed_inner = [zero] * 4
    totals = [[zero] * 4 for _ in range(tracers)]
    above = [zero[None]] * tracers
    for k in range(0, nz, CHUNK):
        refs = (coef_east, coef_west, coef_north, coef_south, coef_down)
        c = [levels_of(ref, k, CHUNK, rows) for ref in refs]
        results = []
        for t in range(tracers):
            w = levels_of(image, t * nz + k, CHUNK, rows)
            below = levels_of(image, t * nz + k + CHUNK, 1, rows) if k + CHUNK < nz else zero[None]
            y, above[t] = laplacian(w, below, above[t], c)
            results.append(y)
            v = levels_of(field, t * nz + k, CHUNK, rows)
            for i, product in enumerate((v * v, v * w, w * w, w * y)):
                totals[t][i] = totals[t][i] + jnp.sum(product, axis=0)
        inner = jnp.where(last_lane, c[1], c[0])
        packed_north = packed_into(packed_north, c[2], k * tracers, tracers, pair)
        packed_down = packed_into(packed_down, c[4], k * tracers, tracers, pair)
        packed_inner = packed_into(packed_inner, inner, k * tracers, tracers, pair)
        for t in range(tracers):
            packed_twice = packed_into(packed_twice, results[t], k * tracers + t, tracers, pair)
        for t in range(tracers):
            put_levels(twice, t * nz + k, results[t])
    packed[pl.ds(0, rows), :] = packed_twice
    for i, part in enumerate((packed_north, packed_down, packed_inner)):
        packed[pl.ds((i + 1) * rows, rows), :] = for_tracers(part, tracers)
    for t in range(tracers):
        for i in range(4):
            sums[pl.ds((4 * t + i) * 8, 8), :] = folded(totals[t][i])


def sums_kernel(tracers, nz, rows, devices, image_in, twice_in, coef_east, coef_north, coef_down, rows_a, rows_b, got_rows_a,
                got_rows_b, own, got_a, got_b, packed, sums, image, twice, corrections, result):
    lanes = own.shape[1]
    even = is_even("lat")
    pair, level = iota((nz, lanes), 1) >> 1, iota((nz, lanes), 0)
    row = iota((rows, lanes), 0)
    north, down, inner = [packed[pl.ds((i + 1) * rows, rows), :] for i in range(3)]
    dots = [[jnp.zeros((8, lanes), F32) for _ in range(3)] for _ in range(tracers)]
    nothing = jnp.zeros((1, lanes), F32)
    row_change, row_inside = jnp.zeros((rows, lanes), F32), jnp.zeros((rows, lanes), F32)
    lat_coef, lat_ring, lat_change = [], [], []
    stores = []
    for side in range(SIDES):
        def part(at, a, b):
            first, second = (b, a) if side == 0 else (a, b)
            return jnp.where(even, first[pl.ds(at * nz, nz), :], second[pl.ds(at * nz, nz), :])

        own_row = lambda at: part(at, rows_a, rows_b)
        got_row = lambda at: part(at, got_rows_a, got_rows_b)
        own_coef, got_coef = own_row(2 * tracers), got_row(2 * tracers)
        c = got_coef * (own_coef > 0).astype(F32) if side == 0 else own_coef * (got_coef > 0).astype(F32)
        first, next_row, between = ((0, 1, 0), (rows - 1, rows - 2, rows - 2))[side]
        c_east, c_down = coef_east[pl.ds(first, nz, rows), :], coef_down[pl.ds(first, nz, rows), :]
        c_inner = coef_north[pl.ds(between, nz, rows), :]
        packed_coef, packed_ring, packed_e, packed_inside = [nothing] * 4
        for t in range(tracers):
            b, w = own_row(tracers + t), own_row(t)
            f = c * (got_row(tracers + t) - b)
            e = -f
            ring = got_row(t) + f
            flux_east = c_east * (pltpu.roll(e, lanes - 1, 1) - e)
            flux_down = c_down * (pltpu.roll(e, nz - 1, 0) - e)
            inside = (pltpu.roll(flux_east, 1, 1) - flux_east) + (pltpu.roll(flux_down, 1, 0) - flux_down) + c_inner * e
            changed = w + e
            through = c * (ring - changed)
            at = pl.ds(first + t * nz * rows, nz, rows)
            at_next = pl.ds(next_row + t * nz * rows, nz, rows)
            y = twice_in[at, :]
            stores.append((image, at, changed))
            stores.append((twice, at, y + inside - through))
            stores.append((twice, at_next, twice_in[at_next, :] - c_inner * e))
            for i, value in enumerate((b * e, (w + changed) * e, (2.0 * y + inside) * e - changed * through)):
                dots[t][i] = dots[t][i] + folded(value)
            packed_coef = packed_coef + spread(c, t, tracers, pair, level)
            packed_ring = packed_ring + spread(ring, t, tracers, pair, level)
            packed_e = packed_e + spread(e, t, tracers, pair, level)
            packed_inside = packed_inside + spread(inside, t, tracers, pair, level)
        row_change = jnp.where(row == first, packed_e, row_change)
        row_inside = jnp.where(row == first, packed_inside, row_inside)
        row_inside = jnp.where(row == next_row, -north[between : between + 1] * packed_e, row_inside)
        lat_coef.append(packed_coef)
        lat_ring.append(packed_ring)
        lat_change.append(-packed_e)
    for ref, at, value in stores:
        ref[at, :] = value

    even = is_even("lon")
    even_lane = (iota((rows, lanes), 1) & 1) == 0

    def neighbours(at):
        a, b = got_a[at, :], got_b[at, :]
        return jnp.where(even, a, b), jnp.where(even, b, a)

    parts = [pl.ds(i * rows, rows) for i in range(3)]
    own_image, own_field, own_east = [own[p, :] for p in parts]
    columns = neighbours(parts[0])
    got_image, got_field = from_neighbours(*columns, even_lane), jnp.where(even_lane, *columns)
    got_east = from_neighbours(*neighbours(parts[1]), even_lane)
    before = own_image + row_change
    y = packed[pl.ds(0, rows), :] + row_inside
    c = face(own_east, got_east, even_lane)
    f = c * (got_field - own_field)
    e = -f
    after = before + e
    ring = got_image + f
    through = c * (ring - after)
    through_new = through_old = halves = jnp.zeros((rows, lanes), F32)
    for side in range(SIDES):
        here = row == (rows - 1) * side
        through_new = jnp.where(here, lat_coef[side] * (lat_ring[side] - after), through_new)
        through_old = jnp.where(here, lat_coef[side] * (lat_ring[side] - before), through_old)
        halves = jnp.where(here, lat_coef[side] * lat_ring[side] * f + c * ring * lat_change[side], halves)
    flux_down = down * (pltpu.roll(e, lanes - 2 * tracers, 1) - e)
    flux_north = north * (pltpu.roll(e, rows - 1, 0) - e)
    inside = (pltpu.roll(flux_down, 2 * tracers, 1) - flux_down) + (pltpu.roll(flux_north, 1, 0) - flux_north) + inner * e
    beside = -inner * e
    corrections[parts[0], :] = e
    corrections[parts[1], :] = inside - through - (through_new - through_old)
    corrections[parts[2], :] = beside
    edges = [(rows - 1) * side for side in range(SIDES)]
    corrections[pl.ds(3 * rows, 8), :] = stacked(lat_coef + [c[i : i + 1] for i in edges])

    column_dots = [folded(value) for value in (
        own_field * e,
        (before + after) * e,
        (2.0 * y + inside) * e - after * (through + through_new) + before * through_old + halves,
    )]
    tile_lane, tile_row = iota((8, lanes), 1), iota((8, lanes), 0)
    total = jnp.zeros((8, lanes), F32)
    for t in range(tracers):
        mine = lax.rem(tile_lane >> 1, tracers) == t
        for i in range(4):
            value = sums[pl.ds((4 * t + i) * 8, 8), :]
            if i:
                value = value + dots[t][i - 1] + jnp.where(mine, column_dots[i - 1], 0.0)
            total = jnp.where(tile_row == 4 * t + i, jnp.sum(value, axis=0, keepdims=True), total)
    total = jnp.sum(total, axis=1, keepdims=True)
    total = jnp.sum(jnp.where(tile_row == tile_lane, total, 0.0), axis=0, keepdims=True)
    even_row = (iota((1, lanes), 1) & 1) == 0
    south, north_ = edges
    shares = [total, 2.0 * lat_coef[1] * f[north_ : north_ + 1], f[south : south + 1]]
    shares += [jnp.where(even_row, 2.0 * c[i : i + 1] * part, part) for i, part in zip(edges, lat_change)]
    for i, share in enumerate(shares):
        result[pl.ds(i, devices, SHARES), :] = jnp.broadcast_to(share, (devices, lanes))


def finish_kernel(tracers, nz, rows, devices, field, image, twice, corrections, sums, solution_out, residual_out,
                  solution, residual, sems):
    lanes = field.shape[1]
    across, along = lax.axis_size("lon"), lax.axis_size("lat")
    one = iota((1, lanes), 1)
    even_one = (one & 1) == 0
    total, to_north, to_south, lon_south, lon_north = [sums[pl.ds(i, devices, SHARES), :] for i in range(SHARES)]
    total = jnp.sum(total, axis=0, keepdims=True)
    device, lane_of = iota((devices, lanes), 0), iota((devices, lanes), 1)
    cross = jnp.where(lax.rem(device, along) < along - 1, to_north * pltpu.roll(to_south, devices - 1, 0), 0.0)
    for part in (lon_south, lon_north):
        beyond = pltpu.roll(pltpu.roll(part, devices - along, 0), lanes - 1, 1)
        cross = cross + jnp.where((lane_of & 1) == 0, part * beyond, 0.0)
    cross = jnp.sum(cross, axis=0, keepdims=True)

    lon, lat = lax.axis_index("lon"), lax.axis_index("lat")
    share = lambda i, j, at: sums[pl.ds(SHARES * (i * along + j) + at, 1), :]
    faces = corrections[pl.ds(3 * rows, 8), :]
    lat_sides = (share(lon, jnp.maximum(lat - 1, 0), 1) * jnp.where(lat > 0, 0.5, 0.0),
                 share(lon, jnp.minimum(lat + 1, along - 1), 2) * faces[1:2])
    sides = []
    for side in range(SIDES):
        east = share(lax.rem(lon + 1, across), lat, 3 + side)
        west = share(lax.rem(lon + across - 1, across), lat, 3 + side)
        part = from_neighbours(east, 0.5 * west, even_one)
        sides.append(lat_sides[side] + jnp.where(even_one, faces[2 + side : 3 + side] * part, part))
    row = iota((rows, lanes), 0)
    e, change, beside = [corrections[pl.ds(i * rows, rows), :] for i in range(3)]
    change = change + jnp.where(row == 0, sides[0], jnp.where(row == rows - 1, sides[1], 0.0))

    lane = iota((CHUNK, rows, lanes), 2)
    narrow = iota((rows, lanes), 1)
    edge = (lane == 0) | (lane == lanes - 1)
    near = (lane <= 1) | (lane >= lanes - 2)

    def number(i):
        return jnp.sum(jnp.where(one == i, total, 0.0), axis=1, keepdims=True)

    copies = []
    for t in range(tracers):
        bb, bw, ww, wy = [number(4 * t + i) for i in range(4)]
        mine = lax.rem(one >> 1, tracers) == t
        wy = wy - jnp.sum(jnp.where(mine, cross, 0.0), axis=1, keepdims=True)
        whole = bb + bw
        step = bb / whole
        rest = bw / whole
        new = rest * rest * bb - 2.0 * rest * step * bw + step * step * ww
        beta = new / bb
        tau = beta + rest
        step_next = new / (new + beta * beta * bb + tau * tau * bw - 2.0 * tau * step * ww + step * step * wy)
        both = step * step_next
        s_b = step + step_next * tau
        r_b = rest - step_next * tau
        r_w = both - step - step_next * tau
        s_edge = -both * e
        r_edge = jnp.where(lax.rem(narrow >> 1, tracers) == t, r_w * e + both * change,
                           both * jnp.where((narrow & 1) == 0, pltpu.roll(beside, 1, 1), pltpu.roll(beside, lanes - 1, 1)))
        for k in range(0, nz, CHUNK):
            slot, first = t * nz + k, k * tracers + t
            v, w, y = [levels_of(ref, slot, CHUNK, rows) for ref in (field, image, twice)]
            more = jnp.where(edge, unpacked(s_edge, first, tracers, CHUNK), 0.0)
            much = jnp.where(near, unpacked(r_edge, first, tracers, CHUNK), 0.0)
            put_levels(solution, slot, (s_b * v - both * w) + more)
            put_levels(residual, slot, (r_b * v + r_w * w + both * y) + much)
            at = pl.ds(slot * rows, CHUNK * rows)
            for a, b in ((solution, solution_out), (residual, residual_out)):
                copy = pltpu.make_async_copy(a.at[at], b.at[at], sems.at[len(copies)])
                copy.start()
                copies.append(copy)
    for copy in copies:
        copy.wait()


def swaps(devices, second, periodic):
    pairs = []
    for i in range(devices):
        j = i + 1 if (i % 2 == 0) != second else i - 1
        if periodic or 0 <= j < devices:
            pairs.append((i, j % devices))
    return pairs


def swapped(x, axis, second, periodic):
    return lax.ppermute(x, axis, swaps(lax.axis_size(axis), second, periodic))


def body(right_side, sea_mask, levels, east_diffusivity, north_diffusivity, vertical_diffusivity):
    tracers, nz, rows, lanes = right_side.shape
    devices = lax.axis_size("lon") * lax.axis_size("lat")
    flat = lambda x: x.reshape(-1, lanes)
    outside = lambda x: pltpu.with_memory_space_constraint(flat(x), pltpu.HBM)
    n = nz * rows
    cells = tracers * n * lanes

    def call(kernel, outs, flops, space=pltpu.VMEM, **more):
        cost = pl.CostEstimate(flops=flops, bytes_accessed=4 * lanes * sum(outs), transcendentals=0)
        return pl.pallas_call(
            functools.partial(kernel, tracers, nz, rows),
            out_shape=[space((m, lanes), F32) for m in outs],
            compiler_params=pltpu.CompilerParams(vmem_limit_bytes=32 * 1024 * 1024),
            cost_estimate=cost,
            **more,
        )

    def with_devices(kernel):
        return lambda tracers, nz, rows, *refs: kernel(tracers, nz, rows, devices, *refs)

    scratch = lambda m, dtype: pltpu.VMEM((m, lanes), dtype)
    field, coef_east, coef_west, coef_north, coef_south, coef_down, east_own, north_own, image, own, message = call(
        prepare_kernel,
        [tracers * n] + [n] * 7 + [tracers * n, 3 * rows, 2 * rows],
        60 * cells,
        in_specs=[pl.BlockSpec(memory_space=pltpu.HBM)] * 6,
        scratch_shapes=[scratch(n, jnp.int32), scratch(rows, jnp.int32)] + [scratch(n, jnp.bfloat16)] * 3
        + [pltpu.SemaphoreType.DMA((9 + 2 * tracers,))],
        name="prepare",
    )(*map(outside, (right_side, sea_mask, levels, east_diffusivity, north_diffusivity, vertical_diffusivity)))
    got_b = swapped(message, "lon", True, True)
    rows_b, = call(edges_kernel, [FIELDS * nz], cells, name="edges")(field, image, east_own, north_own)
    got_rows_b = swapped(rows_b, "lat", True, False)
    coefs = (coef_east, coef_west, coef_north, coef_south, coef_down)
    rows_a, message_a = call(later_kernel, [FIELDS * nz, 2 * rows], cells, name="later")(
        field, image, east_own, north_own, own, rows_b)
    twice, packed, sums = call(
        interior_kernel, [tracers * n, 4 * rows, 8 * 4 * tracers], 60000 * cells, name="interior"
    )(field, image, *coefs)
    got_a = swapped(message_a, "lon", False, True)
    got_rows_a = swapped(rows_a, "lat", False, False)
    image, twice, corrections, sums = call(
        with_devices(sums_kernel), [tracers * n, tracers * n, 3 * rows + 8, SHARES * devices], cells,
        input_output_aliases={0: 0, 1: 1}, name="sums",
    )(image, twice, coef_east, coef_north, coef_down, rows_a, rows_b, got_rows_a, got_rows_b, own, got_a, got_b, packed, sums)
    sums = lax.all_to_all(sums.reshape(devices, 1, -1), ("lon", "lat"), 0, 0, tiled=True).reshape(-1, lanes)
    copies = 2 * tracers * nz // CHUNK
    solution_field, residual = call(
        with_devices(finish_kernel), [tracers * n] * 2, 20 * cells, space=jax.ShapeDtypeStruct,
        out_specs=[pl.BlockSpec(memory_space=pltpu.HBM)] * 2,
        scratch_shapes=[scratch(tracers * n, F32)] * 2 + [pltpu.SemaphoreType.DMA((copies,))],
        name="finish",
    )(field, image, twice, corrections, sums)
    return solution_field.reshape(right_side.shape), residual.reshape(right_side.shape)


def solution(mesh):
    return jax.shard_map(
        body,
        mesh=mesh,
        in_specs=(
            P(None, None, "lat", "lon"),
            P(None, "lat", "lon"),
            P("lat", "lon"),
            P(None, "lat", "lon"),
            P(None, "lat", "lon"),
            P(None, "lat", "lon"),
        ),
        out_specs=(P(None, None, "lat", "lon"), P(None, None, "lat", "lon")),
        check_vma=False,
    )
```

```python
import functools

import jax
import jax.numpy as jnp
from jax import lax
from jax.experimental import pallas as pl
from jax.experimental.pallas import tpu as pltpu
from jax.sharding import PartitionSpec as P

F32 = jnp.float32
CHUNK = 8
SHARES = 4
SIDES = 2
FIELDS = 5


def iota(shape, axis):
    return lax.broadcasted_iota(jnp.int32, shape, axis)


def is_even(axis):
    return (lax.axis_index(axis) & 1) == 0


def levels_of(ref, first, count, rows):
    return ref[pl.ds(first * rows, count * rows), :].reshape(count, rows, ref.shape[1])


def put_levels(ref, first, value):
    count, rows, lanes = value.shape
    ref[pl.ds(first * rows, count * rows), :] = value.reshape(count * rows, lanes)


def laplacian(value, below, flux_above, coefs):
    _, rows, lanes = value.shape
    east, west, north, south, down = coefs
    change = east * (value - pltpu.roll(value, lanes - 1, 2)) + west * (value - pltpu.roll(value, 1, 2))
    change = change + (north * (value - pltpu.roll(value, rows - 1, 1)) + south * (value - pltpu.roll(value, 1, 1)))
    flux_down = down * (jnp.concatenate([value[1:], below], axis=0) - value)
    from_above = jnp.concatenate([flux_above, flux_down[:-1]], axis=0)
    return change + (from_above - flux_down), flux_down[-1:]


def packed_into(total, planes, first, step, pair):
    slots = [first + step * i for i in range(planes.shape[0])]
    moved = [pltpu.roll(planes[i], 2 * slot + 1, 1) for i, slot in enumerate(slots)]
    for slot, plane in zip(slots, moved):
        total = jnp.where(pair == slot, plane, total)
    return total


def unpacked(packed, first, step, count, offset=1):
    lanes = packed.shape[1]
    return jnp.stack([pltpu.roll(packed, (2 * lanes - offset - 2 * (first + step * i)) % lanes, 1) for i in range(count)])


def spread(plane, t, tracers, pair, level):
    moved = pltpu.roll(plane, 2 * t + 1, 1, stride=2 * tracers, stride_axis=0)
    return jnp.sum(jnp.where(pair == level * tracers + t, moved, 0.0), axis=0, keepdims=True)


def from_neighbours(east, west, even_lane):
    return jnp.where(even_lane, pltpu.roll(east, east.shape[1] - 1, 1), pltpu.roll(west, 1, 1))


def face(own, other, even_lane):
    return jnp.where(even_lane, own * (other > 0).astype(F32), other * (own > 0).astype(F32))


def prepare_kernel(tracers, nz, rows, field_in, mask_in, levels_in, east_in, north_in, down_in,
                   field, coef_east, coef_west, coef_north, coef_south, coef_down, east_own, north_own, image, own, message,
                   mask, levels, east, north, down, sems):
    first = nz // 4
    chunks = [(0, first), (first, (nz - first) // 2), (first + (nz - first) // 2, nz - first - (nz - first) // 2)]
    half = first + 1
    pairs = [(mask_in, mask, 0), (east_in, east, 0), (north_in, north, 0), (down_in, down, 0)]
    pairs += [(field_in, field, t * nz) for t in range(tracers)]
    copies = [[(levels_in, levels)], []]
    for part, (start, count) in enumerate(((0, half), (half, nz - half))):
        for a, b, offset in pairs:
            at = pl.ds((offset + start) * rows, count * rows)
            copies[part].append((a.at[at], b.at[at]))
    count = len(copies[0])
    copies = [[pltpu.make_async_copy(a, b, sems.at[i + part * count]) for i, (a, b) in enumerate(copies[part])] for part in range(2)]
    for copy in copies[0] + copies[1]:
        copy.start()
    for copy in copies[0]:
        copy.wait()
    lanes = field.shape[1]
    shape = (1, rows, lanes)
    last_lane, last_row = iota(shape, 2) == lanes - 1, iota(shape, 1) == rows - 1
    first_lane, first_row = iota(shape, 2) == 0, iota(shape, 1) == 0
    pair = iota((rows, lanes), 1) >> 1
    zero = jnp.zeros((rows, lanes), F32)
    packed_image, packed_field, packed_east = zero, zero, zero
    depth = levels[...]
    above = [zero[None]] * tracers
    for k, chunk in chunks:
        if k == first:
            for copy in copies[1]:
                copy.wait()
        level = iota((chunk + 1, rows, lanes), 0)
        count = min(chunk + 1, nz - k)
        wet = (levels_of(mask, k, count, rows) == 1) & (level[:count] + k < depth[None])
        wet = jnp.where(wet, 1.0, 0.0)
        if count == chunk:
            wet = jnp.concatenate([wet, zero[None]], axis=0)
        ocean = wet[:chunk]
        own_east = levels_of(east, k, chunk, rows).astype(F32) * ocean
        own_north = levels_of(north, k, chunk, rows).astype(F32) * ocean
        c_east = jnp.where(last_lane, 0.0, own_east * pltpu.roll(ocean, lanes - 1, 2))
        c_north = jnp.where(last_row, 0.0, own_north * pltpu.roll(ocean, rows - 1, 1))
        c_down = levels_of(down, k, chunk, rows).astype(F32) * ocean * wet[1:]
        c_west = jnp.where(first_lane, 0.0, pltpu.roll(own_east, 1, 2) * ocean)
        c_south = jnp.where(first_row, 0.0, pltpu.roll(own_north, 1, 1) * ocean)
        c = (c_east, c_west, c_north, c_south, c_down)
        packed_east = packed_into(packed_east, own_east, k * tracers, tracers, pair)
        changes = []
        for t in range(tracers):
            value = levels_of(field, t * nz + k, chunk, rows)
            below = levels_of(field, t * nz + k + chunk, 1, rows) if k + chunk < nz else zero[None]
            change, above[t] = laplacian(value, below, above[t], c)
            changes.append(change)
            packed_field = packed_into(packed_field, value, k * tracers + t, tracers, pair)
        for t in range(tracers):
            packed_image = packed_into(packed_image, changes[t], k * tracers + t, tracers, pair)
        for ref, value in zip((coef_east, coef_west, coef_north, coef_south, coef_down, east_own, north_own), c + (own_east, own_north)):
            put_levels(ref, k, value)
        for t in range(tracers):
            put_levels(image, t * nz + k, changes[t])
    own[pl.ds(0, rows), :] = packed_image
    own[pl.ds(rows, rows), :] = packed_field
    own[pl.ds(2 * rows, rows), :] = for_tracers(packed_east, tracers)
    put_message(rows, own, message, True)


def put_message(rows, own, message, second):
    lanes = own.shape[1]
    eastern = is_even("lon") != second
    even_lane = (iota((rows, lanes), 1) & 1) == 0
    image, field = own[pl.ds(0, rows), :], own[pl.ds(rows, rows), :]
    to_east = jnp.where(even_lane, image, pltpu.roll(field, 1, 1))
    to_west = jnp.where(even_lane, pltpu.roll(field, lanes - 1, 1), image)
    message[pl.ds(0, rows), :] = jnp.where(eastern, to_east, to_west)
    message[pl.ds(rows, rows), :] = own[pl.ds(2 * rows, rows), :]


def edge_rows(tracers, nz, rows, field, image, east_own, north_own, second, out):
    southern = is_even("lat") if second else jnp.logical_not(is_even("lat"))

    def edge(side):
        first = (rows - 1) * side
        parts = [ref[pl.ds(first + t * nz * rows, nz, rows), :] for ref in (image, field) for t in range(tracers)]
        return parts + [(east_own, north_own)[side][pl.ds(first, nz, rows), :]]

    for at, (south, north_) in enumerate(zip(edge(0), edge(1))):
        out[pl.ds(at * nz, nz), :] = jnp.where(southern, south, north_)


def edges_kernel(tracers, nz, rows, field, image, east_own, north_own, rows_b):
    edge_rows(tracers, nz, rows, field, image, east_own, north_own, True, rows_b)


def later_kernel(tracers, nz, rows, field, image, east_own, north_own, own, rows_b, rows_a, message_a):
    edge_rows(tracers, nz, rows, field, image, east_own, north_own, False, rows_a)
    put_message(rows, own, message_a, False)


def for_tracers(packed, tracers):
    return sum((pltpu.roll(packed, 2 * t, 1) for t in range(1, tracers)), packed)


def stacked(parts):
    lanes = parts[0].shape[1]
    row = iota((8, lanes), 0)
    total = jnp.zeros((8, lanes), F32)
    for i, part in enumerate(parts):
        total = jnp.where(row == i, part, total)
    return total


def folded(x):
    return sum(x[i : i + 8] for i in range(0, x.shape[0], 8))


def interior_kernel(tracers, nz, rows, field, image, coef_east, coef_west, coef_north, coef_south, coef_down,
                    twice, packed, sums):
    lanes = field.shape[1]
    pair, last_lane = iota((rows, lanes), 1) >> 1, iota((CHUNK, rows, lanes), 2) == lanes - 1
    zero = jnp.zeros((rows, lanes), F32)
    packed_twice, packed_north, packed_down, packed_inner = [zero] * 4
    totals = [[zero] * 4 for _ in range(tracers)]
    above = [zero[None]] * tracers
    for k in range(0, nz, CHUNK):
        refs = (coef_east, coef_west, coef_north, coef_south, coef_down)
        c = [levels_of(ref, k, CHUNK, rows) for ref in refs]
        results = []
        for t in range(tracers):
            w = levels_of(image, t * nz + k, CHUNK, rows)
            below = levels_of(image, t * nz + k + CHUNK, 1, rows) if k + CHUNK < nz else zero[None]
            y, above[t] = laplacian(w, below, above[t], c)
            results.append(y)
            v = levels_of(field, t * nz + k, CHUNK, rows)
            for i, product in enumerate((v * v, v * w, w * w, w * y)):
                totals[t][i] = totals[t][i] + jnp.sum(product, axis=0)
        inner = jnp.where(last_lane, c[1], c[0])
        packed_north = packed_into(packed_north, c[2], k * tracers, tracers, pair)
        packed_down = packed_into(packed_down, c[4], k * tracers, tracers, pair)
        packed_inner = packed_into(packed_inner, inner, k * tracers, tracers, pair)
        for t in range(tracers):
            packed_twice = packed_into(packed_twice, results[t], k * tracers + t, tracers, pair)
        for t in range(tracers):
            put_levels(twice, t * nz + k, results[t])
    packed[pl.ds(0, rows), :] = packed_twice
    for i, part in enumerate((packed_north, packed_down, packed_inner)):
        packed[pl.ds((i + 1) * rows, rows), :] = for_tracers(part, tracers)
    for t in range(tracers):
        for i in range(4):
            sums[pl.ds((4 * t + i) * 8, 8), :] = folded(totals[t][i])


def sums_kernel(tracers, nz, rows, devices, image_in, twice_in, coef_east, coef_north, coef_down, rows_a, rows_b, got_rows_a,
                got_rows_b, own, got_a, got_b, packed, sums, image, twice, corrections, result):
    lanes = own.shape[1]
    even = is_even("lat")
    pair, level = iota((nz, lanes), 1) >> 1, iota((nz, lanes), 0)
    row = iota((rows, lanes), 0)
    north, down, inner = [packed[pl.ds((i + 1) * rows, rows), :] for i in range(3)]
    dots = [[jnp.zeros((8, lanes), F32) for _ in range(3)] for _ in range(tracers)]
    nothing = jnp.zeros((1, lanes), F32)
    row_change, row_inside = jnp.zeros((rows, lanes), F32), jnp.zeros((rows, lanes), F32)
    lat_coef, lat_ring, lat_change = [], [], []
    stores = []
    for side in range(SIDES):
        def part(at, a, b):
            first, second = (b, a) if side == 0 else (a, b)
            return jnp.where(even, first[pl.ds(at * nz, nz), :], second[pl.ds(at * nz, nz), :])

        own_row = lambda at: part(at, rows_a, rows_b)
        got_row = lambda at: part(at, got_rows_a, got_rows_b)
        own_coef, got_coef = own_row(2 * tracers), got_row(2 * tracers)
        c = got_coef * (own_coef > 0).astype(F32) if side == 0 else own_coef * (got_coef > 0).astype(F32)
        c = c * jnp.where(lax.axis_index("lat") == (0, lax.axis_size("lat") - 1)[side], 0.0, 1.0)
        first, next_row, between = ((0, 1, 0), (rows - 1, rows - 2, rows - 2))[side]
        c_east, c_down = coef_east[pl.ds(first, nz, rows), :], coef_down[pl.ds(first, nz, rows), :]
        c_inner = coef_north[pl.ds(between, nz, rows), :]
        packed_coef, packed_ring, packed_e, packed_inside = [nothing] * 4
        for t in range(tracers):
            b, w = own_row(tracers + t), own_row(t)
            f = c * (got_row(tracers + t) - b)
            e = -f
            ring = got_row(t) + f
            flux_east = c_east * (pltpu.roll(e, lanes - 1, 1) - e)
            flux_down = c_down * (pltpu.roll(e, nz - 1, 0) - e)
            inside = (pltpu.roll(flux_east, 1, 1) - flux_east) + (pltpu.roll(flux_down, 1, 0) - flux_down) + c_inner * e
            changed = w + e
            through = c * (ring - changed)
            at = pl.ds(first + t * nz * rows, nz, rows)
            at_next = pl.ds(next_row + t * nz * rows, nz, rows)
            y = twice_in[at, :]
            stores.append((image, at, changed))
            stores.append((twice, at, y + inside - through))
            stores.append((twice, at_next, twice_in[at_next, :] - c_inner * e))
            for i, value in enumerate((b * e, (w + changed) * e, (2.0 * y + inside) * e - changed * through)):
                dots[t][i] = dots[t][i] + folded(value)
            packed_coef = packed_coef + spread(c, t, tracers, pair, level)
            packed_ring = packed_ring + spread(ring, t, tracers, pair, level)
            packed_e = packed_e + spread(e, t, tracers, pair, level)
            packed_inside = packed_inside + spread(inside, t, tracers, pair, level)
        row_change = jnp.where(row == first, packed_e, row_change)
        row_inside = jnp.where(row == first, packed_inside, row_inside)
        row_inside = jnp.where(row == next_row, -north[between : between + 1] * packed_e, row_inside)
        lat_coef.append(packed_coef)
        lat_ring.append(packed_ring)
        lat_change.append(-packed_e)
    for ref, at, value in stores:
        ref[at, :] = value

    even = is_even("lon")
    even_lane = (iota((rows, lanes), 1) & 1) == 0

    def neighbours(at):
        a, b = got_a[at, :], got_b[at, :]
        return jnp.where(even, a, b), jnp.where(even, b, a)

    parts = [pl.ds(i * rows, rows) for i in range(3)]
    own_image, own_field, own_east = [own[p, :] for p in parts]
    columns = neighbours(parts[0])
    got_image, got_field = from_neighbours(*columns, even_lane), jnp.where(even_lane, *columns)
    got_east = from_neighbours(*neighbours(parts[1]), even_lane)
    before = own_image + row_change
    y = packed[pl.ds(0, rows), :] + row_inside
    c = face(own_east, got_east, even_lane)
    f = c * (got_field - own_field)
    e = -f
    after = before + e
    ring = got_image + f
    through = c * (ring - after)
    through_new = through_old = halves = jnp.zeros((rows, lanes), F32)
    for side in range(SIDES):
        here = row == (rows - 1) * side
        through_new = jnp.where(here, lat_coef[side] * (lat_ring[side] - after), through_new)
        through_old = jnp.where(here, lat_coef[side] * (lat_ring[side] - before), through_old)
        halves = jnp.where(here, lat_coef[side] * lat_ring[side] * f + c * ring * lat_change[side], halves)
    flux_down = down * (pltpu.roll(e, lanes - 2 * tracers, 1) - e)
    flux_north = north * (pltpu.roll(e, rows - 1, 0) - e)
    inside = (pltpu.roll(flux_down, 2 * tracers, 1) - flux_down) + (pltpu.roll(flux_north, 1, 0) - flux_north) + inner * e
    beside = -inner * e
    corrections[parts[0], :] = e
    corrections[parts[1], :] = inside - through - (through_new - through_old)
    corrections[parts[2], :] = beside
    edges = [(rows - 1) * side for side in range(SIDES)]
    corrections[pl.ds(3 * rows, 8), :] = stacked(lat_coef + [c[i : i + 1] for i in edges])

    column_dots = [folded(value) for value in (
        own_field * e,
        (before + after) * e,
        (2.0 * y + inside) * e - after * (through + through_new) + before * through_old + halves,
    )]
    tile_lane, tile_row = iota((8, lanes), 1), iota((8, lanes), 0)
    total = jnp.zeros((8, lanes), F32)
    for t in range(tracers):
        mine = lax.rem(tile_lane >> 1, tracers) == t
        for i in range(4):
            value = sums[pl.ds((4 * t + i) * 8, 8), :]
            if i:
                value = value + dots[t][i - 1] + jnp.where(mine, column_dots[i - 1], 0.0)
            total = jnp.where(tile_row == 4 * t + i, jnp.sum(value, axis=0, keepdims=True), total)
    total = jnp.sum(total, axis=1, keepdims=True)
    total = jnp.sum(jnp.where(tile_row == tile_lane, total, 0.0), axis=0, keepdims=True)
    even_row = (iota((1, lanes), 1) & 1) == 0
    south, north_ = edges
    lon_shares = [2.0 * c[i : i + 1] * part for i, part in zip(edges, lat_change)]
    shares = [total, 2.0 * lat_coef[1] * f[north_ : north_ + 1], jnp.where(even_row, lon_shares[0], lat_change[0]),
              jnp.where(even_row, lon_shares[1], f[south : south + 1])]
    for i, share in enumerate(shares):
        result[pl.ds(i, devices, SHARES), :] = jnp.broadcast_to(share, (devices, lanes))


def finish_kernel(tracers, nz, rows, devices, field, image, twice, corrections, sums, solution_out, residual_out,
                  solution, residual, sems):
    lanes = field.shape[1]
    across, along = lax.axis_size("lon"), lax.axis_size("lat")
    one = iota((1, lanes), 1)
    even_one = (one & 1) == 0
    total, to_north, lon_south, mixed = [sums[pl.ds(i, devices, SHARES), :] for i in range(SHARES)]
    total = jnp.sum(total, axis=0, keepdims=True)
    even_lane = (iota((devices, lanes), 1) & 1) == 0
    from_east = lambda x: pltpu.roll(pltpu.roll(x, devices - along, 0), lanes - 1, 1)
    from_north = lambda x: pltpu.roll(x, devices - 1, 0)
    beyond = from_east(lon_south)
    cross = jnp.where(even_lane, lon_south * beyond - mixed * from_north(beyond), 0.0)
    cross = cross + to_north * from_north(jnp.where(even_lane, -from_east(mixed), mixed))
    cross = jnp.sum(cross, axis=0, keepdims=True)

    lon, lat = lax.axis_index("lon"), lax.axis_index("lat")
    share = lambda i, j, at: sums[pl.ds(SHARES * (i * along + j) + at, 1), :]
    faces = corrections[pl.ds(3 * rows, 8), :]
    east, west = lax.rem(lon + 1, across), lax.rem(lon + across - 1, across)
    south, north = jnp.maximum(lat - 1, 0), jnp.minimum(lat + 1, along - 1)
    northern = jnp.where(lat < along - 1, 1.0, 0.0)
    lat_sides = (share(lon, south, 1) * jnp.where(lat > 0, 0.5, 0.0),
                 faces[1:2] * jnp.where(even_one, -pltpu.roll(share(east, north, 3), lanes - 1, 1), share(lon, north, 3)))
    lon_sides = (from_neighbours(share(east, lat, 2), 0.5 * share(west, lat, 2), even_one),
                 from_neighbours(-northern * share(east, north, 2), 0.5 * share(west, lat, 3), even_one))
    sides = [lat_sides[i] + jnp.where(even_one, faces[2 + i : 3 + i] * lon_sides[i], lon_sides[i]) for i in range(SIDES)]
    row = iota((rows, lanes), 0)
    e, change, beside = [corrections[pl.ds(i * rows, rows), :] for i in range(3)]
    change = change + jnp.where(row == 0, sides[0], jnp.where(row == rows - 1, sides[1], 0.0))

    lane = iota((CHUNK, rows, lanes), 2)
    narrow = iota((rows, lanes), 1)
    edge = (lane == 0) | (lane == lanes - 1)
    near = (lane <= 1) | (lane >= lanes - 2)

    def number(i):
        return jnp.sum(jnp.where(one == i, total, 0.0), axis=1, keepdims=True)

    copies = []
    for t in range(tracers):
        bb, bw, ww, wy = [number(4 * t + i) for i in range(4)]
        mine = lax.rem(one >> 1, tracers) == t
        wy = wy - jnp.sum(jnp.where(mine, cross, 0.0), axis=1, keepdims=True)
        whole = 1.0 / (bb + bw)
        step = bb * whole
        rest = bw * whole
        beta = step * (ww * whole) - rest * rest
        new = beta * bb
        tau = beta + rest
        step_next = new / (new + beta * new + tau * tau * bw - 2.0 * tau * step * ww + step * step * wy)
        both = step * step_next
        s_b = step + step_next * tau
        r_b = rest - step_next * tau
        r_w = both - step - step_next * tau
        s_edge = -both * e
        r_edge = jnp.where(lax.rem(narrow >> 1, tracers) == t, r_w * e + both * change,
                           both * jnp.where((narrow & 1) == 0, pltpu.roll(beside, 1, 1), pltpu.roll(beside, lanes - 1, 1)))
        for k in range(0, nz, CHUNK):
            slot, first = t * nz + k, k * tracers + t
            v, w, y = [levels_of(ref, slot, CHUNK, rows) for ref in (field, image, twice)]
            more = jnp.where(edge, unpacked(s_edge, first, tracers, CHUNK), 0.0)
            much = jnp.where(near, unpacked(r_edge, first, tracers, CHUNK), 0.0)
            put_levels(solution, slot, (s_b * v - both * w) + more)
            put_levels(residual, slot, (r_b * v + r_w * w + both * y) + much)
            at = pl.ds(slot * rows, CHUNK * rows)
            for a, b in ((solution, solution_out), (residual, residual_out)):
                copy = pltpu.make_async_copy(a.at[at], b.at[at], sems.at[len(copies)])
                copy.start()
                copies.append(copy)
    for copy in copies:
        copy.wait()


def swapped(x, axis, second):
    devices = lax.axis_size(axis)
    forward = [(i % 2 == 0) != second for i in range(devices)]
    return lax.ppermute(x, axis, [(i, (i + 1 if forward[i] else i - 1) % devices) for i in range(devices)])


def body(right_side, sea_mask, levels, east_diffusivity, north_diffusivity, vertical_diffusivity):
    tracers, nz, rows, lanes = right_side.shape
    devices = lax.axis_size("lon") * lax.axis_size("lat")
    flat = lambda x: x.reshape(-1, lanes)
    outside = lambda x: pltpu.with_memory_space_constraint(flat(x), pltpu.HBM)
    n = nz * rows
    cells = tracers * n * lanes

    def call(kernel, outs, flops, space=pltpu.VMEM, **more):
        cost = pl.CostEstimate(flops=flops, bytes_accessed=4 * lanes * sum(outs), transcendentals=0)
        return pl.pallas_call(
            functools.partial(kernel, tracers, nz, rows),
            out_shape=[space((m, lanes), F32) for m in outs],
            compiler_params=pltpu.CompilerParams(vmem_limit_bytes=32 * 1024 * 1024),
            cost_estimate=cost,
            **more,
        )

    def with_devices(kernel):
        return lambda tracers, nz, rows, *refs: kernel(tracers, nz, rows, devices, *refs)

    scratch = lambda m, dtype: pltpu.VMEM((m, lanes), dtype)
    field, coef_east, coef_west, coef_north, coef_south, coef_down, east_own, north_own, image, own, message = call(
        prepare_kernel,
        [tracers * n] + [n] * 7 + [tracers * n, 3 * rows, 2 * rows],
        60 * cells,
        in_specs=[pl.BlockSpec(memory_space=pltpu.HBM)] * 6,
        scratch_shapes=[scratch(n, jnp.int32), scratch(rows, jnp.int32)] + [scratch(n, jnp.bfloat16)] * 3
        + [pltpu.SemaphoreType.DMA((9 + 2 * tracers,))],
        name="prepare",
    )(*map(outside, (right_side, sea_mask, levels, east_diffusivity, north_diffusivity, vertical_diffusivity)))
    got_b = swapped(message, "lon", True)
    rows_b, = call(edges_kernel, [FIELDS * nz], cells, name="edges")(field, image, east_own, north_own)
    got_rows_b = swapped(rows_b, "lat", True)
    coefs = (coef_east, coef_west, coef_north, coef_south, coef_down)
    rows_a, message_a = call(later_kernel, [FIELDS * nz, 2 * rows], cells, name="later")(
        field, image, east_own, north_own, own, rows_b)
    twice, packed, sums = call(
        interior_kernel, [tracers * n, 4 * rows, 8 * 4 * tracers], 60000 * cells, name="interior"
    )(field, image, *coefs)
    got_a = swapped(message_a, "lon", False)
    got_rows_a = swapped(rows_a, "lat", False)
    image, twice, corrections, sums = call(
        with_devices(sums_kernel), [tracers * n, tracers * n, 3 * rows + 8, SHARES * devices], cells,
        input_output_aliases={0: 0, 1: 1}, name="sums",
    )(image, twice, coef_east, coef_north, coef_down, rows_a, rows_b, got_rows_a, got_rows_b, own, got_a, got_b, packed, sums)
    sums = lax.all_to_all(sums.reshape(devices, 1, -1), ("lon", "lat"), 0, 0, tiled=True).reshape(-1, lanes)
    copies = 2 * tracers * nz // CHUNK
    solution_field, residual = call(
        with_devices(finish_kernel), [tracers * n] * 2, 20 * cells, space=jax.ShapeDtypeStruct,
        out_specs=[pl.BlockSpec(memory_space=pltpu.HBM)] * 2,
        scratch_shapes=[scratch(tracers * n, F32)] * 2 + [pltpu.SemaphoreType.DMA((copies,))],
        name="finish",
    )(field, image, twice, corrections, sums)
    return solution_field.reshape(right_side.shape), residual.reshape(right_side.shape)


def solution(mesh):
    return jax.shard_map(
        body,
        mesh=mesh,
        in_specs=(
            P(None, None, "lat", "lon"),
            P(None, "lat", "lon"),
            P("lat", "lon"),
            P(None, "lat", "lon"),
            P(None, "lat", "lon"),
            P(None, "lat", "lon"),
        ),
        out_specs=(P(None, None, "lat", "lon"), P(None, None, "lat", "lon")),
        check_vma=False,
    )
```

```python
import functools

import jax
import jax.numpy as jnp
from jax import lax
from jax.experimental import pallas as pl
from jax.experimental.pallas import tpu as pltpu
from jax.sharding import PartitionSpec as P

F32 = jnp.float32
CHUNK = 8
SHARES = 4
SIDES = 2
FIELDS = 5


def iota(shape, axis):
    return lax.broadcasted_iota(jnp.int32, shape, axis)


def is_even(axis):
    return (lax.axis_index(axis) & 1) == 0


def levels_of(ref, first, count, rows):
    return ref[pl.ds(first * rows, count * rows), :].reshape(count, rows, ref.shape[1])


def put_levels(ref, first, value):
    count, rows, lanes = value.shape
    ref[pl.ds(first * rows, count * rows), :] = value.reshape(count * rows, lanes)


def laplacian(value, below, flux_above, coefs):
    _, rows, lanes = value.shape
    east, west, north, south, down = coefs
    change = east * (value - pltpu.roll(value, lanes - 1, 2)) + west * (value - pltpu.roll(value, 1, 2))
    change = change + (north * (value - pltpu.roll(value, rows - 1, 1)) + south * (value - pltpu.roll(value, 1, 1)))
    flux_down = down * (jnp.concatenate([value[1:], below], axis=0) - value)
    from_above = jnp.concatenate([flux_above, flux_down[:-1]], axis=0)
    return change + (from_above - flux_down), flux_down[-1:]


def packed_into(total, planes, first, step, pair):
    slots = [first + step * i for i in range(planes.shape[0])]
    moved = [pltpu.roll(planes[i], 2 * slot + 1, 1) for i, slot in enumerate(slots)]
    for slot, plane in zip(slots, moved):
        total = jnp.where(pair == slot, plane, total)
    return total


def unpacked(packed, first, step, count, offset=1):
    lanes = packed.shape[1]
    return jnp.stack([pltpu.roll(packed, (2 * lanes - offset - 2 * (first + step * i)) % lanes, 1) for i in range(count)])


def spread(plane, t, tracers, pair, level):
    moved = pltpu.roll(plane, 2 * t + 1, 1, stride=2 * tracers, stride_axis=0)
    return jnp.sum(jnp.where(pair == level * tracers + t, moved, 0.0), axis=0, keepdims=True)


def fours_into(total, planes, first, four):
    moved = [pltpu.roll(planes[i], 4 * (first + i) + 2, 1) for i in range(planes.shape[0])]
    for i, plane in enumerate(moved):
        total = jnp.where(four == first + i, plane, total)
    return total


def pairs_of(fours, lane):
    lanes = lane.shape[1]
    return jnp.where((lane & 2) == 0, pltpu.roll(fours[0], lanes - 1, 1), pltpu.roll(fours[1], 1, 1))


def from_neighbours(east, west, even_lane):
    return jnp.where(even_lane, pltpu.roll(east, east.shape[1] - 1, 1), pltpu.roll(west, 1, 1))


def face(own, other, even_lane):
    return jnp.where(even_lane, own * (other > 0).astype(F32), other * (own > 0).astype(F32))


def columns_kernel(tracers, nz, rows, field_in, mask_in, levels_in, east_in, north_in, down_in,
                   field, mask, levels, east, north, down, own, message, packed, sems):
    pairs = ((levels_in, levels), (mask_in, mask), (field_in, field), (east_in, east), (north_in, north), (down_in, down))
    copies = [pltpu.make_async_copy(a, b, sems.at[i]) for i, (a, b) in enumerate(pairs)]
    for copy in copies:
        copy.start()
    lanes = field.shape[1]
    lane, row = iota((rows, lanes), 1), iota((rows, lanes), 0)
    four, place = lane >> 2, lane & 3
    zero = jnp.zeros((rows, lanes), F32)
    chunk = nz // 2

    def fours_of(ref, start=0, see=lambda value, k: value.astype(F32)):
        total = zero
        for k in range(0, nz, chunk):
            total = fours_into(total, see(levels_of(ref, start + k, chunk, rows), k), k, four)
        return total

    for copy in copies[:3]:
        copy.wait()
    depth = levels[...]
    level = iota((chunk, rows, lanes), 0)
    wet = fours_of(mask, see=lambda value, k: jnp.where((value == 1) & (level + k < depth[None]), 1.0, 0.0))
    fields = [fours_of(field, t * nz) for t in range(tracers)]
    for copy in copies[3:]:
        copy.wait()
    wide_east, wide_north, wide_down = fours_of(east), fours_of(north), fours_of(down)
    own_east = wide_east * wet
    inner = own_east * pltpu.roll(wet, lanes - 1, 1)
    inner = jnp.where(place == 1, pltpu.roll(inner, 1, 1), inner)
    c_north = jnp.where(row == rows - 1, 0.0, wide_north * wet * pltpu.roll(wet, rows - 1, 0))
    c_south = pltpu.roll(c_north, 1, 0)
    c_down = jnp.where(four == nz - 1, 0.0, wide_down * wet * pltpu.roll(wet, lanes - 4, 1))
    images = []
    for v in fields:
        beside = jnp.where(place == 1, pltpu.roll(v, 1, 1), pltpu.roll(v, lanes - 1, 1))
        flux_down = c_down * (pltpu.roll(v, lanes - 4, 1) - v)
        change = inner * (v - beside) + c_north * (v - pltpu.roll(v, rows - 1, 0)) + c_south * (v - pltpu.roll(v, 1, 0))
        images.append(change + (pltpu.roll(flux_down, 4, 1) - flux_down))
    for i, parts in enumerate((images, fields, (own_east, own_east))):
        own[pl.ds(i * rows, rows), :] = pairs_of(parts, lane)
    put_message(rows, own, message, True)
    for i, part in enumerate((c_north, c_down, inner)):
        packed[pl.ds(i * rows, rows), :] = pairs_of((part, part), lane)


def block_kernel(tracers, nz, rows, field, mask, levels, east, north, down,
                 coef_east, coef_west, coef_north, coef_south, coef_down, east_own, north_own, image, rows_b):
    lanes = field.shape[1]
    chunk = nz // 2
    shape = (1, rows, lanes)
    last_lane, last_row = iota(shape, 2) == lanes - 1, iota(shape, 1) == rows - 1
    first_lane, first_row = iota(shape, 2) == 0, iota(shape, 1) == 0
    zero = jnp.zeros((rows, lanes), F32)
    depth = levels[...]
    level = iota((chunk + 1, rows, lanes), 0)
    above = [zero[None]] * tracers
    for k in range(0, nz, chunk):
        count = min(chunk + 1, nz - k)
        wet = (levels_of(mask, k, count, rows) == 1) & (level[:count] + k < depth[None])
        wet = jnp.where(wet, 1.0, 0.0)
        if count == chunk:
            wet = jnp.concatenate([wet, zero[None]], axis=0)
        ocean = wet[:chunk]
        own_east = levels_of(east, k, chunk, rows).astype(F32) * ocean
        own_north = levels_of(north, k, chunk, rows).astype(F32) * ocean
        c_east = jnp.where(last_lane, 0.0, own_east * pltpu.roll(ocean, lanes - 1, 2))
        c_north = jnp.where(last_row, 0.0, own_north * pltpu.roll(ocean, rows - 1, 1))
        c_down = levels_of(down, k, chunk, rows).astype(F32) * ocean * wet[1:]
        c_west = jnp.where(first_lane, 0.0, pltpu.roll(own_east, 1, 2) * ocean)
        c_south = jnp.where(first_row, 0.0, pltpu.roll(own_north, 1, 1) * ocean)
        c = (c_east, c_west, c_north, c_south, c_down)
        changes = []
        for t in range(tracers):
            value = levels_of(field, t * nz + k, chunk, rows)
            below = levels_of(field, t * nz + k + chunk, 1, rows) if k + chunk < nz else zero[None]
            change, above[t] = laplacian(value, below, above[t], c)
            changes.append(change)
        for ref, value in zip((coef_east, coef_west, coef_north, coef_south, coef_down, east_own, north_own), c + (own_east, own_north)):
            put_levels(ref, k, value)
        for t in range(tracers):
            put_levels(image, t * nz + k, changes[t])
    edge_rows(tracers, nz, rows, field, image, east_own, north_own, True, rows_b)


def put_message(rows, own, message, second):
    lanes = own.shape[1]
    eastern = is_even("lon") != second
    even_lane = (iota((rows, lanes), 1) & 1) == 0
    image, field = own[pl.ds(0, rows), :], own[pl.ds(rows, rows), :]
    to_east = jnp.where(even_lane, image, pltpu.roll(field, 1, 1))
    to_west = jnp.where(even_lane, pltpu.roll(field, lanes - 1, 1), image)
    message[pl.ds(0, rows), :] = jnp.where(eastern, to_east, to_west)
    message[pl.ds(rows, rows), :] = own[pl.ds(2 * rows, rows), :]


def edge_rows(tracers, nz, rows, field, image, east_own, north_own, second, out):
    southern = is_even("lat") if second else jnp.logical_not(is_even("lat"))

    def edge(side):
        first = (rows - 1) * side
        parts = [ref[pl.ds(first + t * nz * rows, nz, rows), :] for ref in (image, field) for t in range(tracers)]
        return parts + [(east_own, north_own)[side][pl.ds(first, nz, rows), :]]

    for at, (south, north_) in enumerate(zip(edge(0), edge(1))):
        out[pl.ds(at * nz, nz), :] = jnp.where(southern, south, north_)


def later_kernel(tracers, nz, rows, field, image, east_own, north_own, own, rows_b, rows_a, message_a):
    edge_rows(tracers, nz, rows, field, image, east_own, north_own, False, rows_a)
    put_message(rows, own, message_a, False)


def stacked(parts):
    lanes = parts[0].shape[1]
    row = iota((8, lanes), 0)
    total = jnp.zeros((8, lanes), F32)
    for i, part in enumerate(parts):
        total = jnp.where(row == i, part, total)
    return total


def folded(x):
    return sum(x[i : i + 8] for i in range(0, x.shape[0], 8))


def interior_kernel(tracers, nz, rows, field, image, coef_east, coef_west, coef_north, coef_south, coef_down,
                    twice, packed, sums):
    lanes = field.shape[1]
    pair = iota((rows, lanes), 1) >> 1
    zero = packed_twice = jnp.zeros((rows, lanes), F32)
    totals = [[zero] * 4 for _ in range(tracers)]
    above = [zero[None]] * tracers
    for k in range(0, nz, CHUNK):
        refs = (coef_east, coef_west, coef_north, coef_south, coef_down)
        c = [levels_of(ref, k, CHUNK, rows) for ref in refs]
        results = []
        for t in range(tracers):
            w = levels_of(image, t * nz + k, CHUNK, rows)
            below = levels_of(image, t * nz + k + CHUNK, 1, rows) if k + CHUNK < nz else zero[None]
            y, above[t] = laplacian(w, below, above[t], c)
            results.append(y)
            v = levels_of(field, t * nz + k, CHUNK, rows)
            for i, product in enumerate((v * v, v * w, w * w, w * y)):
                totals[t][i] = totals[t][i] + jnp.sum(product, axis=0)
        for t in range(tracers):
            packed_twice = packed_into(packed_twice, results[t], k * tracers + t, tracers, pair)
        for t in range(tracers):
            put_levels(twice, t * nz + k, results[t])
    packed[...] = packed_twice
    for t in range(tracers):
        for i in range(4):
            sums[pl.ds((4 * t + i) * 8, 8), :] = folded(totals[t][i])


def sums_kernel(tracers, nz, rows, devices, image_in, twice_in, coef_east, coef_north, coef_down, rows_a, rows_b, got_rows_a,
                got_rows_b, own, got_a, got_b, packed, packed_twice, sums, image, twice, corrections, result):
    lanes = own.shape[1]
    even = is_even("lat")
    pair, level = iota((nz, lanes), 1) >> 1, iota((nz, lanes), 0)
    row = iota((rows, lanes), 0)
    north, down, inner = [packed[pl.ds(i * rows, rows), :] for i in range(3)]
    dots = [[jnp.zeros((8, lanes), F32) for _ in range(3)] for _ in range(tracers)]
    nothing = jnp.zeros((1, lanes), F32)
    row_change, row_inside = jnp.zeros((rows, lanes), F32), jnp.zeros((rows, lanes), F32)
    lat_coef, lat_ring, lat_change = [], [], []
    stores = []
    for side in range(SIDES):
        def part(at, a, b):
            first, second = (b, a) if side == 0 else (a, b)
            return jnp.where(even, first[pl.ds(at * nz, nz), :], second[pl.ds(at * nz, nz), :])

        own_row = lambda at: part(at, rows_a, rows_b)
        got_row = lambda at: part(at, got_rows_a, got_rows_b)
        own_coef, got_coef = own_row(2 * tracers), got_row(2 * tracers)
        c = got_coef * (own_coef > 0).astype(F32) if side == 0 else own_coef * (got_coef > 0).astype(F32)
        c = c * jnp.where(lax.axis_index("lat") == (0, lax.axis_size("lat") - 1)[side], 0.0, 1.0)
        first, next_row, between = ((0, 1, 0), (rows - 1, rows - 2, rows - 2))[side]
        c_east, c_down = coef_east[pl.ds(first, nz, rows), :], coef_down[pl.ds(first, nz, rows), :]
        c_inner = coef_north[pl.ds(between, nz, rows), :]
        packed_coef, packed_ring, packed_e, packed_inside = [nothing] * 4
        for t in range(tracers):
            b, w = own_row(tracers + t), own_row(t)
            f = c * (got_row(tracers + t) - b)
            e = -f
            ring = got_row(t) + f
            flux_east = c_east * (pltpu.roll(e, lanes - 1, 1) - e)
            flux_down = c_down * (pltpu.roll(e, nz - 1, 0) - e)
            inside = (pltpu.roll(flux_east, 1, 1) - flux_east) + (pltpu.roll(flux_down, 1, 0) - flux_down) + c_inner * e
            changed = w + e
            through = c * (ring - changed)
            at = pl.ds(first + t * nz * rows, nz, rows)
            at_next = pl.ds(next_row + t * nz * rows, nz, rows)
            y = twice_in[at, :]
            stores.append((image, at, changed))
            stores.append((twice, at, y + inside - through))
            stores.append((twice, at_next, twice_in[at_next, :] - c_inner * e))
            for i, value in enumerate((b * e, (w + changed) * e, (2.0 * y + inside) * e - changed * through)):
                dots[t][i] = dots[t][i] + folded(value)
            packed_coef = packed_coef + spread(c, t, tracers, pair, level)
            packed_ring = packed_ring + spread(ring, t, tracers, pair, level)
            packed_e = packed_e + spread(e, t, tracers, pair, level)
            packed_inside = packed_inside + spread(inside, t, tracers, pair, level)
        row_change = jnp.where(row == first, packed_e, row_change)
        row_inside = jnp.where(row == first, packed_inside, row_inside)
        row_inside = jnp.where(row == next_row, -north[between : between + 1] * packed_e, row_inside)
        lat_coef.append(packed_coef)
        lat_ring.append(packed_ring)
        lat_change.append(-packed_e)
    for ref, at, value in stores:
        ref[at, :] = value

    even = is_even("lon")
    even_lane = (iota((rows, lanes), 1) & 1) == 0

    def neighbours(at):
        a, b = got_a[at, :], got_b[at, :]
        return jnp.where(even, a, b), jnp.where(even, b, a)

    parts = [pl.ds(i * rows, rows) for i in range(3)]
    own_image, own_field, own_east = [own[p, :] for p in parts]
    columns = neighbours(parts[0])
    got_image, got_field = from_neighbours(*columns, even_lane), jnp.where(even_lane, *columns)
    got_east = from_neighbours(*neighbours(parts[1]), even_lane)
    before = own_image + row_change
    y = packed_twice[...] + row_inside
    c = face(own_east, got_east, even_lane)
    f = c * (got_field - own_field)
    e = -f
    after = before + e
    ring = got_image + f
    through = c * (ring - after)
    through_new = through_old = halves = jnp.zeros((rows, lanes), F32)
    for side in range(SIDES):
        here = row == (rows - 1) * side
        through_new = jnp.where(here, lat_coef[side] * (lat_ring[side] - after), through_new)
        through_old = jnp.where(here, lat_coef[side] * (lat_ring[side] - before), through_old)
        halves = jnp.where(here, lat_coef[side] * lat_ring[side] * f + c * ring * lat_change[side], halves)
    flux_down = down * (pltpu.roll(e, lanes - 2 * tracers, 1) - e)
    flux_north = north * (pltpu.roll(e, rows - 1, 0) - e)
    inside = (pltpu.roll(flux_down, 2 * tracers, 1) - flux_down) + (pltpu.roll(flux_north, 1, 0) - flux_north) + inner * e
    beside = -inner * e
    corrections[parts[0], :] = e
    corrections[parts[1], :] = inside - through - (through_new - through_old)
    corrections[parts[2], :] = beside
    edges = [(rows - 1) * side for side in range(SIDES)]
    corrections[pl.ds(3 * rows, 8), :] = stacked(lat_coef + [c[i : i + 1] for i in edges])

    column_dots = [folded(value) for value in (
        own_field * e,
        (before + after) * e,
        (2.0 * y + inside) * e - after * (through + through_new) + before * through_old + halves,
    )]
    tile_lane, tile_row = iota((8, lanes), 1), iota((8, lanes), 0)
    total = jnp.zeros((8, lanes), F32)
    for t in range(tracers):
        mine = lax.rem(tile_lane >> 1, tracers) == t
        for i in range(4):
            value = sums[pl.ds((4 * t + i) * 8, 8), :]
            if i:
                value = value + dots[t][i - 1] + jnp.where(mine, column_dots[i - 1], 0.0)
            total = jnp.where(tile_row == 4 * t + i, jnp.sum(value, axis=0, keepdims=True), total)
    total = jnp.sum(total, axis=1, keepdims=True)
    total = jnp.sum(jnp.where(tile_row == tile_lane, total, 0.0), axis=0, keepdims=True)
    even_row = (iota((1, lanes), 1) & 1) == 0
    south, north_ = edges
    lon_shares = [2.0 * c[i : i + 1] * part for i, part in zip(edges, lat_change)]
    shares = [total, 2.0 * lat_coef[1] * f[north_ : north_ + 1], jnp.where(even_row, lon_shares[0], lat_change[0]),
              jnp.where(even_row, lon_shares[1], f[south : south + 1])]
    for i, share in enumerate(shares):
        result[pl.ds(i, devices, SHARES), :] = jnp.broadcast_to(share, (devices, lanes))


def finish_kernel(tracers, nz, rows, devices, field, image, twice, corrections, sums, solution_out, residual_out,
                  solution, residual, sems):
    lanes = field.shape[1]
    across, along = lax.axis_size("lon"), lax.axis_size("lat")
    one = iota((1, lanes), 1)
    even_one = (one & 1) == 0
    total, to_north, lon_south, mixed = [sums[pl.ds(i, devices, SHARES), :] for i in range(SHARES)]
    total = jnp.sum(total, axis=0, keepdims=True)
    even_lane = (iota((devices, lanes), 1) & 1) == 0
    from_east = lambda x: pltpu.roll(pltpu.roll(x, devices - along, 0), lanes - 1, 1)
    from_north = lambda x: pltpu.roll(x, devices - 1, 0)
    beyond = from_east(lon_south)
    cross = jnp.where(even_lane, lon_south * beyond - mixed * from_north(beyond), 0.0)
    cross = cross + to_north * from_north(jnp.where(even_lane, -from_east(mixed), mixed))
    cross = jnp.sum(cross, axis=0, keepdims=True)

    lon, lat = lax.axis_index("lon"), lax.axis_index("lat")
    share = lambda i, j, at: sums[pl.ds(SHARES * (i * along + j) + at, 1), :]
    faces = corrections[pl.ds(3 * rows, 8), :]
    east, west = lax.rem(lon + 1, across), lax.rem(lon + across - 1, across)
    south, north = jnp.maximum(lat - 1, 0), jnp.minimum(lat + 1, along - 1)
    northern = jnp.where(lat < along - 1, 1.0, 0.0)
    lat_sides = (share(lon, south, 1) * jnp.where(lat > 0, 0.5, 0.0),
                 faces[1:2] * jnp.where(even_one, -pltpu.roll(share(east, north, 3), lanes - 1, 1), share(lon, north, 3)))
    lon_sides = (from_neighbours(share(east, lat, 2), 0.5 * share(west, lat, 2), even_one),
                 from_neighbours(-northern * share(east, north, 2), 0.5 * share(west, lat, 3), even_one))
    sides = [lat_sides[i] + jnp.where(even_one, faces[2 + i : 3 + i] * lon_sides[i], lon_sides[i]) for i in range(SIDES)]
    row = iota((rows, lanes), 0)
    e, change, beside = [corrections[pl.ds(i * rows, rows), :] for i in range(3)]
    change = change + jnp.where(row == 0, sides[0], jnp.where(row == rows - 1, sides[1], 0.0))

    lane = iota((CHUNK, rows, lanes), 2)
    narrow = iota((rows, lanes), 1)
    edge = (lane == 0) | (lane == lanes - 1)
    near = (lane <= 1) | (lane >= lanes - 2)

    def number(i):
        return jnp.sum(jnp.where(one == i, total, 0.0), axis=1, keepdims=True)

    copies = []
    for t in range(tracers):
        bb, bw, ww, wy = [number(4 * t + i) for i in range(4)]
        mine = lax.rem(one >> 1, tracers) == t
        wy = wy - jnp.sum(jnp.where(mine, cross, 0.0), axis=1, keepdims=True)
        whole = 1.0 / (bb + bw)
        step = bb * whole
        rest = bw * whole
        beta = step * (ww * whole) - rest * rest
        new = beta * bb
        tau = beta + rest
        step_next = new / (new + beta * new + tau * tau * bw - 2.0 * tau * step * ww + step * step * wy)
        both = step * step_next
        s_b = step + step_next * tau
        r_b = rest - step_next * tau
        r_w = both - step - step_next * tau
        s_edge = -both * e
        r_edge = jnp.where(lax.rem(narrow >> 1, tracers) == t, r_w * e + both * change,
                           both * jnp.where((narrow & 1) == 0, pltpu.roll(beside, 1, 1), pltpu.roll(beside, lanes - 1, 1)))
        for k in range(0, nz, CHUNK):
            slot, first = t * nz + k, k * tracers + t
            v, w, y = [levels_of(ref, slot, CHUNK, rows) for ref in (field, image, twice)]
            more = jnp.where(edge, unpacked(s_edge, first, tracers, CHUNK), 0.0)
            much = jnp.where(near, unpacked(r_edge, first, tracers, CHUNK), 0.0)
            put_levels(solution, slot, (s_b * v - both * w) + more)
            put_levels(residual, slot, (r_b * v + r_w * w + both * y) + much)
            at = pl.ds(slot * rows, CHUNK * rows)
            for a, b in ((solution, solution_out), (residual, residual_out)):
                copy = pltpu.make_async_copy(a.at[at], b.at[at], sems.at[len(copies)])
                copy.start()
                copies.append(copy)
    for copy in copies:
        copy.wait()


def swapped(x, axis, second):
    devices = lax.axis_size(axis)
    forward = [(i % 2 == 0) != second for i in range(devices)]
    return lax.ppermute(x, axis, [(i, (i + 1 if forward[i] else i - 1) % devices) for i in range(devices)])


def body(right_side, sea_mask, levels, east_diffusivity, north_diffusivity, vertical_diffusivity):
    tracers, nz, rows, lanes = right_side.shape
    devices = lax.axis_size("lon") * lax.axis_size("lat")
    flat = lambda x: x.reshape(-1, lanes)
    outside = lambda x: pltpu.with_memory_space_constraint(flat(x), pltpu.HBM)
    n = nz * rows
    cells = tracers * n * lanes

    def call(kernel, outs, flops, space=pltpu.VMEM, **more):
        outs = [m if isinstance(m, tuple) else (m, F32) for m in outs]
        cost = pl.CostEstimate(flops=flops, bytes_accessed=4 * lanes * sum(m for m, _ in outs), transcendentals=0)
        return pl.pallas_call(
            functools.partial(kernel, tracers, nz, rows),
            out_shape=[space((m, lanes), dtype) for m, dtype in outs],
            compiler_params=pltpu.CompilerParams(vmem_limit_bytes=32 * 1024 * 1024),
            cost_estimate=cost,
            **more,
        )

    def with_devices(kernel):
        return lambda tracers, nz, rows, *refs: kernel(tracers, nz, rows, devices, *refs)

    scratch = lambda m, dtype: pltpu.VMEM((m, lanes), dtype)
    *inputs, own, message, packed = call(
        columns_kernel,
        [tracers * n, (n, jnp.int32), (rows, jnp.int32)] + [(n, jnp.bfloat16)] * 3 + [3 * rows, 2 * rows, 3 * rows],
        20 * cells,
        in_specs=[pl.BlockSpec(memory_space=pltpu.HBM)] * 6,
        scratch_shapes=[pltpu.SemaphoreType.DMA((6,))],
        name="columns",
    )(*map(outside, (right_side, sea_mask, levels, east_diffusivity, north_diffusivity, vertical_diffusivity)))
    field = inputs[0]
    got_b = swapped(message, "lon", True)
    coef_east, coef_west, coef_north, coef_south, coef_down, east_own, north_own, image, rows_b = call(
        block_kernel, [n] * 7 + [tracers * n, FIELDS * nz], 20 * cells, name="block")(*inputs)
    got_rows_b = swapped(rows_b, "lat", True)
    coefs = (coef_east, coef_west, coef_north, coef_south, coef_down)
    rows_a, message_a = call(later_kernel, [FIELDS * nz, 2 * rows], cells, name="later")(
        field, image, east_own, north_own, own, rows_b)
    twice, packed_twice, sums = call(
        interior_kernel, [tracers * n, rows, 8 * 4 * tracers], 60000 * cells, name="interior"
    )(field, image, *coefs)
    got_a = swapped(message_a, "lon", False)
    got_rows_a = swapped(rows_a, "lat", False)
    image, twice, corrections, sums = call(
        with_devices(sums_kernel), [tracers * n, tracers * n, 3 * rows + 8, SHARES * devices], cells,
        input_output_aliases={0: 0, 1: 1}, name="sums",
    )(image, twice, coef_east, coef_north, coef_down, rows_a, rows_b, got_rows_a, got_rows_b, own, got_a, got_b, packed, packed_twice, sums)
    sums = lax.all_to_all(sums.reshape(devices, 1, -1), ("lon", "lat"), 0, 0, tiled=True).reshape(-1, lanes)
    copies = 2 * tracers * nz // CHUNK
    solution_field, residual = call(
        with_devices(finish_kernel), [tracers * n] * 2, 20 * cells, space=jax.ShapeDtypeStruct,
        out_specs=[pl.BlockSpec(memory_space=pltpu.HBM)] * 2,
        scratch_shapes=[scratch(tracers * n, F32)] * 2 + [pltpu.SemaphoreType.DMA((copies,))],
        name="finish",
    )(field, image, twice, corrections, sums)
    return solution_field.reshape(right_side.shape), residual.reshape(right_side.shape)


def solution(mesh):
    return jax.shard_map(
        body,
        mesh=mesh,
        in_specs=(
            P(None, None, "lat", "lon"),
            P(None, "lat", "lon"),
            P("lat", "lon"),
            P(None, "lat", "lon"),
            P(None, "lat", "lon"),
            P(None, "lat", "lon"),
        ),
        out_specs=(P(None, None, "lat", "lon"), P(None, None, "lat", "lon")),
        check_vma=False,
    )
```

```python
import functools

import jax
import jax.numpy as jnp
from jax import lax
from jax.experimental import pallas as pl
from jax.experimental.pallas import tpu as pltpu
from jax.sharding import PartitionSpec as P

F32 = jnp.float32
CHUNK = 8
SHARES = 4
SIDES = 2
FIELDS = 5


def iota(shape, axis):
    return lax.broadcasted_iota(jnp.int32, shape, axis)


def is_even(axis):
    return (lax.axis_index(axis) & 1) == 0


def levels_of(ref, first, count, rows):
    return ref[pl.ds(first * rows, count * rows), :].reshape(count, rows, ref.shape[1])


def put_levels(ref, first, value):
    count, rows, lanes = value.shape
    ref[pl.ds(first * rows, count * rows), :] = value.reshape(count * rows, lanes)


def laplacian(value, below, flux_above, coefs):
    _, rows, lanes = value.shape
    east, west, north, south, down = coefs
    change = east * (value - pltpu.roll(value, lanes - 1, 2)) + west * (value - pltpu.roll(value, 1, 2))
    change = change + (north * (value - pltpu.roll(value, rows - 1, 1)) + south * (value - pltpu.roll(value, 1, 1)))
    flux_down = down * (jnp.concatenate([value[1:], below], axis=0) - value)
    from_above = jnp.concatenate([flux_above, flux_down[:-1]], axis=0)
    return change + (from_above - flux_down), flux_down[-1:]


def packed_into(total, planes, first, step, pair):
    slots = [first + step * i for i in range(planes.shape[0])]
    moved = [pltpu.roll(planes[i], 2 * slot + 1, 1) for i, slot in enumerate(slots)]
    for slot, plane in zip(slots, moved):
        total = jnp.where(pair == slot, plane, total)
    return total


def unpacked(packed, first, step, count, offset=1):
    lanes = packed.shape[1]
    return jnp.stack([pltpu.roll(packed, (2 * lanes - offset - 2 * (first + step * i)) % lanes, 1) for i in range(count)])


def spread(plane, t, tracers, pair, level):
    moved = pltpu.roll(plane, 2 * t + 1, 1, stride=2 * tracers, stride_axis=0)
    return jnp.sum(jnp.where(pair == level * tracers + t, moved, 0.0), axis=0, keepdims=True)


def fours_into(total, planes, first, four):
    moved = [pltpu.roll(planes[i], 4 * (first + i) + 2, 1) for i in range(planes.shape[0])]
    for i, plane in enumerate(moved):
        total = jnp.where(four == first + i, plane, total)
    return total


def pairs_of(fours, lane):
    lanes = lane.shape[1]
    return jnp.where((lane & 2) == 0, pltpu.roll(fours[0], lanes - 1, 1), pltpu.roll(fours[1], 1, 1))


def from_neighbours(east, west, even_lane):
    return jnp.where(even_lane, pltpu.roll(east, east.shape[1] - 1, 1), pltpu.roll(west, 1, 1))


def face(own, other, even_lane):
    return jnp.where(even_lane, own * (other > 0).astype(F32), other * (own > 0).astype(F32))


def columns_kernel(tracers, nz, rows, field_in, mask_in, levels_in, east_in, north_in, down_in,
                   field, mask, levels, east, north, down, own, message, packed, sems):
    pairs = ((levels_in, levels), (mask_in, mask), (field_in, field), (east_in, east), (north_in, north), (down_in, down))
    copies = [pltpu.make_async_copy(a, b, sems.at[i]) for i, (a, b) in enumerate(pairs)]
    for copy in copies:
        copy.start()
    lanes = field.shape[1]
    lane, row = iota((rows, lanes), 1), iota((rows, lanes), 0)
    four, place = lane >> 2, lane & 3
    zero = jnp.zeros((rows, lanes), F32)
    chunk = nz // 2

    def fours_of(ref, start=0, see=lambda value, k: value.astype(F32)):
        total = zero
        for k in range(0, nz, chunk):
            total = fours_into(total, see(levels_of(ref, start + k, chunk, rows), k), k, four)
        return total

    for copy in copies[:3]:
        copy.wait()
    depth = levels[...]
    level = iota((chunk, rows, lanes), 0)
    wet = fours_of(mask, see=lambda value, k: jnp.where((value == 1) & (level + k < depth[None]), 1.0, 0.0))
    fields = [fours_of(field, t * nz) for t in range(tracers)]
    for copy in copies[3:]:
        copy.wait()
    wide_east, wide_north, wide_down = fours_of(east), fours_of(north), fours_of(down)
    own_east = wide_east * wet
    inner = own_east * pltpu.roll(wet, lanes - 1, 1)
    inner = jnp.where(place == 1, pltpu.roll(inner, 1, 1), inner)
    c_north = jnp.where(row == rows - 1, 0.0, wide_north * wet * pltpu.roll(wet, rows - 1, 0))
    c_south = pltpu.roll(c_north, 1, 0)
    c_down = jnp.where(four == nz - 1, 0.0, wide_down * wet * pltpu.roll(wet, lanes - 4, 1))
    images = []
    for v in fields:
        beside = jnp.where(place == 1, pltpu.roll(v, 1, 1), pltpu.roll(v, lanes - 1, 1))
        flux_down = c_down * (pltpu.roll(v, lanes - 4, 1) - v)
        change = inner * (v - beside) + c_north * (v - pltpu.roll(v, rows - 1, 0)) + c_south * (v - pltpu.roll(v, 1, 0))
        images.append(change + (pltpu.roll(flux_down, 4, 1) - flux_down))
    for i, parts in enumerate((images, fields, (own_east, own_east))):
        own[pl.ds(i * rows, rows), :] = pairs_of(parts, lane)
    put_message(rows, own, message, True)
    for i, part in enumerate((c_north, c_down, inner)):
        packed[pl.ds(i * rows, rows), :] = pairs_of((part, part), lane)


def block_kernel(tracers, nz, rows, field, mask, levels, east, north, down,
                 coef_east, coef_west, coef_north, coef_south, coef_down, east_own, north_own, image, rows_b):
    lanes = field.shape[1]
    chunk = nz // 2
    shape = (1, rows, lanes)
    last_lane, last_row = iota(shape, 2) == lanes - 1, iota(shape, 1) == rows - 1
    first_lane, first_row = iota(shape, 2) == 0, iota(shape, 1) == 0
    zero = jnp.zeros((rows, lanes), F32)
    depth = levels[...]
    level = iota((chunk + 1, rows, lanes), 0)
    above = [zero[None]] * tracers
    for k in range(0, nz, chunk):
        count = min(chunk + 1, nz - k)
        wet = (levels_of(mask, k, count, rows) == 1) & (level[:count] + k < depth[None])
        wet = jnp.where(wet, 1.0, 0.0)
        if count == chunk:
            wet = jnp.concatenate([wet, zero[None]], axis=0)
        ocean = wet[:chunk]
        own_east = levels_of(east, k, chunk, rows).astype(F32) * ocean
        own_north = levels_of(north, k, chunk, rows).astype(F32) * ocean
        c_east = jnp.where(last_lane, 0.0, own_east * pltpu.roll(ocean, lanes - 1, 2))
        c_north = jnp.where(last_row, 0.0, own_north * pltpu.roll(ocean, rows - 1, 1))
        c_down = levels_of(down, k, chunk, rows).astype(F32) * ocean * wet[1:]
        c_west = jnp.where(first_lane, 0.0, pltpu.roll(own_east, 1, 2) * ocean)
        c_south = jnp.where(first_row, 0.0, pltpu.roll(own_north, 1, 1) * ocean)
        c = (c_east, c_west, c_north, c_south, c_down)
        changes = []
        for t in range(tracers):
            value = levels_of(field, t * nz + k, chunk, rows)
            below = levels_of(field, t * nz + k + chunk, 1, rows) if k + chunk < nz else zero[None]
            change, above[t] = laplacian(value, below, above[t], c)
            changes.append(change)
        for ref, value in zip((coef_east, coef_west, coef_north, coef_south, coef_down, east_own, north_own), c + (own_east, own_north)):
            put_levels(ref, k, value)
        for t in range(tracers):
            put_levels(image, t * nz + k, changes[t])
    edge_rows(tracers, nz, rows, field, image, east_own, north_own, True, rows_b)


def put_message(rows, own, message, second):
    lanes = own.shape[1]
    eastern = is_even("lon") != second
    even_lane = (iota((rows, lanes), 1) & 1) == 0
    image, field = own[pl.ds(0, rows), :], own[pl.ds(rows, rows), :]
    to_east = jnp.where(even_lane, image, pltpu.roll(field, 1, 1))
    to_west = jnp.where(even_lane, pltpu.roll(field, lanes - 1, 1), image)
    message[pl.ds(0, rows), :] = jnp.where(eastern, to_east, to_west)
    message[pl.ds(rows, rows), :] = own[pl.ds(2 * rows, rows), :]


def edge_rows(tracers, nz, rows, field, image, east_own, north_own, second, out):
    southern = is_even("lat") if second else jnp.logical_not(is_even("lat"))

    def edge(side):
        first = (rows - 1) * side
        parts = [ref[pl.ds(first + t * nz * rows, nz, rows), :] for ref in (image, field) for t in range(tracers)]
        return parts + [(east_own, north_own)[side][pl.ds(first, nz, rows), :]]

    for at, (south, north_) in enumerate(zip(edge(0), edge(1))):
        out[pl.ds(at * nz, nz), :] = jnp.where(southern, south, north_)


def later_kernel(tracers, nz, rows, field, image, east_own, north_own, own, rows_b, rows_a, message_a):
    edge_rows(tracers, nz, rows, field, image, east_own, north_own, False, rows_a)
    put_message(rows, own, message_a, False)


def stacked(parts):
    lanes = parts[0].shape[1]
    row = iota((8, lanes), 0)
    total = jnp.zeros((8, lanes), F32)
    for i, part in enumerate(parts):
        total = jnp.where(row == i, part, total)
    return total


def folded(x):
    return sum(x[i : i + 8] for i in range(0, x.shape[0], 8))


def interior_kernel(tracers, nz, rows, field, image, coef_east, coef_west, coef_north, coef_south, coef_down,
                    twice, packed, sums):
    lanes = field.shape[1]
    pair = iota((rows, lanes), 1) >> 1
    zero = packed_twice = jnp.zeros((rows, lanes), F32)
    totals = [[zero] * 4 for _ in range(tracers)]
    above = [zero[None]] * tracers
    for k in range(0, nz, CHUNK):
        refs = (coef_east, coef_west, coef_north, coef_south, coef_down)
        c = [levels_of(ref, k, CHUNK, rows) for ref in refs]
        results = []
        for t in range(tracers):
            w = levels_of(image, t * nz + k, CHUNK, rows)
            below = levels_of(image, t * nz + k + CHUNK, 1, rows) if k + CHUNK < nz else zero[None]
            y, above[t] = laplacian(w, below, above[t], c)
            results.append(y)
            v = levels_of(field, t * nz + k, CHUNK, rows)
            for i, product in enumerate((v * v, v * w, w * w, w * y)):
                totals[t][i] = totals[t][i] + jnp.sum(product, axis=0)
        for t in range(tracers):
            packed_twice = packed_into(packed_twice, results[t], k * tracers + t, tracers, pair)
        for t in range(tracers):
            put_levels(twice, t * nz + k, results[t])
    packed[...] = packed_twice
    for t in range(tracers):
        for i in range(4):
            sums[pl.ds((4 * t + i) * 8, 8), :] = folded(totals[t][i])


def sums_kernel(tracers, nz, rows, devices, image_in, twice_in, coef_east, coef_north, coef_down, rows_a, rows_b, got_rows_a,
                got_rows_b, own, got_a, got_b, packed, packed_twice, sums, image, twice, corrections, result):
    lanes = own.shape[1]
    even = is_even("lat")
    pair, level = iota((nz, lanes), 1) >> 1, iota((nz, lanes), 0)
    row = iota((rows, lanes), 0)
    north, down, inner = [packed[pl.ds(i * rows, rows), :] for i in range(3)]
    dots = [[jnp.zeros((8, lanes), F32) for _ in range(3)] for _ in range(tracers)]
    nothing = jnp.zeros((1, lanes), F32)
    row_change, row_inside = jnp.zeros((rows, lanes), F32), jnp.zeros((rows, lanes), F32)
    lat_coef, lat_ring, lat_change = [], [], []
    stores = []
    for side in range(SIDES):
        def part(at, a, b):
            first, second = (b, a) if side == 0 else (a, b)
            return jnp.where(even, first[pl.ds(at * nz, nz), :], second[pl.ds(at * nz, nz), :])

        own_row = lambda at: part(at, rows_a, rows_b)
        got_row = lambda at: part(at, got_rows_a, got_rows_b)
        own_coef, got_coef = own_row(2 * tracers), got_row(2 * tracers)
        c = got_coef * (own_coef > 0).astype(F32) if side == 0 else own_coef * (got_coef > 0).astype(F32)
        c = c * jnp.where(lax.axis_index("lat") == (0, lax.axis_size("lat") - 1)[side], 0.0, 1.0)
        first, next_row, between = ((0, 1, 0), (rows - 1, rows - 2, rows - 2))[side]
        c_east, c_down = coef_east[pl.ds(first, nz, rows), :], coef_down[pl.ds(first, nz, rows), :]
        c_inner = coef_north[pl.ds(between, nz, rows), :]
        packed_coef, packed_ring, packed_e, packed_inside = [nothing] * 4
        for t in range(tracers):
            b, w = own_row(tracers + t), own_row(t)
            f = c * (got_row(tracers + t) - b)
            e = -f
            ring = got_row(t) + f
            flux_east = c_east * (pltpu.roll(e, lanes - 1, 1) - e)
            flux_down = c_down * (pltpu.roll(e, nz - 1, 0) - e)
            inside = (pltpu.roll(flux_east, 1, 1) - flux_east) + (pltpu.roll(flux_down, 1, 0) - flux_down) + c_inner * e
            changed = w + e
            through = c * (ring - changed)
            at = pl.ds(first + t * nz * rows, nz, rows)
            at_next = pl.ds(next_row + t * nz * rows, nz, rows)
            y = twice_in[at, :]
            stores.append((image, at, changed))
            stores.append((twice, at, y + inside - through))
            stores.append((twice, at_next, twice_in[at_next, :] - c_inner * e))
            for i, value in enumerate((b * e, (w + changed) * e, (2.0 * y + inside) * e - changed * through)):
                dots[t][i] = dots[t][i] + folded(value)
            packed_coef = packed_coef + spread(c, t, tracers, pair, level)
            packed_ring = packed_ring + spread(ring, t, tracers, pair, level)
            packed_e = packed_e + spread(e, t, tracers, pair, level)
            packed_inside = packed_inside + spread(inside, t, tracers, pair, level)
        row_change = jnp.where(row == first, packed_e, row_change)
        row_inside = jnp.where(row == first, packed_inside, row_inside)
        row_inside = jnp.where(row == next_row, -north[between : between + 1] * packed_e, row_inside)
        lat_coef.append(packed_coef)
        lat_ring.append(packed_ring)
        lat_change.append(-packed_e)
    for ref, at, value in stores:
        ref[at, :] = value

    even = is_even("lon")
    even_lane = (iota((rows, lanes), 1) & 1) == 0

    def neighbours(at):
        a, b = got_a[at, :], got_b[at, :]
        return jnp.where(even, a, b), jnp.where(even, b, a)

    parts = [pl.ds(i * rows, rows) for i in range(3)]
    own_image, own_field, own_east = [own[p, :] for p in parts]
    columns = neighbours(parts[0])
    got_image, got_field = from_neighbours(*columns, even_lane), jnp.where(even_lane, *columns)
    got_east = from_neighbours(*neighbours(parts[1]), even_lane)
    before = own_image + row_change
    y = packed_twice[...] + row_inside
    c = face(own_east, got_east, even_lane)
    f = c * (got_field - own_field)
    e = -f
    after = before + e
    ring = got_image + f
    through = c * (ring - after)
    through_new = through_old = halves = jnp.zeros((rows, lanes), F32)
    for side in range(SIDES):
        here = row == (rows - 1) * side
        through_new = jnp.where(here, lat_coef[side] * (lat_ring[side] - after), through_new)
        through_old = jnp.where(here, lat_coef[side] * (lat_ring[side] - before), through_old)
        halves = jnp.where(here, lat_coef[side] * lat_ring[side] * f + c * ring * lat_change[side], halves)
    flux_down = down * (pltpu.roll(e, lanes - 2 * tracers, 1) - e)
    flux_north = north * (pltpu.roll(e, rows - 1, 0) - e)
    inside = (pltpu.roll(flux_down, 2 * tracers, 1) - flux_down) + (pltpu.roll(flux_north, 1, 0) - flux_north) + inner * e
    beside = -inner * e
    corrections[parts[0], :] = e
    corrections[parts[1], :] = inside - through - (through_new - through_old)
    corrections[parts[2], :] = beside
    edges = [(rows - 1) * side for side in range(SIDES)]
    corrections[pl.ds(3 * rows, 8), :] = stacked(lat_coef + [c[i : i + 1] for i in edges])

    column_dots = [folded(value) for value in (
        own_field * e,
        (before + after) * e,
        (2.0 * y + inside) * e - after * (through + through_new) + before * through_old + halves,
    )]
    tile_lane, tile_row = iota((8, lanes), 1), iota((8, lanes), 0)
    total = jnp.zeros((8, lanes), F32)
    for t in range(tracers):
        mine = lax.rem(tile_lane >> 1, tracers) == t
        for i in range(4):
            value = sums[pl.ds((4 * t + i) * 8, 8), :]
            if i:
                value = value + dots[t][i - 1] + jnp.where(mine, column_dots[i - 1], 0.0)
            total = jnp.where(tile_row == 4 * t + i, jnp.sum(value, axis=0, keepdims=True), total)
    total = jnp.sum(total, axis=1, keepdims=True)
    total = jnp.sum(jnp.where(tile_row == tile_lane, total, 0.0), axis=0, keepdims=True)
    even_row = (iota((1, lanes), 1) & 1) == 0
    south, north_ = edges
    lon_shares = [2.0 * c[i : i + 1] * part for i, part in zip(edges, lat_change)]
    shares = [total, 2.0 * lat_coef[1] * f[north_ : north_ + 1], jnp.where(even_row, lon_shares[0], lat_change[0]),
              jnp.where(even_row, lon_shares[1], f[south : south + 1])]
    for i, share in enumerate(shares):
        result[pl.ds(i, devices, SHARES), :] = jnp.broadcast_to(share, (devices, lanes))


def finish_kernel(tracers, nz, rows, devices, field, image, twice, corrections, sums, solution_out, residual_out,
                  solution, residual, sems):
    lanes = field.shape[1]
    across, along = lax.axis_size("lon"), lax.axis_size("lat")
    one = iota((1, lanes), 1)
    even_one = (one & 1) == 0
    total, to_north, lon_south, mixed = [sums[pl.ds(i, devices, SHARES), :] for i in range(SHARES)]
    total = jnp.sum(total, axis=0, keepdims=True)
    even_lane = (iota((devices, lanes), 1) & 1) == 0
    from_east = lambda x: pltpu.roll(pltpu.roll(x, devices - along, 0), lanes - 1, 1)
    from_north = lambda x: pltpu.roll(x, devices - 1, 0)
    beyond = from_east(lon_south)
    cross = jnp.where(even_lane, lon_south * beyond - mixed * from_north(beyond), 0.0)
    cross = cross + to_north * from_north(jnp.where(even_lane, -from_east(mixed), mixed))
    cross = jnp.sum(cross, axis=0, keepdims=True)

    lon, lat = lax.axis_index("lon"), lax.axis_index("lat")
    tile_row = iota((8, lanes), 0)

    def share(i, j, at):
        first = SHARES * (i * along + j)
        tile = sums[pl.ds(pl.multiple_of(first // 8 * 8, 8), 8), :]
        return jnp.sum(jnp.where(tile_row == lax.rem(first, 8) + at, tile, 0.0), axis=0, keepdims=True)

    faces = corrections[pl.ds(3 * rows, 8), :]
    east, west = lax.rem(lon + 1, across), lax.rem(lon + across - 1, across)
    south, north = jnp.maximum(lat - 1, 0), jnp.minimum(lat + 1, along - 1)
    northern = jnp.where(lat < along - 1, 1.0, 0.0)
    lat_sides = (share(lon, south, 1) * jnp.where(lat > 0, 0.5, 0.0),
                 faces[1:2] * jnp.where(even_one, -pltpu.roll(share(east, north, 3), lanes - 1, 1), share(lon, north, 3)))
    lon_sides = (from_neighbours(share(east, lat, 2), 0.5 * share(west, lat, 2), even_one),
                 from_neighbours(-northern * share(east, north, 2), 0.5 * share(west, lat, 3), even_one))
    sides = [lat_sides[i] + jnp.where(even_one, faces[2 + i : 3 + i] * lon_sides[i], lon_sides[i]) for i in range(SIDES)]
    row = iota((rows, lanes), 0)
    e, change, beside = [corrections[pl.ds(i * rows, rows), :] for i in range(3)]
    change = change + jnp.where(row == 0, sides[0], jnp.where(row == rows - 1, sides[1], 0.0))

    lane = iota((CHUNK, rows, lanes), 2)
    narrow = iota((rows, lanes), 1)
    edge = (lane == 0) | (lane == lanes - 1)
    near = (lane <= 1) | (lane >= lanes - 2)

    def number(i):
        return jnp.sum(jnp.where(one == i, total, 0.0), axis=1, keepdims=True)

    copies = []
    for t in range(tracers):
        bb, bw, ww, wy = [number(4 * t + i) for i in range(4)]
        mine = lax.rem(one >> 1, tracers) == t
        wy = wy - jnp.sum(jnp.where(mine, cross, 0.0), axis=1, keepdims=True)
        whole = 1.0 / (bb + bw)
        step = bb * whole
        rest = bw * whole
        beta = jnp.maximum(step * (ww * whole) - rest * rest, 0.0)
        new = beta * bb
        tau = beta + rest
        step_next = new / (new + beta * new + tau * tau * bw - 2.0 * tau * step * ww + step * step * wy)
        step_next = jnp.minimum(jnp.maximum(step_next, 0.0), 1.0)
        both = step * step_next
        s_b = step + step_next * tau
        r_b = rest - step_next * tau
        r_w = both - step - step_next * tau
        s_edge = -both * e
        r_edge = jnp.where(lax.rem(narrow >> 1, tracers) == t, r_w * e + both * change,
                           both * jnp.where((narrow & 1) == 0, pltpu.roll(beside, 1, 1), pltpu.roll(beside, lanes - 1, 1)))
        for k in range(0, nz, CHUNK):
            slot, first = t * nz + k, k * tracers + t
            v, w, y = [levels_of(ref, slot, CHUNK, rows) for ref in (field, image, twice)]
            more = jnp.where(edge, unpacked(s_edge, first, tracers, CHUNK), 0.0)
            much = jnp.where(near, unpacked(r_edge, first, tracers, CHUNK), 0.0)
            put_levels(solution, slot, (s_b * v - both * w) + more)
            put_levels(residual, slot, (r_b * v + r_w * w + both * y) + much)
            at = pl.ds(slot * rows, CHUNK * rows)
            for a, b in ((solution, solution_out), (residual, residual_out)):
                copy = pltpu.make_async_copy(a.at[at], b.at[at], sems.at[len(copies)])
                copy.start()
                copies.append(copy)
    for copy in copies:
        copy.wait()


def swapped(x, axis, second):
    devices = lax.axis_size(axis)
    forward = [(i % 2 == 0) != second for i in range(devices)]
    return lax.ppermute(x, axis, [(i, (i + 1 if forward[i] else i - 1) % devices) for i in range(devices)])


def body(right_side, sea_mask, levels, east_diffusivity, north_diffusivity, vertical_diffusivity):
    tracers, nz, rows, lanes = right_side.shape
    devices = lax.axis_size("lon") * lax.axis_size("lat")
    flat = lambda x: x.reshape(-1, lanes)
    outside = lambda x: pltpu.with_memory_space_constraint(flat(x), pltpu.HBM)
    n = nz * rows
    cells = tracers * n * lanes

    def call(kernel, outs, flops, space=pltpu.VMEM, **more):
        outs = [m if isinstance(m, tuple) else (m, F32) for m in outs]
        cost = pl.CostEstimate(flops=flops, bytes_accessed=4 * lanes * sum(m for m, _ in outs), transcendentals=0)
        return pl.pallas_call(
            functools.partial(kernel, tracers, nz, rows),
            out_shape=[space((m, lanes), dtype) for m, dtype in outs],
            compiler_params=pltpu.CompilerParams(vmem_limit_bytes=32 * 1024 * 1024),
            cost_estimate=cost,
            **more,
        )

    def with_devices(kernel):
        return lambda tracers, nz, rows, *refs: kernel(tracers, nz, rows, devices, *refs)

    scratch = lambda m, dtype: pltpu.VMEM((m, lanes), dtype)
    *inputs, own, message, packed = call(
        columns_kernel,
        [tracers * n, (n, jnp.int32), (rows, jnp.int32)] + [(n, jnp.bfloat16)] * 3 + [3 * rows, 2 * rows, 3 * rows],
        20 * cells,
        in_specs=[pl.BlockSpec(memory_space=pltpu.HBM)] * 6,
        scratch_shapes=[pltpu.SemaphoreType.DMA((6,))],
        name="columns",
    )(*map(outside, (right_side, sea_mask, levels, east_diffusivity, north_diffusivity, vertical_diffusivity)))
    field = inputs[0]
    got_b = swapped(message, "lon", True)
    coef_east, coef_west, coef_north, coef_south, coef_down, east_own, north_own, image, rows_b = call(
        block_kernel, [n] * 7 + [tracers * n, FIELDS * nz], 20 * cells, name="block")(*inputs)
    got_rows_b = swapped(rows_b, "lat", True)
    coefs = (coef_east, coef_west, coef_north, coef_south, coef_down)
    rows_a, message_a = call(later_kernel, [FIELDS * nz, 2 * rows], cells, name="later")(
        field, image, east_own, north_own, own, rows_b)
    twice, packed_twice, sums = call(
        interior_kernel, [tracers * n, rows, 8 * 4 * tracers], 60000 * cells, name="interior"
    )(field, image, *coefs)
    got_a = swapped(message_a, "lon", False)
    got_rows_a = swapped(rows_a, "lat", False)
    image, twice, corrections, sums = call(
        with_devices(sums_kernel), [tracers * n, tracers * n, 3 * rows + 8, SHARES * devices], cells,
        input_output_aliases={0: 0, 1: 1}, name="sums",
    )(image, twice, coef_east, coef_north, coef_down, rows_a, rows_b, got_rows_a, got_rows_b, own, got_a, got_b, packed, packed_twice, sums)
    sums = lax.all_to_all(sums.reshape(devices, 1, -1), ("lon", "lat"), 0, 0, tiled=True).reshape(-1, lanes)
    copies = 2 * tracers * nz // CHUNK
    solution_field, residual = call(
        with_devices(finish_kernel), [tracers * n] * 2, 20 * cells, space=jax.ShapeDtypeStruct,
        out_specs=[pl.BlockSpec(memory_space=pltpu.HBM)] * 2,
        scratch_shapes=[scratch(tracers * n, F32)] * 2 + [pltpu.SemaphoreType.DMA((copies,))],
        name="finish",
    )(field, image, twice, corrections, sums)
    return solution_field.reshape(right_side.shape), residual.reshape(right_side.shape)


def solution(mesh):
    return jax.shard_map(
        body,
        mesh=mesh,
        in_specs=(
            P(None, None, "lat", "lon"),
            P(None, "lat", "lon"),
            P("lat", "lon"),
            P(None, "lat", "lon"),
            P(None, "lat", "lon"),
            P(None, "lat", "lon"),
        ),
        out_specs=(P(None, None, "lat", "lon"), P(None, None, "lat", "lon")),
        check_vma=False,
    )
```

```python
import functools

import jax
import jax.numpy as jnp
from jax import lax
from jax.experimental import pallas as pl
from jax.experimental.pallas import tpu as pltpu
from jax.sharding import PartitionSpec as P

F32 = jnp.float32
CHUNK = 8
SHARES = 4
SIDES = 2
FIELDS = 5


def iota(shape, axis):
    return lax.broadcasted_iota(jnp.int32, shape, axis)


def is_even(axis):
    return (lax.axis_index(axis) & 1) == 0


def levels_of(ref, first, count, rows):
    return ref[pl.ds(first * rows, count * rows), :].reshape(count, rows, ref.shape[1])


def put_levels(ref, first, value):
    count, rows, lanes = value.shape
    ref[pl.ds(first * rows, count * rows), :] = value.reshape(count * rows, lanes)


def laplacian(value, below, flux_above, coefs):
    _, rows, lanes = value.shape
    east, west, north, south, down = coefs
    change = east * (value - pltpu.roll(value, lanes - 1, 2)) + west * (value - pltpu.roll(value, 1, 2))
    change = change + (north * (value - pltpu.roll(value, rows - 1, 1)) + south * (value - pltpu.roll(value, 1, 1)))
    flux_down = down * (jnp.concatenate([value[1:], below], axis=0) - value)
    from_above = jnp.concatenate([flux_above, flux_down[:-1]], axis=0)
    return change + (from_above - flux_down), flux_down[-1:]


def packed_into(total, planes, first, step, pair):
    slots = [first + step * i for i in range(planes.shape[0])]
    moved = [pltpu.roll(planes[i], 2 * slot + 1, 1) for i, slot in enumerate(slots)]
    for slot, plane in zip(slots, moved):
        total = jnp.where(pair == slot, plane, total)
    return total


def unpacked(packed, first, step, count, offset=1):
    lanes = packed.shape[1]
    return jnp.stack([pltpu.roll(packed, (2 * lanes - offset - 2 * (first + step * i)) % lanes, 1) for i in range(count)])


def spread(plane, t, tracers, pair, level):
    moved = pltpu.roll(plane, 2 * t + 1, 1, stride=2 * tracers, stride_axis=0)
    return jnp.sum(jnp.where(pair == level * tracers + t, moved, 0.0), axis=0, keepdims=True)


def fours_into(total, planes, first, four):
    moved = [pltpu.roll(planes[i], 4 * (first + i) + 2, 1) for i in range(planes.shape[0])]
    for i, plane in enumerate(moved):
        total = jnp.where(four == first + i, plane, total)
    return total


def pairs_of(fours, lane):
    lanes = lane.shape[1]
    return jnp.where((lane & 2) == 0, pltpu.roll(fours[0], lanes - 1, 1), pltpu.roll(fours[1], 1, 1))


def from_neighbours(east, west, even_lane):
    return jnp.where(even_lane, pltpu.roll(east, east.shape[1] - 1, 1), pltpu.roll(west, 1, 1))


def face(own, other, even_lane):
    return jnp.where(even_lane, own * (other > 0).astype(F32), other * (own > 0).astype(F32))


def columns_kernel(tracers, nz, rows, field_in, mask_in, levels_in, east_in, north_in, down_in,
                   field, mask, levels, east, north, down, own, message, packed, sems):
    pairs = ((levels_in, levels), (mask_in, mask), (field_in, field), (east_in, east), (north_in, north), (down_in, down))
    copies = [pltpu.make_async_copy(a, b, sems.at[i]) for i, (a, b) in enumerate(pairs)]
    for copy in copies:
        copy.start()
    lanes = field.shape[1]
    lane, row = iota((rows, lanes), 1), iota((rows, lanes), 0)
    four, place = lane >> 2, lane & 3
    zero = jnp.zeros((rows, lanes), F32)
    chunk = nz // 2

    def fours_of(ref, start=0, see=lambda value, k: value.astype(F32)):
        total = zero
        for k in range(0, nz, chunk):
            total = fours_into(total, see(levels_of(ref, start + k, chunk, rows), k), k, four)
        return total

    for copy in copies[:3]:
        copy.wait()
    depth = levels[...]
    level = iota((chunk, rows, lanes), 0)
    wet = fours_of(mask, see=lambda value, k: jnp.where((value == 1) & (level + k < depth[None]), 1.0, 0.0))
    fields = [fours_of(field, t * nz) for t in range(tracers)]
    for copy in copies[3:]:
        copy.wait()
    wide_east, wide_north, wide_down = fours_of(east), fours_of(north), fours_of(down)
    own_east = wide_east * wet
    inner = own_east * pltpu.roll(wet, lanes - 1, 1)
    inner = jnp.where(place == 1, pltpu.roll(inner, 1, 1), inner)
    c_north = jnp.where(row == rows - 1, 0.0, wide_north * wet * pltpu.roll(wet, rows - 1, 0))
    c_south = pltpu.roll(c_north, 1, 0)
    c_down = jnp.where(four == nz - 1, 0.0, wide_down * wet * pltpu.roll(wet, lanes - 4, 1))
    images = []
    for v in fields:
        beside = jnp.where(place == 1, pltpu.roll(v, 1, 1), pltpu.roll(v, lanes - 1, 1))
        flux_down = c_down * (pltpu.roll(v, lanes - 4, 1) - v)
        change = inner * (v - beside) + c_north * (v - pltpu.roll(v, rows - 1, 0)) + c_south * (v - pltpu.roll(v, 1, 0))
        images.append(change + (pltpu.roll(flux_down, 4, 1) - flux_down))
    for i, parts in enumerate((images, fields, (own_east, own_east))):
        own[pl.ds(i * rows, rows), :] = pairs_of(parts, lane)
    put_message(rows, own, message, True)
    for i, part in enumerate((c_north, c_down, inner)):
        packed[pl.ds(i * rows, rows), :] = pairs_of((part, part), lane)


def block_kernel(tracers, nz, rows, field, mask, levels, east, north, down,
                 coef_east, coef_west, coef_north, coef_south, coef_down, east_own, north_own, image, rows_b):
    lanes = field.shape[1]
    chunk = nz // 2
    shape = (1, rows, lanes)
    last_lane, last_row = iota(shape, 2) == lanes - 1, iota(shape, 1) == rows - 1
    first_lane, first_row = iota(shape, 2) == 0, iota(shape, 1) == 0
    zero = jnp.zeros((rows, lanes), F32)
    depth = levels[...]
    level = iota((chunk + 1, rows, lanes), 0)
    above = [zero[None]] * tracers
    for k in range(0, nz, chunk):
        count = min(chunk + 1, nz - k)
        wet = (levels_of(mask, k, count, rows) == 1) & (level[:count] + k < depth[None])
        wet = jnp.where(wet, 1.0, 0.0)
        if count == chunk:
            wet = jnp.concatenate([wet, zero[None]], axis=0)
        ocean = wet[:chunk]
        own_east = levels_of(east, k, chunk, rows).astype(F32) * ocean
        own_north = levels_of(north, k, chunk, rows).astype(F32) * ocean
        c_east = jnp.where(last_lane, 0.0, own_east * pltpu.roll(ocean, lanes - 1, 2))
        c_north = jnp.where(last_row, 0.0, own_north * pltpu.roll(ocean, rows - 1, 1))
        c_down = levels_of(down, k, chunk, rows).astype(F32) * ocean * wet[1:]
        c_west = jnp.where(first_lane, 0.0, pltpu.roll(own_east, 1, 2) * ocean)
        c_south = jnp.where(first_row, 0.0, pltpu.roll(own_north, 1, 1) * ocean)
        c = (c_east, c_west, c_north, c_south, c_down)
        changes = []
        for t in range(tracers):
            value = levels_of(field, t * nz + k, chunk, rows)
            below = levels_of(field, t * nz + k + chunk, 1, rows) if k + chunk < nz else zero[None]
            change, above[t] = laplacian(value, below, above[t], c)
            changes.append(change)
        for ref, value in zip((coef_east, coef_west, coef_north, coef_south, coef_down, east_own, north_own), c + (own_east, own_north)):
            put_levels(ref, k, value)
        for t in range(tracers):
            put_levels(image, t * nz + k, changes[t])
    edge_rows(tracers, nz, rows, field, image, east_own, north_own, True, rows_b)


def put_message(rows, own, message, second):
    lanes = own.shape[1]
    eastern = is_even("lon") != second
    even_lane = (iota((rows, lanes), 1) & 1) == 0
    image, field = own[pl.ds(0, rows), :], own[pl.ds(rows, rows), :]
    to_east = jnp.where(even_lane, image, pltpu.roll(field, 1, 1))
    to_west = jnp.where(even_lane, pltpu.roll(field, lanes - 1, 1), image)
    message[pl.ds(0, rows), :] = jnp.where(eastern, to_east, to_west)
    message[pl.ds(rows, rows), :] = own[pl.ds(2 * rows, rows), :]


def edge_rows(tracers, nz, rows, field, image, east_own, north_own, second, out):
    southern = is_even("lat") if second else jnp.logical_not(is_even("lat"))

    def edge(side):
        first = (rows - 1) * side
        parts = [ref[pl.ds(first + t * nz * rows, nz, rows), :] for ref in (image, field) for t in range(tracers)]
        return parts + [(east_own, north_own)[side][pl.ds(first, nz, rows), :]]

    for at, (south, north_) in enumerate(zip(edge(0), edge(1))):
        out[pl.ds(at * nz, nz), :] = jnp.where(southern, south, north_)


def later_kernel(tracers, nz, rows, field, image, east_own, north_own, own, rows_b, rows_a, message_a):
    edge_rows(tracers, nz, rows, field, image, east_own, north_own, False, rows_a)
    put_message(rows, own, message_a, False)


def stacked(parts):
    lanes = parts[0].shape[1]
    row = iota((8, lanes), 0)
    total = jnp.zeros((8, lanes), F32)
    for i, part in enumerate(parts):
        total = jnp.where(row == i, part, total)
    return total


def folded(x):
    return sum(x[i : i + 8] for i in range(0, x.shape[0], 8))


def interior_kernel(tracers, nz, rows, field, image, coef_east, coef_west, coef_north, coef_south, coef_down,
                    twice, packed, sums):
    lanes = field.shape[1]
    pair = iota((rows, lanes), 1) >> 1
    zero = packed_twice = jnp.zeros((rows, lanes), F32)
    totals = [[zero] * 4 for _ in range(tracers)]
    above = [zero[None]] * tracers
    for k in range(0, nz, CHUNK):
        refs = (coef_east, coef_west, coef_north, coef_south, coef_down)
        c = [levels_of(ref, k, CHUNK, rows) for ref in refs]
        results = []
        for t in range(tracers):
            w = levels_of(image, t * nz + k, CHUNK, rows)
            below = levels_of(image, t * nz + k + CHUNK, 1, rows) if k + CHUNK < nz else zero[None]
            y, above[t] = laplacian(w, below, above[t], c)
            results.append(y)
            v = levels_of(field, t * nz + k, CHUNK, rows)
            for i, product in enumerate((v * v, v * w, w * w, w * y)):
                totals[t][i] = totals[t][i] + jnp.sum(product, axis=0)
        for t in range(tracers):
            packed_twice = packed_into(packed_twice, results[t], k * tracers + t, tracers, pair)
        for t in range(tracers):
            put_levels(twice, t * nz + k, results[t])
    packed[...] = packed_twice
    for t in range(tracers):
        for i in range(4):
            sums[pl.ds((4 * t + i) * 8, 8), :] = folded(totals[t][i])


def sums_kernel(tracers, nz, rows, devices, image_in, twice_in, coef_east, coef_north, coef_down, rows_a, rows_b, got_rows_a,
                got_rows_b, own, got_a, got_b, packed, packed_twice, sums, image, twice, corrections, result):
    lanes = own.shape[1]
    even = is_even("lat")
    pair, level = iota((nz, lanes), 1) >> 1, iota((nz, lanes), 0)
    row = iota((rows, lanes), 0)
    north, down, inner = [packed[pl.ds(i * rows, rows), :] for i in range(3)]
    dots = [[jnp.zeros((8, lanes), F32) for _ in range(3)] for _ in range(tracers)]
    nothing = jnp.zeros((1, lanes), F32)
    row_change, row_inside = jnp.zeros((rows, lanes), F32), jnp.zeros((rows, lanes), F32)
    lat_coef, lat_ring, lat_change = [], [], []
    stores = []
    for side in range(SIDES):
        def part(at, a, b):
            first, second = (b, a) if side == 0 else (a, b)
            return jnp.where(even, first[pl.ds(at * nz, nz), :], second[pl.ds(at * nz, nz), :])

        own_row = lambda at: part(at, rows_a, rows_b)
        got_row = lambda at: part(at, got_rows_a, got_rows_b)
        own_coef, got_coef = own_row(2 * tracers), got_row(2 * tracers)
        c = got_coef * (own_coef > 0).astype(F32) if side == 0 else own_coef * (got_coef > 0).astype(F32)
        c = c * jnp.where(lax.axis_index("lat") == (0, lax.axis_size("lat") - 1)[side], 0.0, 1.0)
        first, next_row, between = ((0, 1, 0), (rows - 1, rows - 2, rows - 2))[side]
        c_east, c_down = coef_east[pl.ds(first, nz, rows), :], coef_down[pl.ds(first, nz, rows), :]
        c_inner = coef_north[pl.ds(between, nz, rows), :]
        packed_coef, packed_ring, packed_e, packed_inside = [nothing] * 4
        for t in range(tracers):
            b, w = own_row(tracers + t), own_row(t)
            f = c * (got_row(tracers + t) - b)
            e = -f
            ring = got_row(t) + f
            flux_east = c_east * (pltpu.roll(e, lanes - 1, 1) - e)
            flux_down = c_down * (pltpu.roll(e, nz - 1, 0) - e)
            inside = (pltpu.roll(flux_east, 1, 1) - flux_east) + (pltpu.roll(flux_down, 1, 0) - flux_down) + c_inner * e
            changed = w + e
            through = c * (ring - changed)
            at = pl.ds(first + t * nz * rows, nz, rows)
            at_next = pl.ds(next_row + t * nz * rows, nz, rows)
            y = twice_in[at, :]
            stores.append((image, at, changed))
            stores.append((twice, at, y + inside - through))
            stores.append((twice, at_next, twice_in[at_next, :] - c_inner * e))
            for i, value in enumerate((b * e, (w + changed) * e, (2.0 * y + inside) * e - changed * through)):
                dots[t][i] = dots[t][i] + folded(value)
            packed_coef = packed_coef + spread(c, t, tracers, pair, level)
            packed_ring = packed_ring + spread(ring, t, tracers, pair, level)
            packed_e = packed_e + spread(e, t, tracers, pair, level)
            packed_inside = packed_inside + spread(inside, t, tracers, pair, level)
        row_change = jnp.where(row == first, packed_e, row_change)
        row_inside = jnp.where(row == first, packed_inside, row_inside)
        row_inside = jnp.where(row == next_row, -north[between : between + 1] * packed_e, row_inside)
        lat_coef.append(packed_coef)
        lat_ring.append(packed_ring)
        lat_change.append(-packed_e)
    for ref, at, value in stores:
        ref[at, :] = value

    even = is_even("lon")
    even_lane = (iota((rows, lanes), 1) & 1) == 0

    def neighbours(at):
        a, b = got_a[at, :], got_b[at, :]
        return jnp.where(even, a, b), jnp.where(even, b, a)

    parts = [pl.ds(i * rows, rows) for i in range(3)]
    own_image, own_field, own_east = [own[p, :] for p in parts]
    columns = neighbours(parts[0])
    got_image, got_field = from_neighbours(*columns, even_lane), jnp.where(even_lane, *columns)
    got_east = from_neighbours(*neighbours(parts[1]), even_lane)
    before = own_image + row_change
    y = packed_twice[...] + row_inside
    c = face(own_east, got_east, even_lane)
    f = c * (got_field - own_field)
    e = -f
    after = before + e
    ring = got_image + f
    through = c * (ring - after)
    through_new = through_old = halves = jnp.zeros((rows, lanes), F32)
    for side in range(SIDES):
        here = row == (rows - 1) * side
        through_new = jnp.where(here, lat_coef[side] * (lat_ring[side] - after), through_new)
        through_old = jnp.where(here, lat_coef[side] * (lat_ring[side] - before), through_old)
        halves = jnp.where(here, lat_coef[side] * lat_ring[side] * f + c * ring * lat_change[side], halves)
    flux_down = down * (pltpu.roll(e, lanes - 2 * tracers, 1) - e)
    flux_north = north * (pltpu.roll(e, rows - 1, 0) - e)
    inside = (pltpu.roll(flux_down, 2 * tracers, 1) - flux_down) + (pltpu.roll(flux_north, 1, 0) - flux_north) + inner * e
    beside = -inner * e
    corrections[parts[0], :] = e
    corrections[parts[1], :] = inside - through - (through_new - through_old)
    corrections[parts[2], :] = beside
    edges = [(rows - 1) * side for side in range(SIDES)]
    corrections[pl.ds(3 * rows, 8), :] = stacked(lat_coef + [c[i : i + 1] for i in edges])

    column_dots = [folded(value) for value in (
        own_field * e,
        (before + after) * e,
        (2.0 * y + inside) * e - after * (through + through_new) + before * through_old + halves,
    )]
    tile_lane, tile_row = iota((8, lanes), 1), iota((8, lanes), 0)
    total = jnp.zeros((8, lanes), F32)
    for t in range(tracers):
        mine = lax.rem(tile_lane >> 1, tracers) == t
        for i in range(4):
            value = sums[pl.ds((4 * t + i) * 8, 8), :]
            if i:
                value = value + dots[t][i - 1] + jnp.where(mine, column_dots[i - 1], 0.0)
            total = jnp.where(tile_row == 4 * t + i, jnp.sum(value, axis=0, keepdims=True), total)
    total = jnp.sum(total, axis=1, keepdims=True)
    total = jnp.sum(jnp.where(tile_row == tile_lane, total, 0.0), axis=0, keepdims=True)
    even_row = (iota((1, lanes), 1) & 1) == 0
    south, north_ = edges
    lon_shares = [2.0 * c[i : i + 1] * part for i, part in zip(edges, lat_change)]
    shares = [total, 2.0 * lat_coef[1] * f[north_ : north_ + 1], jnp.where(even_row, lon_shares[0], lat_change[0]),
              jnp.where(even_row, lon_shares[1], f[south : south + 1])]
    for i, share in enumerate(shares):
        result[pl.ds(i, devices, SHARES), :] = jnp.broadcast_to(share, (devices, lanes))


def finish_kernel(tracers, nz, rows, devices, field, image, twice, corrections, sums, solution_out, residual_out,
                  solution, residual, sems):
    lanes = field.shape[1]
    across, along = lax.axis_size("lon"), lax.axis_size("lat")
    one = iota((1, lanes), 1)
    even_one = (one & 1) == 0
    total, to_north, lon_south, mixed = [sums[pl.ds(i, devices, SHARES), :] for i in range(SHARES)]
    total = jnp.sum(total, axis=0, keepdims=True)
    even_lane = (iota((devices, lanes), 1) & 1) == 0
    last = lax.rem(iota((devices, lanes), 0), across) == across - 1
    from_east = lambda x: pltpu.roll(jnp.where(last, pltpu.roll(x, across - 1, 0), pltpu.roll(x, devices - 1, 0)), lanes - 1, 1)
    from_north = lambda x: pltpu.roll(x, devices - across, 0)
    beyond = from_east(lon_south)
    cross = jnp.where(even_lane, lon_south * beyond - mixed * from_north(beyond), 0.0)
    cross = cross + to_north * from_north(jnp.where(even_lane, -from_east(mixed), mixed))
    cross = jnp.sum(cross, axis=0, keepdims=True)

    lon, lat = lax.axis_index("lon"), lax.axis_index("lat")
    tile_row = iota((8, lanes), 0)

    def share(i, j, at):
        first = SHARES * (j * across + i)
        tile = sums[pl.ds(pl.multiple_of(first // 8 * 8, 8), 8), :]
        return jnp.sum(jnp.where(tile_row == lax.rem(first, 8) + at, tile, 0.0), axis=0, keepdims=True)

    faces = corrections[pl.ds(3 * rows, 8), :]
    east, west = lax.rem(lon + 1, across), lax.rem(lon + across - 1, across)
    south, north = jnp.maximum(lat - 1, 0), jnp.minimum(lat + 1, along - 1)
    northern = jnp.where(lat < along - 1, 1.0, 0.0)
    lat_sides = (share(lon, south, 1) * jnp.where(lat > 0, 0.5, 0.0),
                 faces[1:2] * jnp.where(even_one, -pltpu.roll(share(east, north, 3), lanes - 1, 1), share(lon, north, 3)))
    lon_sides = (from_neighbours(share(east, lat, 2), 0.5 * share(west, lat, 2), even_one),
                 from_neighbours(-northern * share(east, north, 2), 0.5 * share(west, lat, 3), even_one))
    sides = [lat_sides[i] + jnp.where(even_one, faces[2 + i : 3 + i] * lon_sides[i], lon_sides[i]) for i in range(SIDES)]
    row = iota((rows, lanes), 0)
    e, change, beside = [corrections[pl.ds(i * rows, rows), :] for i in range(3)]
    change = change + jnp.where(row == 0, sides[0], jnp.where(row == rows - 1, sides[1], 0.0))

    lane = iota((CHUNK, rows, lanes), 2)
    narrow = iota((rows, lanes), 1)
    edge = (lane == 0) | (lane == lanes - 1)
    near = (lane <= 1) | (lane >= lanes - 2)

    def number(i):
        return jnp.sum(jnp.where(one == i, total, 0.0), axis=1, keepdims=True)

    copies, factors = [], []
    for t in range(tracers):
        bb, bw, ww, wy = [number(4 * t + i) for i in range(4)]
        mine = lax.rem(one >> 1, tracers) == t
        wy = wy - jnp.sum(jnp.where(mine, cross, 0.0), axis=1, keepdims=True)
        whole = 1.0 / (bb + bw)
        step = bb * whole
        rest = bw * whole
        beta = jnp.maximum(step * (ww * whole) - rest * rest, 0.0)
        new = beta * bb
        tau = beta + rest
        step_next = new / (new + beta * new + tau * tau * bw - 2.0 * tau * step * ww + step * step * wy)
        step_next = jnp.minimum(jnp.maximum(step_next, 0.0), 1.0)
        both = step * step_next
        factors.append((both, step + step_next * tau, rest - step_next * tau, both - step - step_next * tau))
    for t, (both, s_b, r_b, r_w) in enumerate(factors):
        s_edge = -both * e
        r_edge = jnp.where(lax.rem(narrow >> 1, tracers) == t, r_w * e + both * change,
                           both * jnp.where((narrow & 1) == 0, pltpu.roll(beside, 1, 1), pltpu.roll(beside, lanes - 1, 1)))
        for k in range(0, nz, CHUNK):
            slot, first = t * nz + k, k * tracers + t
            v, w, y = [levels_of(ref, slot, CHUNK, rows) for ref in (field, image, twice)]
            more = jnp.where(edge, unpacked(s_edge, first, tracers, CHUNK), 0.0)
            much = jnp.where(near, unpacked(r_edge, first, tracers, CHUNK), 0.0)
            put_levels(solution, slot, (s_b * v - both * w) + more)
            put_levels(residual, slot, (r_b * v + r_w * w + both * y) + much)
            at = pl.ds(slot * rows, CHUNK * rows)
            for a, b in ((solution, solution_out), (residual, residual_out)):
                copy = pltpu.make_async_copy(a.at[at], b.at[at], sems.at[len(copies)])
                copy.start()
                copies.append(copy)
    for copy in copies:
        copy.wait()


def swapped(x, axis, second):
    devices = lax.axis_size(axis)
    forward = [(i % 2 == 0) != second for i in range(devices)]
    return lax.ppermute(x, axis, [(i, (i + 1 if forward[i] else i - 1) % devices) for i in range(devices)])


def body(right_side, sea_mask, levels, east_diffusivity, north_diffusivity, vertical_diffusivity):
    tracers, nz, rows, lanes = right_side.shape
    devices = lax.axis_size("lon") * lax.axis_size("lat")
    flat = lambda x: x.reshape(-1, lanes)
    outside = lambda x: pltpu.with_memory_space_constraint(flat(x), pltpu.HBM)
    n = nz * rows
    cells = tracers * n * lanes

    def call(kernel, outs, flops, space=pltpu.VMEM, **more):
        outs = [m if isinstance(m, tuple) else (m, F32) for m in outs]
        cost = pl.CostEstimate(flops=flops, bytes_accessed=4 * lanes * sum(m for m, _ in outs), transcendentals=0)
        return pl.pallas_call(
            functools.partial(kernel, tracers, nz, rows),
            out_shape=[space((m, lanes), dtype) for m, dtype in outs],
            compiler_params=pltpu.CompilerParams(vmem_limit_bytes=32 * 1024 * 1024),
            cost_estimate=cost,
            **more,
        )

    def with_devices(kernel):
        return lambda tracers, nz, rows, *refs: kernel(tracers, nz, rows, devices, *refs)

    scratch = lambda m, dtype: pltpu.VMEM((m, lanes), dtype)
    *inputs, own, message, packed = call(
        columns_kernel,
        [tracers * n, (n, jnp.int32), (rows, jnp.int32)] + [(n, jnp.bfloat16)] * 3 + [3 * rows, 2 * rows, 3 * rows],
        20 * cells,
        in_specs=[pl.BlockSpec(memory_space=pltpu.HBM)] * 6,
        scratch_shapes=[pltpu.SemaphoreType.DMA((6,))],
        name="columns",
    )(*map(outside, (right_side, sea_mask, levels, east_diffusivity, north_diffusivity, vertical_diffusivity)))
    field = inputs[0]
    got_b = swapped(message, "lon", True)
    coef_east, coef_west, coef_north, coef_south, coef_down, east_own, north_own, image, rows_b = call(
        block_kernel, [n] * 7 + [tracers * n, FIELDS * nz], 20 * cells, name="block")(*inputs)
    got_rows_b = swapped(rows_b, "lat", True)
    coefs = (coef_east, coef_west, coef_north, coef_south, coef_down)
    rows_a, message_a = call(later_kernel, [FIELDS * nz, 2 * rows], cells, name="later")(
        field, image, east_own, north_own, own, rows_b)
    twice, packed_twice, sums = call(
        interior_kernel, [tracers * n, rows, 8 * 4 * tracers], 60000 * cells, name="interior"
    )(field, image, *coefs)
    got_a = swapped(message_a, "lon", False)
    got_rows_a = swapped(rows_a, "lat", False)
    image, twice, corrections, sums = call(
        with_devices(sums_kernel), [tracers * n, tracers * n, 3 * rows + 8, SHARES * devices], cells,
        input_output_aliases={0: 0, 1: 1}, name="sums",
    )(image, twice, coef_east, coef_north, coef_down, rows_a, rows_b, got_rows_a, got_rows_b, own, got_a, got_b, packed, packed_twice, sums)
    sums = lax.all_to_all(sums.reshape(devices, 1, -1), ("lat", "lon"), 0, 0, tiled=True).reshape(-1, lanes)
    copies = 2 * tracers * nz // CHUNK
    solution_field, residual = call(
        with_devices(finish_kernel), [tracers * n] * 2, 20 * cells, space=jax.ShapeDtypeStruct,
        out_specs=[pl.BlockSpec(memory_space=pltpu.HBM)] * 2,
        scratch_shapes=[scratch(tracers * n, F32)] * 2 + [pltpu.SemaphoreType.DMA((copies,))],
        name="finish",
    )(field, image, twice, corrections, sums)
    return solution_field.reshape(right_side.shape), residual.reshape(right_side.shape)


def solution(mesh):
    return jax.shard_map(
        body,
        mesh=mesh,
        in_specs=(
            P(None, None, "lat", "lon"),
            P(None, "lat", "lon"),
            P("lat", "lon"),
            P(None, "lat", "lon"),
            P(None, "lat", "lon"),
            P(None, "lat", "lon"),
        ),
        out_specs=(P(None, None, "lat", "lon"), P(None, None, "lat", "lon")),
        check_vma=False,
    )
```

```python
import functools

import jax
import jax.numpy as jnp
from jax import lax
from jax.experimental import pallas as pl
from jax.experimental.pallas import tpu as pltpu
from jax.sharding import PartitionSpec as P

F32 = jnp.float32
CHUNK = 8
SHARES = 4
SIDES = 2
FIELDS = 5


def iota(shape, axis):
    return lax.broadcasted_iota(jnp.int32, shape, axis)


def is_even(axis):
    return (lax.axis_index(axis) & 1) == 0


def levels_of(ref, first, count, rows):
    return ref[pl.ds(first * rows, count * rows), :].reshape(count, rows, ref.shape[1])


def put_levels(ref, first, value):
    count, rows, lanes = value.shape
    ref[pl.ds(first * rows, count * rows), :] = value.reshape(count * rows, lanes)


def laplacian(value, below, flux_above, coefs):
    _, rows, lanes = value.shape
    east, west, north, south, down = coefs
    change = east * (value - pltpu.roll(value, lanes - 1, 2)) + west * (value - pltpu.roll(value, 1, 2))
    change = change + (north * (value - pltpu.roll(value, rows - 1, 1)) + south * (value - pltpu.roll(value, 1, 1)))
    flux_down = down * (jnp.concatenate([value[1:], below], axis=0) - value)
    from_above = jnp.concatenate([flux_above, flux_down[:-1]], axis=0)
    return change + (from_above - flux_down), flux_down[-1:]


def packed_into(total, planes, first, step, pair):
    slots = [first + step * i for i in range(planes.shape[0])]
    moved = [pltpu.roll(planes[i], 2 * slot + 1, 1) for i, slot in enumerate(slots)]
    for slot, plane in zip(slots, moved):
        total = jnp.where(pair == slot, plane, total)
    return total


def unpacked(packed, first, step, count, offset=1):
    lanes = packed.shape[1]
    return jnp.stack([pltpu.roll(packed, (2 * lanes - offset - 2 * (first + step * i)) % lanes, 1) for i in range(count)])


def spread(plane, t, tracers, pair, level):
    moved = pltpu.roll(plane, 2 * t + 1, 1, stride=2 * tracers, stride_axis=0)
    return jnp.sum(jnp.where(pair == level * tracers + t, moved, 0.0), axis=0, keepdims=True)


def fours_into(total, planes, first, four):
    moved = [pltpu.roll(planes[i], 4 * (first + i) + 2, 1) for i in range(planes.shape[0])]
    for i, plane in enumerate(moved):
        total = jnp.where(four == first + i, plane, total)
    return total


def pairs_of(fours, lane):
    lanes = lane.shape[1]
    return jnp.where((lane & 2) == 0, pltpu.roll(fours[0], lanes - 1, 1), pltpu.roll(fours[1], 1, 1))


def from_neighbours(east, west, even_lane):
    return jnp.where(even_lane, pltpu.roll(east, east.shape[1] - 1, 1), pltpu.roll(west, 1, 1))


def face(own, other, even_lane):
    return jnp.where(even_lane, own * (other > 0).astype(F32), other * (own > 0).astype(F32))


def columns_kernel(tracers, nz, rows, field_in, mask_in, levels_in, east_in, north_in, down_in,
                   field, mask, levels, east, north, down, own, message, packed, sems):
    pairs = ((levels_in, levels), (mask_in, mask), (field_in, field), (east_in, east), (north_in, north), (down_in, down))
    copies = [pltpu.make_async_copy(a, b, sems.at[i]) for i, (a, b) in enumerate(pairs)]
    for copy in copies:
        copy.start()
    lanes = field.shape[1]
    lane, row = iota((rows, lanes), 1), iota((rows, lanes), 0)
    four, place = lane >> 2, lane & 3
    zero = jnp.zeros((rows, lanes), F32)
    chunk = nz // 2

    def fours_of(ref, start=0, see=lambda value, k: value.astype(F32)):
        total = zero
        for k in range(0, nz, chunk):
            total = fours_into(total, see(levels_of(ref, start + k, chunk, rows), k), k, four)
        return total

    for copy in copies[:3]:
        copy.wait()
    depth = levels[...]
    level = iota((chunk, rows, lanes), 0)
    wet = fours_of(mask, see=lambda value, k: jnp.where((value == 1) & (level + k < depth[None]), 1.0, 0.0))
    fields = [fours_of(field, t * nz) for t in range(tracers)]
    for copy in copies[3:]:
        copy.wait()
    wide_east, wide_north, wide_down = fours_of(east), fours_of(north), fours_of(down)
    own_east = wide_east * wet
    inner = own_east * pltpu.roll(wet, lanes - 1, 1)
    inner = jnp.where(place == 1, pltpu.roll(inner, 1, 1), inner)
    c_north = jnp.where(row == rows - 1, 0.0, wide_north * wet * pltpu.roll(wet, rows - 1, 0))
    c_south = pltpu.roll(c_north, 1, 0)
    c_down = jnp.where(four == nz - 1, 0.0, wide_down * wet * pltpu.roll(wet, lanes - 4, 1))
    images = []
    for v in fields:
        beside = jnp.where(place == 1, pltpu.roll(v, 1, 1), pltpu.roll(v, lanes - 1, 1))
        flux_down = c_down * (pltpu.roll(v, lanes - 4, 1) - v)
        change = inner * (v - beside) + c_north * (v - pltpu.roll(v, rows - 1, 0)) + c_south * (v - pltpu.roll(v, 1, 0))
        images.append(change + (pltpu.roll(flux_down, 4, 1) - flux_down))
    for i, parts in enumerate((images, fields, (own_east, own_east))):
        own[pl.ds(i * rows, rows), :] = pairs_of(parts, lane)
    put_message(rows, own, message, True)
    for i, part in enumerate((c_north, c_down, inner)):
        packed[pl.ds(i * rows, rows), :] = pairs_of((part, part), lane)


def block_kernel(tracers, nz, rows, field, mask, levels, east, north, down,
                 coef_east, coef_west, coef_north, coef_south, coef_down, east_own, north_own, image, rows_b):
    lanes = field.shape[1]
    chunk = nz // 2
    shape = (1, rows, lanes)
    last_lane, last_row = iota(shape, 2) == lanes - 1, iota(shape, 1) == rows - 1
    first_lane, first_row = iota(shape, 2) == 0, iota(shape, 1) == 0
    zero = jnp.zeros((rows, lanes), F32)
    depth = levels[...]
    level = iota((chunk + 1, rows, lanes), 0)
    above = [zero[None]] * tracers
    for k in range(0, nz, chunk):
        count = min(chunk + 1, nz - k)
        wet = (levels_of(mask, k, count, rows) == 1) & (level[:count] + k < depth[None])
        wet = jnp.where(wet, 1.0, 0.0)
        if count == chunk:
            wet = jnp.concatenate([wet, zero[None]], axis=0)
        ocean = wet[:chunk]
        own_east = levels_of(east, k, chunk, rows).astype(F32) * ocean
        own_north = levels_of(north, k, chunk, rows).astype(F32) * ocean
        c_east = jnp.where(last_lane, 0.0, own_east * pltpu.roll(ocean, lanes - 1, 2))
        c_north = jnp.where(last_row, 0.0, own_north * pltpu.roll(ocean, rows - 1, 1))
        c_down = levels_of(down, k, chunk, rows).astype(F32) * ocean * wet[1:]
        c_west = jnp.where(first_lane, 0.0, pltpu.roll(own_east, 1, 2) * ocean)
        c_south = jnp.where(first_row, 0.0, pltpu.roll(own_north, 1, 1) * ocean)
        c = (c_east, c_west, c_north, c_south, c_down)
        changes = []
        for t in range(tracers):
            value = levels_of(field, t * nz + k, chunk, rows)
            below = levels_of(field, t * nz + k + chunk, 1, rows) if k + chunk < nz else zero[None]
            change, above[t] = laplacian(value, below, above[t], c)
            changes.append(change)
        for ref, value in zip((coef_east, coef_west, coef_north, coef_south, coef_down, east_own, north_own), c + (own_east, own_north)):
            put_levels(ref, k, value)
        for t in range(tracers):
            put_levels(image, t * nz + k, changes[t])
    edge_rows(tracers, nz, rows, field, image, east_own, north_own, True, rows_b)


def put_message(rows, own, message, second):
    lanes = own.shape[1]
    eastern = is_even("lon") != second
    even_lane = (iota((rows, lanes), 1) & 1) == 0
    image, field = own[pl.ds(0, rows), :], own[pl.ds(rows, rows), :]
    to_east = jnp.where(even_lane, image, pltpu.roll(field, 1, 1))
    to_west = jnp.where(even_lane, pltpu.roll(field, lanes - 1, 1), image)
    message[pl.ds(0, rows), :] = jnp.where(eastern, to_east, to_west)
    message[pl.ds(rows, rows), :] = own[pl.ds(2 * rows, rows), :]


def edge_rows(tracers, nz, rows, field, image, east_own, north_own, second, out):
    southern = is_even("lat") if second else jnp.logical_not(is_even("lat"))

    def edge(side):
        first = (rows - 1) * side
        parts = [ref[pl.ds(first + t * nz * rows, nz, rows), :] for ref in (image, field) for t in range(tracers)]
        return parts + [(east_own, north_own)[side][pl.ds(first, nz, rows), :]]

    for at, (south, north_) in enumerate(zip(edge(0), edge(1))):
        out[pl.ds(at * nz, nz), :] = jnp.where(southern, south, north_)


def later_kernel(tracers, nz, rows, field, image, east_own, north_own, own, rows_b, rows_a, message_a):
    edge_rows(tracers, nz, rows, field, image, east_own, north_own, False, rows_a)
    put_message(rows, own, message_a, False)


def stacked(parts):
    lanes = parts[0].shape[1]
    row = iota((8, lanes), 0)
    total = jnp.zeros((8, lanes), F32)
    for i, part in enumerate(parts):
        total = jnp.where(row == i, part, total)
    return total


def folded(x):
    return sum(x[i : i + 8] for i in range(0, x.shape[0], 8))


def interior_kernel(tracers, nz, rows, field, image, coef_east, coef_west, coef_north, coef_south, coef_down,
                    twice, packed, sums):
    lanes = field.shape[1]
    pair = iota((rows, lanes), 1) >> 1
    zero = packed_twice = jnp.zeros((rows, lanes), F32)
    totals = [[zero] * 4 for _ in range(tracers)]
    above = [zero[None]] * tracers
    for k in range(0, nz, CHUNK):
        refs = (coef_east, coef_west, coef_north, coef_south, coef_down)
        c = [levels_of(ref, k, CHUNK, rows) for ref in refs]
        results = []
        for t in range(tracers):
            w = levels_of(image, t * nz + k, CHUNK, rows)
            below = levels_of(image, t * nz + k + CHUNK, 1, rows) if k + CHUNK < nz else zero[None]
            y, above[t] = laplacian(w, below, above[t], c)
            results.append(y)
            v = levels_of(field, t * nz + k, CHUNK, rows)
            for i, product in enumerate((v * v, v * w, w * w, w * y)):
                totals[t][i] = totals[t][i] + jnp.sum(product, axis=0)
        for t in range(tracers):
            packed_twice = packed_into(packed_twice, results[t], k * tracers + t, tracers, pair)
        for t in range(tracers):
            put_levels(twice, t * nz + k, results[t])
    packed[...] = packed_twice
    for t in range(tracers):
        for i in range(4):
            sums[pl.ds((4 * t + i) * 8, 8), :] = folded(totals[t][i])


def sums_kernel(tracers, nz, rows, devices, image_in, twice_in, coef_east, coef_north, coef_down, rows_a, rows_b, got_rows_a,
                got_rows_b, own, got_a, got_b, packed, packed_twice, sums, image, twice, corrections, result):
    lanes = own.shape[1]
    even = is_even("lat")
    pair, level = iota((nz, lanes), 1) >> 1, iota((nz, lanes), 0)
    row = iota((rows, lanes), 0)
    north, down, inner = [packed[pl.ds(i * rows, rows), :] for i in range(3)]
    dots = [[jnp.zeros((8, lanes), F32) for _ in range(3)] for _ in range(tracers)]
    nothing = jnp.zeros((1, lanes), F32)
    row_change, row_inside = jnp.zeros((rows, lanes), F32), jnp.zeros((rows, lanes), F32)
    lat_coef, lat_ring, lat_change = [], [], []
    stores = []
    for side in range(SIDES):
        def part(at, a, b):
            first, second = (b, a) if side == 0 else (a, b)
            return jnp.where(even, first[pl.ds(at * nz, nz), :], second[pl.ds(at * nz, nz), :])

        own_row = lambda at: part(at, rows_a, rows_b)
        got_row = lambda at: part(at, got_rows_a, got_rows_b)
        own_coef, got_coef = own_row(2 * tracers), got_row(2 * tracers)
        c = got_coef * (own_coef > 0).astype(F32) if side == 0 else own_coef * (got_coef > 0).astype(F32)
        c = c * jnp.where(lax.axis_index("lat") == (0, lax.axis_size("lat") - 1)[side], 0.0, 1.0)
        first, next_row, between = ((0, 1, 0), (rows - 1, rows - 2, rows - 2))[side]
        c_east, c_down = coef_east[pl.ds(first, nz, rows), :], coef_down[pl.ds(first, nz, rows), :]
        c_inner = coef_north[pl.ds(between, nz, rows), :]
        packed_ring, packed_e, packed_inside = [nothing] * 3
        packed_coef = spread(c, 0, tracers, pair, level)
        packed_coef = sum((pltpu.roll(packed_coef, 2 * t, 1) for t in range(1, tracers)), packed_coef)
        for t in range(tracers):
            b, w = own_row(tracers + t), own_row(t)
            f = c * (got_row(tracers + t) - b)
            e = -f
            ring = got_row(t) + f
            flux_east = c_east * (pltpu.roll(e, lanes - 1, 1) - e)
            flux_down = c_down * (pltpu.roll(e, nz - 1, 0) - e)
            inside = (pltpu.roll(flux_east, 1, 1) - flux_east) + (pltpu.roll(flux_down, 1, 0) - flux_down) + c_inner * e
            changed = w + e
            through = c * (ring - changed)
            at = pl.ds(first + t * nz * rows, nz, rows)
            at_next = pl.ds(next_row + t * nz * rows, nz, rows)
            y = twice_in[at, :]
            stores.append((image, at, changed))
            stores.append((twice, at, y + inside - through))
            stores.append((twice, at_next, twice_in[at_next, :] - c_inner * e))
            for i, value in enumerate((b * e, (w + changed) * e, (2.0 * y + inside) * e - changed * through)):
                dots[t][i] = dots[t][i] + folded(value)
            packed_ring = packed_ring + spread(ring, t, tracers, pair, level)
            packed_e = packed_e + spread(e, t, tracers, pair, level)
            packed_inside = packed_inside + spread(inside, t, tracers, pair, level)
        row_change = jnp.where(row == first, packed_e, row_change)
        row_inside = jnp.where(row == first, packed_inside, row_inside)
        row_inside = jnp.where(row == next_row, -north[between : between + 1] * packed_e, row_inside)
        lat_coef.append(packed_coef)
        lat_ring.append(packed_ring)
        lat_change.append(-packed_e)
    for ref, at, value in stores:
        ref[at, :] = value

    even = is_even("lon")
    even_lane = (iota((rows, lanes), 1) & 1) == 0

    def neighbours(at):
        a, b = got_a[at, :], got_b[at, :]
        return jnp.where(even, a, b), jnp.where(even, b, a)

    parts = [pl.ds(i * rows, rows) for i in range(3)]
    own_image, own_field, own_east = [own[p, :] for p in parts]
    columns = neighbours(parts[0])
    got_image, got_field = from_neighbours(*columns, even_lane), jnp.where(even_lane, *columns)
    got_east = from_neighbours(*neighbours(parts[1]), even_lane)
    before = own_image + row_change
    y = packed_twice[...] + row_inside
    c = face(own_east, got_east, even_lane)
    f = c * (got_field - own_field)
    e = -f
    after = before + e
    ring = got_image + f
    through = c * (ring - after)
    through_new = through_old = halves = jnp.zeros((rows, lanes), F32)
    for side in range(SIDES):
        here = row == (rows - 1) * side
        through_new = jnp.where(here, lat_coef[side] * (lat_ring[side] - after), through_new)
        through_old = jnp.where(here, lat_coef[side] * (lat_ring[side] - before), through_old)
        halves = jnp.where(here, lat_coef[side] * lat_ring[side] * f + c * ring * lat_change[side], halves)
    flux_down = down * (pltpu.roll(e, lanes - 2 * tracers, 1) - e)
    flux_north = north * (pltpu.roll(e, rows - 1, 0) - e)
    inside = (pltpu.roll(flux_down, 2 * tracers, 1) - flux_down) + (pltpu.roll(flux_north, 1, 0) - flux_north) + inner * e
    beside = -inner * e
    corrections[parts[0], :] = e
    corrections[parts[1], :] = inside - through - (through_new - through_old)
    corrections[parts[2], :] = beside
    edges = [(rows - 1) * side for side in range(SIDES)]
    corrections[pl.ds(3 * rows, 8), :] = stacked(lat_coef + [c[i : i + 1] for i in edges])

    column_dots = [folded(value) for value in (
        own_field * e,
        (before + after) * e,
        (2.0 * y + inside) * e - after * (through + through_new) + before * through_old + halves,
    )]
    tile_lane, tile_row = iota((8, lanes), 1), iota((8, lanes), 0)
    total = jnp.zeros((8, lanes), F32)
    for t in range(tracers):
        mine = lax.rem(tile_lane >> 1, tracers) == t
        for i in range(4):
            value = sums[pl.ds((4 * t + i) * 8, 8), :]
            if i:
                value = value + dots[t][i - 1] + jnp.where(mine, column_dots[i - 1], 0.0)
            total = jnp.where(tile_row == 4 * t + i, jnp.sum(value, axis=0, keepdims=True), total)
    total = jnp.sum(total, axis=1, keepdims=True)
    total = jnp.sum(jnp.where(tile_row == tile_lane, total, 0.0), axis=0, keepdims=True)
    even_row = (iota((1, lanes), 1) & 1) == 0
    south, north_ = edges
    lon_shares = [2.0 * c[i : i + 1] * part for i, part in zip(edges, lat_change)]
    shares = [total, 2.0 * lat_coef[1] * f[north_ : north_ + 1], jnp.where(even_row, lon_shares[0], lat_change[0]),
              jnp.where(even_row, lon_shares[1], f[south : south + 1])]
    for i, share in enumerate(shares):
        result[pl.ds(i, devices, SHARES), :] = jnp.broadcast_to(share, (devices, lanes))


def finish_kernel(tracers, nz, rows, devices, field, image, twice, corrections, sums, solution_out, residual_out,
                  solution, residual, sems):
    lanes = field.shape[1]
    across, along = lax.axis_size("lon"), lax.axis_size("lat")
    one = iota((1, lanes), 1)
    even_one = (one & 1) == 0
    total, to_north, lon_south, mixed = [sums[pl.ds(i, devices, SHARES), :] for i in range(SHARES)]
    total = jnp.sum(total, axis=0, keepdims=True)
    even_lane = (iota((devices, lanes), 1) & 1) == 0
    last = lax.rem(iota((devices, lanes), 0), across) == across - 1
    from_east = lambda x: pltpu.roll(jnp.where(last, pltpu.roll(x, across - 1, 0), pltpu.roll(x, devices - 1, 0)), lanes - 1, 1)
    from_north = lambda x: pltpu.roll(x, devices - across, 0)
    beyond = from_east(lon_south)
    cross = jnp.where(even_lane, lon_south * beyond - mixed * from_north(beyond), 0.0)
    cross = cross + to_north * from_north(jnp.where(even_lane, -from_east(mixed), mixed))
    cross = jnp.sum(cross, axis=0, keepdims=True)

    lon, lat = lax.axis_index("lon"), lax.axis_index("lat")
    tile_row = iota((8, lanes), 0)

    def share(i, j, at):
        first = SHARES * (j * across + i)
        tile = sums[pl.ds(pl.multiple_of(first // 8 * 8, 8), 8), :]
        return jnp.sum(jnp.where(tile_row == lax.rem(first, 8) + at, tile, 0.0), axis=0, keepdims=True)

    faces = corrections[pl.ds(3 * rows, 8), :]
    east, west = lax.rem(lon + 1, across), lax.rem(lon + across - 1, across)
    south, north = jnp.maximum(lat - 1, 0), jnp.minimum(lat + 1, along - 1)
    northern = jnp.where(lat < along - 1, 1.0, 0.0)
    lat_sides = (share(lon, south, 1) * jnp.where(lat > 0, 0.5, 0.0),
                 faces[1:2] * jnp.where(even_one, -pltpu.roll(share(east, north, 3), lanes - 1, 1), share(lon, north, 3)))
    lon_sides = (from_neighbours(share(east, lat, 2), 0.5 * share(west, lat, 2), even_one),
                 from_neighbours(-northern * share(east, north, 2), 0.5 * share(west, lat, 3), even_one))
    sides = [lat_sides[i] + jnp.where(even_one, faces[2 + i : 3 + i] * lon_sides[i], lon_sides[i]) for i in range(SIDES)]
    row = iota((rows, lanes), 0)
    e, change, beside = [corrections[pl.ds(i * rows, rows), :] for i in range(3)]
    change = change + jnp.where(row == 0, sides[0], jnp.where(row == rows - 1, sides[1], 0.0))

    lane = iota((CHUNK, rows, lanes), 2)
    narrow = iota((rows, lanes), 1)
    edge = (lane == 0) | (lane == lanes - 1)
    near = (lane <= 1) | (lane >= lanes - 2)

    def number(i):
        return jnp.sum(jnp.where(one == i, total, 0.0), axis=1, keepdims=True)

    copies, factors = [], []
    for t in range(tracers):
        bb, bw, ww, wy = [number(4 * t + i) for i in range(4)]
        mine = lax.rem(one >> 1, tracers) == t
        wy = wy - jnp.sum(jnp.where(mine, cross, 0.0), axis=1, keepdims=True)
        whole = 1.0 / (bb + bw)
        step = bb * whole
        rest = bw * whole
        beta = jnp.maximum(step * (ww * whole) - rest * rest, 0.0)
        new = beta * bb
        tau = beta + rest
        step_next = new / (new + beta * new + tau * tau * bw - 2.0 * tau * step * ww + step * step * wy)
        step_next = jnp.minimum(jnp.maximum(step_next, 0.0), 1.0)
        both = step * step_next
        factors.append((both, step + step_next * tau, rest - step_next * tau, both - step - step_next * tau))
    for t, (both, s_b, r_b, r_w) in enumerate(factors):
        s_edge = -both * e
        r_edge = jnp.where(lax.rem(narrow >> 1, tracers) == t, r_w * e + both * change,
                           both * jnp.where((narrow & 1) == 0, pltpu.roll(beside, 1, 1), pltpu.roll(beside, lanes - 1, 1)))
        for k in range(0, nz, CHUNK):
            slot, first = t * nz + k, k * tracers + t
            v, w, y = [levels_of(ref, slot, CHUNK, rows) for ref in (field, image, twice)]
            more = jnp.where(edge, unpacked(s_edge, first, tracers, CHUNK), 0.0)
            much = jnp.where(near, unpacked(r_edge, first, tracers, CHUNK), 0.0)
            put_levels(solution, slot, (s_b * v - both * w) + more)
            put_levels(residual, slot, (r_b * v + r_w * w + both * y) + much)
            at = pl.ds(slot * rows, CHUNK * rows)
            for a, b in ((solution, solution_out), (residual, residual_out)):
                copy = pltpu.make_async_copy(a.at[at], b.at[at], sems.at[len(copies)])
                copy.start()
                copies.append(copy)
    for copy in copies:
        copy.wait()


def swapped(x, axis, second):
    devices = lax.axis_size(axis)
    forward = [(i % 2 == 0) != second for i in range(devices)]
    return lax.ppermute(x, axis, [(i, (i + 1 if forward[i] else i - 1) % devices) for i in range(devices)])


def body(right_side, sea_mask, levels, east_diffusivity, north_diffusivity, vertical_diffusivity):
    tracers, nz, rows, lanes = right_side.shape
    devices = lax.axis_size("lon") * lax.axis_size("lat")
    flat = lambda x: x.reshape(-1, lanes)
    outside = lambda x: pltpu.with_memory_space_constraint(flat(x), pltpu.HBM)
    n = nz * rows
    cells = tracers * n * lanes

    def call(kernel, outs, flops, space=pltpu.VMEM, **more):
        outs = [m if isinstance(m, tuple) else (m, F32) for m in outs]
        cost = pl.CostEstimate(flops=flops, bytes_accessed=4 * lanes * sum(m for m, _ in outs), transcendentals=0)
        return pl.pallas_call(
            functools.partial(kernel, tracers, nz, rows),
            out_shape=[space((m, lanes), dtype) for m, dtype in outs],
            compiler_params=pltpu.CompilerParams(vmem_limit_bytes=32 * 1024 * 1024),
            cost_estimate=cost,
            **more,
        )

    def with_devices(kernel):
        return lambda tracers, nz, rows, *refs: kernel(tracers, nz, rows, devices, *refs)

    scratch = lambda m, dtype: pltpu.VMEM((m, lanes), dtype)
    *inputs, own, message, packed = call(
        columns_kernel,
        [tracers * n, (n, jnp.int32), (rows, jnp.int32)] + [(n, jnp.bfloat16)] * 3 + [3 * rows, 2 * rows, 3 * rows],
        20 * cells,
        in_specs=[pl.BlockSpec(memory_space=pltpu.HBM)] * 6,
        scratch_shapes=[pltpu.SemaphoreType.DMA((6,))],
        name="columns",
    )(*map(outside, (right_side, sea_mask, levels, east_diffusivity, north_diffusivity, vertical_diffusivity)))
    field = inputs[0]
    got_b = swapped(message, "lon", True)
    coef_east, coef_west, coef_north, coef_south, coef_down, east_own, north_own, image, rows_b = call(
        block_kernel, [n] * 7 + [tracers * n, FIELDS * nz], 20 * cells, name="block")(*inputs)
    got_rows_b = swapped(rows_b, "lat", True)
    coefs = (coef_east, coef_west, coef_north, coef_south, coef_down)
    rows_a, message_a = call(later_kernel, [FIELDS * nz, 2 * rows], cells, name="later")(
        field, image, east_own, north_own, own, rows_b)
    twice, packed_twice, sums = call(
        interior_kernel, [tracers * n, rows, 8 * 4 * tracers], 60000 * cells, name="interior"
    )(field, image, *coefs)
    got_a = swapped(message_a, "lon", False)
    got_rows_a = swapped(rows_a, "lat", False)
    image, twice, corrections, sums = call(
        with_devices(sums_kernel), [tracers * n, tracers * n, 3 * rows + 8, SHARES * devices], cells,
        input_output_aliases={0: 0, 1: 1}, name="sums",
    )(image, twice, coef_east, coef_north, coef_down, rows_a, rows_b, got_rows_a, got_rows_b, own, got_a, got_b, packed, packed_twice, sums)
    sums = lax.all_to_all(sums.reshape(devices, 1, -1), ("lat", "lon"), 0, 0, tiled=True).reshape(-1, lanes)
    copies = 2 * tracers * nz // CHUNK
    solution_field, residual = call(
        with_devices(finish_kernel), [tracers * n] * 2, 20 * cells, space=jax.ShapeDtypeStruct,
        out_specs=[pl.BlockSpec(memory_space=pltpu.HBM)] * 2,
        scratch_shapes=[scratch(tracers * n, F32)] * 2 + [pltpu.SemaphoreType.DMA((copies,))],
        name="finish",
    )(field, image, twice, corrections, sums)
    return solution_field.reshape(right_side.shape), residual.reshape(right_side.shape)


def solution(mesh):
    return jax.shard_map(
        body,
        mesh=mesh,
        in_specs=(
            P(None, None, "lat", "lon"),
            P(None, "lat", "lon"),
            P("lat", "lon"),
            P(None, "lat", "lon"),
            P(None, "lat", "lon"),
            P(None, "lat", "lon"),
        ),
        out_specs=(P(None, None, "lat", "lon"), P(None, None, "lat", "lon")),
        check_vma=False,
    )
```

```python
import functools

import jax
import jax.numpy as jnp
from jax import lax
from jax.experimental import pallas as pl
from jax.experimental.pallas import tpu as pltpu
from jax.sharding import PartitionSpec as P

F32 = jnp.float32
CHUNK = 8
SHARES = 4
SIDES = 2
FIELDS = 5


def iota(shape, axis):
    return lax.broadcasted_iota(jnp.int32, shape, axis)


def is_even(axis):
    return (lax.axis_index(axis) & 1) == 0


def levels_of(ref, first, count, rows):
    return ref[pl.ds(first * rows, count * rows), :].reshape(count, rows, ref.shape[1])


def put_levels(ref, first, value):
    count, rows, lanes = value.shape
    ref[pl.ds(first * rows, count * rows), :] = value.reshape(count * rows, lanes)


def laplacian(value, below, flux_above, coefs):
    _, rows, lanes = value.shape
    east, west, north, south, down = coefs
    change = east * (value - pltpu.roll(value, lanes - 1, 2)) + west * (value - pltpu.roll(value, 1, 2))
    change = change + (north * (value - pltpu.roll(value, rows - 1, 1)) + south * (value - pltpu.roll(value, 1, 1)))
    flux_down = down * (jnp.concatenate([value[1:], below], axis=0) - value)
    from_above = jnp.concatenate([flux_above, flux_down[:-1]], axis=0)
    return change + (from_above - flux_down), flux_down[-1:]


def packed_into(total, planes, first, step, pair):
    slots = [first + step * i for i in range(planes.shape[0])]
    moved = [pltpu.roll(planes[i], 2 * slot + 1, 1) for i, slot in enumerate(slots)]
    for slot, plane in zip(slots, moved):
        total = jnp.where(pair == slot, plane, total)
    return total


def unpacked(packed, first, step, count, offset=1):
    lanes = packed.shape[1]
    return jnp.stack([pltpu.roll(packed, (2 * lanes - offset - 2 * (first + step * i)) % lanes, 1) for i in range(count)])


def spread(plane, t, tracers, pair, level):
    moved = pltpu.roll(plane, 2 * t + 1, 1, stride=2 * tracers, stride_axis=0)
    return jnp.sum(jnp.where(pair == level * tracers + t, moved, 0.0), axis=0, keepdims=True)


def fours_into(total, planes, first, four):
    moved = [pltpu.roll(planes[i], 4 * (first + i) + 2, 1) for i in range(planes.shape[0])]
    for i, plane in enumerate(moved):
        total = jnp.where(four == first + i, plane, total)
    return total


def pairs_of(fours, lane):
    lanes = lane.shape[1]
    return jnp.where((lane & 2) == 0, pltpu.roll(fours[0], lanes - 1, 1), pltpu.roll(fours[1], 1, 1))


def from_neighbours(east, west, even_lane):
    return jnp.where(even_lane, pltpu.roll(east, east.shape[1] - 1, 1), pltpu.roll(west, 1, 1))


def face(own, other, even_lane):
    return jnp.where(even_lane, own * (other > 0).astype(F32), other * (own > 0).astype(F32))


def columns_kernel(tracers, nz, rows, field_in, mask_in, levels_in, east_in, north_in, down_in,
                   field, mask, levels, east, north, down, own, message, packed, sems):
    pairs = ((levels_in, levels), (mask_in, mask), (field_in, field), (east_in, east), (north_in, north), (down_in, down))
    copies = [pltpu.make_async_copy(a, b, sems.at[i]) for i, (a, b) in enumerate(pairs)]
    for copy in copies:
        copy.start()
    lanes = field.shape[1]
    lane, row = iota((rows, lanes), 1), iota((rows, lanes), 0)
    four, place = lane >> 2, lane & 3
    zero = jnp.zeros((rows, lanes), F32)
    chunk = nz // 2

    def fours_of(ref, start=0, see=lambda value, k: value.astype(F32)):
        total = zero
        for k in range(0, nz, chunk):
            total = fours_into(total, see(levels_of(ref, start + k, chunk, rows), k), k, four)
        return total

    for copy in copies[:3]:
        copy.wait()
    depth = levels[...]
    level = iota((chunk, rows, lanes), 0)
    wet = fours_of(mask, see=lambda value, k: jnp.where((value == 1) & (level + k < depth[None]), 1.0, 0.0))
    fields = [fours_of(field, t * nz) for t in range(tracers)]
    for copy in copies[3:]:
        copy.wait()
    wide_east, wide_north, wide_down = fours_of(east), fours_of(north), fours_of(down)
    own_east = wide_east * wet
    inner = own_east * pltpu.roll(wet, lanes - 1, 1)
    inner = jnp.where(place == 1, pltpu.roll(inner, 1, 1), inner)
    c_north = jnp.where(row == rows - 1, 0.0, wide_north * wet * pltpu.roll(wet, rows - 1, 0))
    c_south = pltpu.roll(c_north, 1, 0)
    c_down = jnp.where(four == nz - 1, 0.0, wide_down * wet * pltpu.roll(wet, lanes - 4, 1))
    images = []
    for v in fields:
        beside = jnp.where(place == 1, pltpu.roll(v, 1, 1), pltpu.roll(v, lanes - 1, 1))
        flux_down = c_down * (pltpu.roll(v, lanes - 4, 1) - v)
        change = inner * (v - beside) + c_north * (v - pltpu.roll(v, rows - 1, 0)) + c_south * (v - pltpu.roll(v, 1, 0))
        images.append(change + (pltpu.roll(flux_down, 4, 1) - flux_down))
    for i, parts in enumerate((images, fields, (own_east, own_east))):
        own[pl.ds(i * rows, rows), :] = pairs_of(parts, lane)
    put_message(rows, own, message, True)
    for i, part in enumerate((c_north, c_down, inner)):
        packed[pl.ds(i * rows, rows), :] = pairs_of((part, part), lane)


def block_kernel(tracers, nz, rows, field, mask, levels, east, north, down,
                 coef_east, coef_west, coef_north, coef_south, coef_down, east_own, north_own, image, rows_b):
    lanes = field.shape[1]
    chunk = nz // 2
    shape = (1, rows, lanes)
    last_lane, last_row = iota(shape, 2) == lanes - 1, iota(shape, 1) == rows - 1
    first_lane, first_row = iota(shape, 2) == 0, iota(shape, 1) == 0
    zero = jnp.zeros((rows, lanes), F32)
    depth = levels[...]
    level = iota((chunk + 1, rows, lanes), 0)
    above = [zero[None]] * tracers
    for k in range(0, nz, chunk):
        count = min(chunk + 1, nz - k)
        wet = (levels_of(mask, k, count, rows) == 1) & (level[:count] + k < depth[None])
        wet = jnp.where(wet, 1.0, 0.0)
        if count == chunk:
            wet = jnp.concatenate([wet, zero[None]], axis=0)
        ocean = wet[:chunk]
        own_east = levels_of(east, k, chunk, rows).astype(F32) * ocean
        own_north = levels_of(north, k, chunk, rows).astype(F32) * ocean
        c_east = jnp.where(last_lane, 0.0, own_east * pltpu.roll(ocean, lanes - 1, 2))
        c_north = jnp.where(last_row, 0.0, own_north * pltpu.roll(ocean, rows - 1, 1))
        c_down = levels_of(down, k, chunk, rows).astype(F32) * ocean * wet[1:]
        c_west = jnp.where(first_lane, 0.0, pltpu.roll(own_east, 1, 2) * ocean)
        c_south = jnp.where(first_row, 0.0, pltpu.roll(own_north, 1, 1) * ocean)
        c = (c_east, c_west, c_north, c_south, c_down)
        changes = []
        for t in range(tracers):
            value = levels_of(field, t * nz + k, chunk, rows)
            below = levels_of(field, t * nz + k + chunk, 1, rows) if k + chunk < nz else zero[None]
            change, above[t] = laplacian(value, below, above[t], c)
            changes.append(change)
        for ref, value in zip((coef_east, coef_west, coef_north, coef_south, coef_down, east_own, north_own), c + (own_east, own_north)):
            put_levels(ref, k, value)
        for t in range(tracers):
            put_levels(image, t * nz + k, changes[t])
    edge_rows(tracers, nz, rows, field, image, east_own, north_own, True, rows_b)


def put_message(rows, own, message, second):
    lanes = own.shape[1]
    eastern = is_even("lon") != second
    even_lane = (iota((rows, lanes), 1) & 1) == 0
    image, field = own[pl.ds(0, rows), :], own[pl.ds(rows, rows), :]
    to_east = jnp.where(even_lane, image, pltpu.roll(field, 1, 1))
    to_west = jnp.where(even_lane, pltpu.roll(field, lanes - 1, 1), image)
    message[pl.ds(0, rows), :] = jnp.where(eastern, to_east, to_west)
    message[pl.ds(rows, rows), :] = own[pl.ds(2 * rows, rows), :]


def edge_rows(tracers, nz, rows, field, image, east_own, north_own, second, out):
    southern = is_even("lat") if second else jnp.logical_not(is_even("lat"))

    def edge(side):
        first = (rows - 1) * side
        parts = [ref[pl.ds(first + t * nz * rows, nz, rows), :] for ref in (image, field) for t in range(tracers)]
        return parts + [(east_own, north_own)[side][pl.ds(first, nz, rows), :]]

    for at, (south, north_) in enumerate(zip(edge(0), edge(1))):
        out[pl.ds(at * nz, nz), :] = jnp.where(southern, south, north_)


def later_kernel(tracers, nz, rows, field, image, east_own, north_own, own, rows_b, rows_a, message_a):
    edge_rows(tracers, nz, rows, field, image, east_own, north_own, False, rows_a)
    put_message(rows, own, message_a, False)


def stacked(parts):
    lanes = parts[0].shape[1]
    row = iota((8, lanes), 0)
    total = jnp.zeros((8, lanes), F32)
    for i, part in enumerate(parts):
        total = jnp.where(row == i, part, total)
    return total


def folded(x):
    return sum(x[i : i + 8] for i in range(0, x.shape[0], 8))


def interior_kernel(tracers, nz, rows, field, image, coef_east, coef_west, coef_north, coef_south, coef_down,
                    twice, packed, sums):
    lanes = field.shape[1]
    pair = iota((rows, lanes), 1) >> 1
    zero = packed_twice = jnp.zeros((rows, lanes), F32)
    totals = [[zero] * 4 for _ in range(tracers)]
    above = [zero[None]] * tracers
    for k in range(0, nz, CHUNK):
        refs = (coef_east, coef_west, coef_north, coef_south, coef_down)
        c = [levels_of(ref, k, CHUNK, rows) for ref in refs]
        results = []
        for t in range(tracers):
            w = levels_of(image, t * nz + k, CHUNK, rows)
            below = levels_of(image, t * nz + k + CHUNK, 1, rows) if k + CHUNK < nz else zero[None]
            y, above[t] = laplacian(w, below, above[t], c)
            results.append(y)
            v = levels_of(field, t * nz + k, CHUNK, rows)
            for i, product in enumerate((v * v, v * w, w * w, w * y)):
                totals[t][i] = totals[t][i] + jnp.sum(product, axis=0)
        for t in range(tracers):
            packed_twice = packed_into(packed_twice, results[t], k * tracers + t, tracers, pair)
        for t in range(tracers):
            put_levels(twice, t * nz + k, results[t])
    packed[...] = packed_twice
    for t in range(tracers):
        for i in range(4):
            sums[pl.ds((4 * t + i) * 8, 8), :] = folded(totals[t][i])


def sums_kernel(tracers, nz, rows, devices, image_in, twice_in, coef_east, coef_north, coef_down, rows_a, rows_b, got_rows_a,
                got_rows_b, own, got_a, got_b, packed, packed_twice, sums, image, twice, corrections, result):
    lanes = own.shape[1]
    even = is_even("lat")
    pair, level = iota((nz, lanes), 1) >> 1, iota((nz, lanes), 0)
    row = iota((rows, lanes), 0)
    north, down, inner = [packed[pl.ds(i * rows, rows), :] for i in range(3)]
    dots = [[jnp.zeros((8, lanes), F32) for _ in range(3)] for _ in range(tracers)]
    nothing = jnp.zeros((1, lanes), F32)
    row_change, row_inside = jnp.zeros((rows, lanes), F32), jnp.zeros((rows, lanes), F32)
    lat_coef, lat_ring, lat_change = [], [], []
    stores = []
    for side in range(SIDES):
        def part(at, a, b):
            first, second = (b, a) if side == 0 else (a, b)
            return jnp.where(even, first[pl.ds(at * nz, nz), :], second[pl.ds(at * nz, nz), :])

        own_row = lambda at: part(at, rows_a, rows_b)
        got_row = lambda at: part(at, got_rows_a, got_rows_b)
        own_coef, got_coef = own_row(2 * tracers), got_row(2 * tracers)
        c = got_coef * (own_coef > 0).astype(F32) if side == 0 else own_coef * (got_coef > 0).astype(F32)
        c = c * jnp.where(lax.axis_index("lat") == (0, lax.axis_size("lat") - 1)[side], 0.0, 1.0)
        first, next_row, between = ((0, 1, 0), (rows - 1, rows - 2, rows - 2))[side]
        c_east, c_down = coef_east[pl.ds(first, nz, rows), :], coef_down[pl.ds(first, nz, rows), :]
        c_inner = coef_north[pl.ds(between, nz, rows), :]
        packed_coef, packed_ring, packed_e, packed_inside = [nothing] * 4
        for t in range(tracers):
            b, w = own_row(tracers + t), own_row(t)
            f = c * (got_row(tracers + t) - b)
            e = -f
            ring = got_row(t) + f
            flux_east = c_east * (pltpu.roll(e, lanes - 1, 1) - e)
            flux_down = c_down * (pltpu.roll(e, nz - 1, 0) - e)
            inside = (pltpu.roll(flux_east, 1, 1) - flux_east) + (pltpu.roll(flux_down, 1, 0) - flux_down) + c_inner * e
            changed = w + e
            through = c * (ring - changed)
            at = pl.ds(first + t * nz * rows, nz, rows)
            at_next = pl.ds(next_row + t * nz * rows, nz, rows)
            y = twice_in[at, :]
            stores.append((image, at, changed))
            stores.append((twice, at, y + inside - through))
            stores.append((twice, at_next, twice_in[at_next, :] - c_inner * e))
            for i, value in enumerate((b * e, (w + changed) * e, (2.0 * y + inside) * e - changed * through)):
                dots[t][i] = dots[t][i] + folded(value)
            packed_coef = packed_coef + spread(c, t, tracers, pair, level)
            packed_ring = packed_ring + spread(ring, t, tracers, pair, level)
            packed_e = packed_e + spread(e, t, tracers, pair, level)
            packed_inside = packed_inside + spread(inside, t, tracers, pair, level)
        row_change = jnp.where(row == first, packed_e, row_change)
        row_inside = jnp.where(row == first, packed_inside, row_inside)
        row_inside = jnp.where(row == next_row, -north[between : between + 1] * packed_e, row_inside)
        lat_coef.append(packed_coef)
        lat_ring.append(packed_ring)
        lat_change.append(-packed_e)

    even = is_even("lon")
    even_lane = (iota((rows, lanes), 1) & 1) == 0

    def neighbours(at):
        a, b = got_a[at, :], got_b[at, :]
        return jnp.where(even, a, b), jnp.where(even, b, a)

    parts = [pl.ds(i * rows, rows) for i in range(3)]
    own_image, own_field, own_east = [own[p, :] for p in parts]
    columns = neighbours(parts[0])
    got_image, got_field = from_neighbours(*columns, even_lane), jnp.where(even_lane, *columns)
    got_east = from_neighbours(*neighbours(parts[1]), even_lane)
    before = own_image + row_change
    y = packed_twice[...] + row_inside
    c = face(own_east, got_east, even_lane)
    f = c * (got_field - own_field)
    e = -f
    after = before + e
    ring = got_image + f
    through = c * (ring - after)
    through_new = through_old = halves = jnp.zeros((rows, lanes), F32)
    for side in range(SIDES):
        here = row == (rows - 1) * side
        through_new = jnp.where(here, lat_coef[side] * (lat_ring[side] - after), through_new)
        through_old = jnp.where(here, lat_coef[side] * (lat_ring[side] - before), through_old)
        halves = jnp.where(here, lat_coef[side] * lat_ring[side] * f + c * ring * lat_change[side], halves)
    flux_down = down * (pltpu.roll(e, lanes - 2 * tracers, 1) - e)
    flux_north = north * (pltpu.roll(e, rows - 1, 0) - e)
    inside = (pltpu.roll(flux_down, 2 * tracers, 1) - flux_down) + (pltpu.roll(flux_north, 1, 0) - flux_north) + inner * e
    beside = -inner * e
    corrections[parts[0], :] = e
    corrections[parts[1], :] = inside - through - (through_new - through_old)
    corrections[parts[2], :] = beside
    edges = [(rows - 1) * side for side in range(SIDES)]
    corrections[pl.ds(3 * rows, 8), :] = stacked(lat_coef + [c[i : i + 1] for i in edges])

    column_dots = [folded(value) for value in (
        own_field * e,
        (before + after) * e,
        (2.0 * y + inside) * e - after * (through + through_new) + before * through_old + halves,
    )]
    tile_lane, tile_row = iota((8, lanes), 1), iota((8, lanes), 0)
    total = jnp.zeros((8, lanes), F32)
    for t in range(tracers):
        mine = lax.rem(tile_lane >> 1, tracers) == t
        for i in range(4):
            value = sums[pl.ds((4 * t + i) * 8, 8), :]
            if i:
                value = value + dots[t][i - 1] + jnp.where(mine, column_dots[i - 1], 0.0)
            total = jnp.where(tile_row == 4 * t + i, jnp.sum(value, axis=0, keepdims=True), total)
    total = jnp.sum(total, axis=1, keepdims=True)
    total = jnp.sum(jnp.where(tile_row == tile_lane, total, 0.0), axis=0, keepdims=True)
    even_row = (iota((1, lanes), 1) & 1) == 0
    south, north_ = edges
    lon_shares = [2.0 * c[i : i + 1] * part for i, part in zip(edges, lat_change)]
    shares = [total, 2.0 * lat_coef[1] * f[north_ : north_ + 1], jnp.where(even_row, lon_shares[0], lat_change[0]),
              jnp.where(even_row, lon_shares[1], f[south : south + 1])]
    for i, share in enumerate(shares):
        result[pl.ds(i, devices, SHARES), :] = jnp.broadcast_to(share, (devices, lanes))
    for ref, at, value in stores:
        ref[at, :] = value


def finish_kernel(tracers, nz, rows, devices, field, image, twice, corrections, sums, solution_out, residual_out,
                  solution, residual, sems):
    lanes = field.shape[1]
    across, along = lax.axis_size("lon"), lax.axis_size("lat")
    one = iota((1, lanes), 1)
    even_one = (one & 1) == 0
    total, to_north, lon_south, mixed = [sums[pl.ds(i, devices, SHARES), :] for i in range(SHARES)]
    total = jnp.sum(total, axis=0, keepdims=True)
    even_lane = (iota((devices, lanes), 1) & 1) == 0
    last = lax.rem(iota((devices, lanes), 0), across) == across - 1
    from_east = lambda x: pltpu.roll(jnp.where(last, pltpu.roll(x, across - 1, 0), pltpu.roll(x, devices - 1, 0)), lanes - 1, 1)
    from_north = lambda x: pltpu.roll(x, devices - across, 0)
    beyond = from_east(lon_south)
    cross = jnp.where(even_lane, lon_south * beyond - mixed * from_north(beyond), 0.0)
    cross = cross + to_north * from_north(jnp.where(even_lane, -from_east(mixed), mixed))
    cross = jnp.sum(cross, axis=0, keepdims=True)

    lon, lat = lax.axis_index("lon"), lax.axis_index("lat")
    tile_row = iota((8, lanes), 0)

    def share(i, j, at):
        first = SHARES * (j * across + i)
        tile = sums[pl.ds(pl.multiple_of(first // 8 * 8, 8), 8), :]
        return jnp.sum(jnp.where(tile_row == lax.rem(first, 8) + at, tile, 0.0), axis=0, keepdims=True)

    faces = corrections[pl.ds(3 * rows, 8), :]
    east, west = lax.rem(lon + 1, across), lax.rem(lon + across - 1, across)
    south, north = jnp.maximum(lat - 1, 0), jnp.minimum(lat + 1, along - 1)
    northern = jnp.where(lat < along - 1, 1.0, 0.0)
    lat_sides = (share(lon, south, 1) * jnp.where(lat > 0, 0.5, 0.0),
                 faces[1:2] * jnp.where(even_one, -pltpu.roll(share(east, north, 3), lanes - 1, 1), share(lon, north, 3)))
    lon_sides = (from_neighbours(share(east, lat, 2), 0.5 * share(west, lat, 2), even_one),
                 from_neighbours(-northern * share(east, north, 2), 0.5 * share(west, lat, 3), even_one))
    sides = [lat_sides[i] + jnp.where(even_one, faces[2 + i : 3 + i] * lon_sides[i], lon_sides[i]) for i in range(SIDES)]
    row = iota((rows, lanes), 0)
    e, change, beside = [corrections[pl.ds(i * rows, rows), :] for i in range(3)]
    change = change + jnp.where(row == 0, sides[0], jnp.where(row == rows - 1, sides[1], 0.0))

    lane = iota((CHUNK, rows, lanes), 2)
    narrow = iota((rows, lanes), 1)
    edge = (lane == 0) | (lane == lanes - 1)
    near = (lane <= 1) | (lane >= lanes - 2)

    def number(i):
        return jnp.sum(jnp.where(one == i, total, 0.0), axis=1, keepdims=True)

    copies, factors = [], []
    for t in range(tracers):
        bb, bw, ww, wy = [number(4 * t + i) for i in range(4)]
        mine = lax.rem(one >> 1, tracers) == t
        wy = wy - jnp.sum(jnp.where(mine, cross, 0.0), axis=1, keepdims=True)
        whole = 1.0 / (bb + bw)
        step = bb * whole
        rest = bw * whole
        beta = jnp.maximum(step * (ww * whole) - rest * rest, 0.0)
        new = beta * bb
        tau = beta + rest
        step_next = new / (new + beta * new + tau * tau * bw - 2.0 * tau * step * ww + step * step * wy)
        step_next = jnp.minimum(jnp.maximum(step_next, 0.0), 1.0)
        both = step * step_next
        factors.append((both, step + step_next * tau, rest - step_next * tau, both - step - step_next * tau))
    for t, (both, s_b, r_b, r_w) in enumerate(factors):
        s_edge = -both * e
        r_edge = jnp.where(lax.rem(narrow >> 1, tracers) == t, r_w * e + both * change,
                           both * jnp.where((narrow & 1) == 0, pltpu.roll(beside, 1, 1), pltpu.roll(beside, lanes - 1, 1)))
        for k in range(0, nz, CHUNK):
            slot, first = t * nz + k, k * tracers + t
            v, w, y = [levels_of(ref, slot, CHUNK, rows) for ref in (field, image, twice)]
            more = jnp.where(edge, unpacked(s_edge, first, tracers, CHUNK), 0.0)
            much = jnp.where(near, unpacked(r_edge, first, tracers, CHUNK), 0.0)
            put_levels(solution, slot, (s_b * v - both * w) + more)
            put_levels(residual, slot, (r_b * v + r_w * w + both * y) + much)
            at = pl.ds(slot * rows, CHUNK * rows)
            for a, b in ((solution, solution_out), (residual, residual_out)):
                copy = pltpu.make_async_copy(a.at[at], b.at[at], sems.at[len(copies)])
                copy.start()
                copies.append(copy)
    for copy in copies:
        copy.wait()


def swapped(x, axis, second):
    devices = lax.axis_size(axis)
    forward = [(i % 2 == 0) != second for i in range(devices)]
    return lax.ppermute(x, axis, [(i, (i + 1 if forward[i] else i - 1) % devices) for i in range(devices)])


def body(right_side, sea_mask, levels, east_diffusivity, north_diffusivity, vertical_diffusivity):
    tracers, nz, rows, lanes = right_side.shape
    devices = lax.axis_size("lon") * lax.axis_size("lat")
    flat = lambda x: x.reshape(-1, lanes)
    outside = lambda x: pltpu.with_memory_space_constraint(flat(x), pltpu.HBM)
    n = nz * rows
    cells = tracers * n * lanes

    def call(kernel, outs, flops, space=pltpu.VMEM, **more):
        outs = [m if isinstance(m, tuple) else (m, F32) for m in outs]
        cost = pl.CostEstimate(flops=flops, bytes_accessed=4 * lanes * sum(m for m, _ in outs), transcendentals=0)
        return pl.pallas_call(
            functools.partial(kernel, tracers, nz, rows),
            out_shape=[space((m, lanes), dtype) for m, dtype in outs],
            compiler_params=pltpu.CompilerParams(vmem_limit_bytes=32 * 1024 * 1024),
            cost_estimate=cost,
            **more,
        )

    def with_devices(kernel):
        return lambda tracers, nz, rows, *refs: kernel(tracers, nz, rows, devices, *refs)

    scratch = lambda m, dtype: pltpu.VMEM((m, lanes), dtype)
    *inputs, own, message, packed = call(
        columns_kernel,
        [tracers * n, (n, jnp.int32), (rows, jnp.int32)] + [(n, jnp.bfloat16)] * 3 + [3 * rows, 2 * rows, 3 * rows],
        20 * cells,
        in_specs=[pl.BlockSpec(memory_space=pltpu.HBM)] * 6,
        scratch_shapes=[pltpu.SemaphoreType.DMA((6,))],
        name="columns",
    )(*map(outside, (right_side, sea_mask, levels, east_diffusivity, north_diffusivity, vertical_diffusivity)))
    field = inputs[0]
    got_b = swapped(message, "lon", True)
    coef_east, coef_west, coef_north, coef_south, coef_down, east_own, north_own, image, rows_b = call(
        block_kernel, [n] * 7 + [tracers * n, FIELDS * nz], 20 * cells, name="block")(*inputs)
    got_rows_b = swapped(rows_b, "lat", True)
    coefs = (coef_east, coef_west, coef_north, coef_south, coef_down)
    rows_a, message_a = call(later_kernel, [FIELDS * nz, 2 * rows], cells, name="later")(
        field, image, east_own, north_own, own, rows_b)
    twice, packed_twice, sums = call(
        interior_kernel, [tracers * n, rows, 8 * 4 * tracers], 60000 * cells, name="interior"
    )(field, image, *coefs)
    got_a = swapped(message_a, "lon", False)
    got_rows_a = swapped(rows_a, "lat", False)
    image, twice, corrections, sums = call(
        with_devices(sums_kernel), [tracers * n, tracers * n, 3 * rows + 8, SHARES * devices], cells,
        input_output_aliases={0: 0, 1: 1}, name="sums",
    )(image, twice, coef_east, coef_north, coef_down, rows_a, rows_b, got_rows_a, got_rows_b, own, got_a, got_b, packed, packed_twice, sums)
    sums = lax.all_to_all(sums.reshape(devices, 1, -1), ("lat", "lon"), 0, 0, tiled=True).reshape(-1, lanes)
    copies = 2 * tracers * nz // CHUNK
    solution_field, residual = call(
        with_devices(finish_kernel), [tracers * n] * 2, 20 * cells, space=jax.ShapeDtypeStruct,
        out_specs=[pl.BlockSpec(memory_space=pltpu.HBM)] * 2,
        scratch_shapes=[scratch(tracers * n, F32)] * 2 + [pltpu.SemaphoreType.DMA((copies,))],
        name="finish",
    )(field, image, twice, corrections, sums)
    return solution_field.reshape(right_side.shape), residual.reshape(right_side.shape)


def solution(mesh):
    return jax.shard_map(
        body,
        mesh=mesh,
        in_specs=(
            P(None, None, "lat", "lon"),
            P(None, "lat", "lon"),
            P("lat", "lon"),
            P(None, "lat", "lon"),
            P(None, "lat", "lon"),
            P(None, "lat", "lon"),
        ),
        out_specs=(P(None, None, "lat", "lon"), P(None, None, "lat", "lon")),
        check_vma=False,
    )
```
